32 devices in a mesh: dp: 8 (over z, y), ctx: 4 (over x, core).
Axes of the slice: x: 2, y: 2, z: 4, core: 2. Of those that a mesh axis runs over, the one named last changes fastest.
Arguments:
- block_in: bfloat16 [16, 1024, 1024], P('dp', 'ctx'), may hold values from -6 to 6
- out_grad: bfloat16 [16, 1024, 1024], P('dp', 'ctx'), may hold values from -6 to 6
- w_in: float32 [1024, 4384], P(('dp', 'ctx')), may hold values from -0.1875 to 0.1875
- w_in_m: float32 [1024, 4384], P(('dp', 'ctx')), may hold values from -28 to 28
- w_in_v: float32 [1024, 4384], P(('dp', 'ctx')), may hold values from 1.47456 to 5.89824
- w_out: float32 [2048, 1024], P(('dp', 'ctx')), may hold values from -0.125 to 0.125
- w_out_m: float32 [2048, 1024], P(('dp', 'ctx')), may hold values from -80 to 80
- w_out_v: float32 [2048, 1024], P(('dp', 'ctx')), may hold values from 16.384 to 65.536
- small_params: float32 [14688], replicated, may hold values from -8 to 8
- small_m: float32 [14688], replicated, may hold values from -24 to 24
- small_v: float32 [14688], replicated, may hold values from 1.6384 to 6.5536
Outputs:
- block_out: bfloat16 [16, 1024, 1024], P('dp', 'ctx')
- input_grad: bfloat16 [16, 1024, 1024], P('dp', 'ctx')
- grad_w_in: float32 [1024, 4384], P(('dp', 'ctx'))
- w_in_v_new: float32 [1024, 4384], P(('dp', 'ctx'))
- w_in_new: float32 [1024, 4384], P(('dp', 'ctx'))
- grad_w_out: float32 [2048, 1024], P(('dp', 'ctx'))
- w_out_v_new: float32 [2048, 1024], P(('dp', 'ctx'))
- w_out_new: float32 [2048, 1024], P(('dp', 'ctx'))
- grad_small: float32 [14688], replicated
- small_v_new: float32 [14688], replicated
- small_new: float32 [14688], replicated
The draws below stay inside these ranges and needn't reach their ends.
All inputs are finite; a program needn't handle non-finite values.
Results may differ from the reference program's by a relative error of at most 0.0078.
Values may be sent and summed in bfloat16 or wider, within the bound.
No kernel may reach another device: no remote copies, remote signals or barrier semaphores. Data moves between devices by JAX's collectives and lax.ppermute only.
A program may use at most 192 MiB of HBM per device.

```python
import math
import jax
import jax.numpy as jnp
from jax import lax

D = 1024
HEADS = 32
HD = 64
NS = 128
KCONV = 4
GROUP = 256
STEP = 10
DI = 2048
PROJ = 4384
SMALL = 14688
LEN = 1024
NSEQ = 16
N_CTX = 4


def draw_small_params(key, part):
    key = jax.random.fold_in(key, 7)
    subkeys = jax.random.split(key, 9)
    channels = DI + 2 * NS
    norm_gain = jax.random.uniform(subkeys[0], (D,), jnp.float32, 0.5, 1.5)
    gate_gain = jax.random.uniform(subkeys[1], (DI,), jnp.float32, 0.5, 1.5)
    conv_taps = 0.5 * jnp.clip(jax.random.normal(subkeys[2], (KCONV * channels,), jnp.float32), -4.0, 4.0)
    conv_bias = 0.3 * jnp.clip(jax.random.normal(subkeys[3], (channels,), jnp.float32), -4.0, 4.0)
    dt_bias = jax.random.uniform(subkeys[4], (HEADS,), jnp.float32, -4.0, -2.0)
    fast_heads = jax.random.randint(subkeys[5], (HEADS,), 0, 2) == 0
    slow_rate = jax.random.uniform(subkeys[6], (HEADS,), jnp.float32, 0.5, 1.5) / (LEN * 0.05)
    fast_rate = jax.random.uniform(subkeys[7], (HEADS,), jnp.float32, 0.7, 1.4) / (40.0 * 0.05)
    a_log = jnp.log(jnp.where(fast_heads, fast_rate, slow_rate))
    skip_gain = jax.random.uniform(subkeys[8], (HEADS,), jnp.float32, 0.5, 1.5)
    return jnp.concatenate([norm_gain, gate_gain, conv_taps, conv_bias, dt_bias, a_log, skip_gain])


def level_of(key, shape, shards, least, largest):
    gain = 1.0
    for dim, parts in shards:
        heights = jax.random.uniform(jax.random.fold_in(jax.random.fold_in(key, 6), dim), (parts,), jnp.float32, least / len(shards), largest / len(shards))
        gain = gain * jnp.repeat(jnp.exp(heights), shape[dim] // parts).reshape((-1,) + (1,) * (len(shape) - 1 - dim))
    return gain


def bell_draw(key, shape, deviation, most, shards=(), dtype=jnp.bfloat16):
    factor_of = level_of(key, shape, shards, -0.22, 0.18) if shards else 1.0
    values = jax.random.normal(key, shape, jnp.float32) * deviation * factor_of
    return jnp.minimum(jnp.maximum(values, -most), most).astype(dtype)


def setup_inputs(seed: int = 0) -> dict:
    streams_of = jax.random.split(jax.random.key(seed), 12)
    block_in = bell_draw(streams_of[0], (NSEQ, LEN, D), 1.0, 6.0, ((0, 8), (1, 4)))
    out_grad = bell_draw(streams_of[1], (NSEQ, LEN, D), 1.0, 6.0, ((0, 8), (1, 4)))
    w_in = bell_draw(streams_of[2], (D, PROJ), D ** -0.5, 0.1875, ((0, 32),), jnp.float32)
    w_in_m = bell_draw(streams_of[3], (D, PROJ), (0.035 * (NSEQ * LEN) ** 0.5), 28.0, ((0, 32),), jnp.float32)
    w_in_v = jnp.clip(jnp.exp(math.log(5.89824) - 1.3862944 * jax.random.uniform(streams_of[4], (D, PROJ), jnp.float32) ** level_of(streams_of[4], (D, PROJ), ((0, 32),), -0.2, 0.2)), 1.47456, 5.89824)
    w_out = bell_draw(streams_of[5], (DI, D), DI ** -0.5, 0.125, ((0, 32),), jnp.float32)
    w_out_m = bell_draw(streams_of[6], (DI, D), (0.11 * (NSEQ * LEN) ** 0.5), 80.0, ((0, 32),), jnp.float32)
    w_out_v = jnp.clip(jnp.exp(math.log(65.536) - 1.3862944 * jax.random.uniform(streams_of[7], (DI, D), jnp.float32) ** level_of(streams_of[7], (DI, D), ((0, 32),), -0.2, 0.2)), 16.384, 65.536)
    small_params = draw_small_params(jax.random.fold_in(streams_of[11], 71), 0)
    small_m = bell_draw(streams_of[9], (SMALL,), (0.03 * (NSEQ * LEN) ** 0.5), 24.0, (), jnp.float32)
    small_v = jnp.clip(jnp.exp(jax.random.uniform(streams_of[10], (SMALL,), jnp.float32, math.log(1.6384), math.log(6.5536))), 1.6384, 6.5536)
    return {"block_in": block_in, "out_grad": out_grad, "w_in": w_in, "w_in_m": w_in_m, "w_in_v": w_in_v, "w_out": w_out, "w_out_m": w_out_m, "w_out_v": w_out_v, "small_params": small_params, "small_m": small_m, "small_v": small_v}


NORM_EPS = 1e-05
ADAM_EPS = 1e-08
BETA_ONE = 0.9
BETA_TWO = 0.999
RATE_BIG = 0.03
RATE_SMALL = 0.3
DECAY_WEIGHT = 0.01
PRECISE = lax.Precision.HIGHEST

@jax.custom_vjp
def low(v):
    return lax.optimization_barrier(v.astype(jnp.bfloat16)).astype(jnp.float32)

@jax.custom_vjp
def low_back(v):
    return v

def low_keep(v):
    return (low(v), None)

def low_pass(kept, grad):
    return (grad,)

def back_keep(v):
    return (v, None)

def back_low(kept, grad):
    return (low(grad),)
low.defvjp(low_keep, low_pass)
low_back.defvjp(back_keep, back_low)

def split_small(packed):
    channels = DI + 2 * NS
    pieces = []
    offset = 0
    for amount in (D, DI, KCONV * channels, channels, HEADS, HEADS, HEADS):
        pieces.append(packed[offset:offset + amount])
        offset = offset + amount
    return (pieces[0], pieces[1], pieces[2].reshape(KCONV, channels), pieces[3], pieces[4], pieces[5], pieces[6])

def rms_scale(values, scale_gain):
    return values * lax.rsqrt(lax.optimization_barrier(jnp.mean(values * values, axis=-1, keepdims=True)) + NORM_EPS) * scale_gain

def conv_part(projected, prev_rim, conv_taps, conv_bias, dt_bias, a_log):
    channels = DI + 2 * NS
    batch_rows, span_rows = (projected.shape[0], projected.shape[1])
    conv_in = projected[:, :, DI:DI + channels]
    padded = jnp.concatenate([prev_rim, conv_in], axis=1)
    conv_out = conv_bias + sum((conv_taps[tap_index] * padded[:, tap_index:tap_index + span_rows] for tap_index in range(KCONV)))
    active = jax.nn.silu(conv_out)
    values = active[:, :, :DI].reshape(batch_rows, span_rows, HEADS, HD)
    in_b = active[:, :, DI:DI + NS]
    out_c = active[:, :, DI + NS:]
    step_size = jax.nn.softplus(projected[:, :, DI + channels:] + dt_bias)
    rates = -jnp.exp(a_log) * step_size
    return (values, in_b, out_c, step_size, rates)

def group_state(values, in_b, step_size, cumulative):
    totals = cumulative[:, -1, :]
    weights = jnp.exp(totals[:, None, :] - cumulative) * step_size
    states = jnp.einsum('bqh,bqn,bqhp->bhpn', weights, in_b, values, precision=PRECISE)
    return (states, totals)

def group_output(values, in_b, out_c, step_size, cumulative, incoming, skip_gain):
    span_rows = values.shape[1]
    by_head = jnp.swapaxes(cumulative, 1, 2)
    differ = by_head[:, :, :, None] - by_head[:, :, None, :]
    causal = jnp.arange(span_rows)[:, None] >= jnp.arange(span_rows)[None, :]
    decays = jnp.exp(jnp.where(causal, differ, -1e+30))
    scores = jnp.einsum('btn,bun->btu', out_c, in_b, precision=PRECISE)
    mixing = decays * scores[:, None] * jnp.swapaxes(step_size, 1, 2)[:, :, None, :]
    inner_part = jnp.einsum('bhtu,buhp->bthp', mixing, values, precision=PRECISE)
    outer_part = jnp.einsum('btn,bth,bhpn->bthp', out_c, jnp.exp(cumulative), incoming, precision=PRECISE)
    return inner_part + outer_part + skip_gain[:, None] * values

def sequence_forward(tokens, w_in_low, w_out_low, small_parts):
    norm_gain, gate_gain, conv_taps, conv_bias, dt_bias, a_log, skip_gain = small_parts
    channels = DI + 2 * NS
    normed = rms_scale(tokens, norm_gain)
    projected = low_back(jnp.dot(low(normed), w_in_low, precision=PRECISE))
    values, in_b, out_c, step_size, rates = conv_part(projected[None], jnp.zeros((1, KCONV - 1, channels), jnp.float32), conv_taps, conv_bias, dt_bias, a_log)
    values = values.reshape(N_CTX, GROUP, HEADS, HD)
    in_b = in_b.reshape(N_CTX, GROUP, NS)
    out_c = out_c.reshape(N_CTX, GROUP, NS)
    step_size = step_size.reshape(N_CTX, GROUP, HEADS)
    cumulative = jnp.cumsum(rates.reshape(N_CTX, GROUP, HEADS), axis=1)
    states, totals = group_state(values, in_b, step_size, cumulative)

    def carry_step(carried, group_item):
        state_now, total_now = group_item
        return (jnp.exp(total_now)[:, None, None] * carried + state_now, carried)
    _, incoming = lax.scan(carry_step, jnp.zeros((HEADS, HD, NS), jnp.float32), (states, totals))
    mixed = group_output(values, in_b, out_c, step_size, cumulative, incoming, skip_gain)
    gated = mixed.reshape(LEN, DI) * jax.nn.silu(projected[:, :DI])
    normed_out = rms_scale(gated, gate_gain)
    return tokens + jnp.dot(low(normed_out), w_out_low, precision=PRECISE)

def adam_step(weight, first_old, second_old, gradient, step_rate):
    first_new = BETA_ONE * first_old + (1.0 - BETA_ONE) * gradient
    second_new = BETA_TWO * second_old + (1.0 - BETA_TWO) * gradient * gradient
    first_hat = first_new / (1.0 - BETA_ONE ** STEP)
    second_hat = second_new / (1.0 - BETA_TWO ** STEP)
    weight_new = weight - step_rate * (first_hat / (jnp.sqrt(second_hat) + ADAM_EPS) + DECAY_WEIGHT * weight)
    return (second_new, weight_new)

def reference(block_in, out_grad, w_in, w_in_m, w_in_v, w_out, w_out_m, w_out_v, small_params, small_m, small_v):
    tokens = block_in.astype(jnp.float32)
    cotangent = out_grad.astype(jnp.float32)

    def forward(tokens_all, w_in_all, w_out_all, small_all):
        small_parts = split_small(small_all)
        w_in_low = low(w_in_all)
        w_out_low = low(w_out_all)

        def per_sequence(carried, sequence):
            return (carried, sequence_forward(sequence, w_in_low, w_out_low, small_parts))
        _, outputs = lax.scan(jax.checkpoint(per_sequence), None, tokens_all)
        return outputs
    result, back_fn = jax.vjp(forward, tokens, w_in, w_out, small_params)
    grad_tokens, grad_in, grad_out, grad_small = back_fn(cotangent)
    in_second, in_new = adam_step(w_in, w_in_m, w_in_v, grad_in, RATE_BIG)
    out_second, out_new = adam_step(w_out, w_out_m, w_out_v, grad_out, RATE_BIG)
    small_second, small_updated = adam_step(small_params, small_m, small_v, grad_small, RATE_SMALL)
    return (result.astype(jnp.bfloat16), grad_tokens.astype(jnp.bfloat16), grad_in, in_second, in_new, grad_out, out_second, out_new, grad_small, small_second, small_updated)
```

```python
import functools

import jax
import jax.numpy as jnp
from jax import lax
from jax.experimental import pallas as pl
from jax.experimental.pallas import tpu as pltpu
from jax.sharding import PartitionSpec as P

D = 1024
HEADS = 32
HD = 64
NS = 128
KCONV = 4
STEP = 10
DI = 2048
CHANNELS = DI + 2 * NS

CHUNK = 128
LANES = 128
RIM = 8
ROWS = 256

NORM_EPS = 1e-05
ADAM_EPS = 1e-08
BETA_ONE = 0.9
BETA_TWO = 0.999
RATE_BIG = 0.03
RATE_SMALL = 0.3
DECAY_WEIGHT = 0.01

F32 = jnp.float32
BF16 = jnp.bfloat16
VMEM_BYTES = 48 * 1024 * 1024


def dot(a, b, contract=((1,), (0,))):
    return lax.dot_general(a, b, (contract, ((), ())), preferred_element_type=F32)


def terms(a, count):
    parts = []
    for _ in range(count):
        part = a.astype(BF16)
        parts.append(part)
        a = a - part.astype(F32)
    return parts


def spread_dot(a, spread):
    return dot(
        jnp.concatenate(terms(a, 2), axis=1), jnp.concatenate([spread, spread], axis=0)
    )


def sum_dot(ones, a, count):
    return sum(dot(ones, part) for part in terms(a, count))


ROW_ROW = ((1,), (1,))
COL_COL = ((0,), (0,))


def sigmoid(v):
    return 1.0 / (1.0 + jnp.exp(-v))


def softplus(v):
    return jnp.maximum(v, 0.0) + jnp.log1p(jnp.exp(-jnp.abs(v)))


def expander(inner):
    head = lax.broadcasted_iota(jnp.int32, (LANES, inner), 0)
    column = lax.broadcasted_iota(jnp.int32, (LANES, inner), 1)
    inside = (column >= head * HD) & (column < (head + 1) * HD)
    return jnp.where(inside, 1.0, 0.0).astype(BF16)


def lower_ones():
    row = lax.broadcasted_iota(jnp.int32, (CHUNK, CHUNK), 0)
    column = lax.broadcasted_iota(jnp.int32, (CHUNK, CHUNK), 1)
    return jnp.where(row >= column, 1.0, 0.0)


def row_sums(a):
    lanes = a[:, :LANES]
    for start in range(LANES, a.shape[1], LANES):
        lanes = lanes + a[:, start : start + LANES]
    return jnp.sum(lanes.T, axis=0, keepdims=True)


def side_by_side(pair):
    lane = lax.broadcasted_iota(jnp.int32, pair.shape, 1)
    zero = jnp.zeros_like(pair)
    return jnp.concatenate(
        [jnp.where(lane < HD, pair, zero), jnp.where(lane < HD, zero, pair)], axis=0
    )


def decay_terms(step, rate, spread, tri):
    cum = sum_dot(tri.astype(BF16), rate, 3)
    total = cum[CHUNK - 1 : CHUNK, :]
    wide = spread_dot(
        jnp.concatenate([step, jnp.exp(cum), jnp.exp(total - cum)], axis=0), spread
    )
    return cum, cum.T, wide[:CHUNK], wide[CHUNK : 2 * CHUNK], wide[2 * CHUNK :]


def pair_mixing(cum, cum_t, scores, pair):
    decays = []
    for head in (2 * pair, 2 * pair + 1):
        differ = cum[:, head : head + 1] - cum_t[head : head + 1, :]
        decays.append(jnp.exp(jnp.minimum(differ, 0.0)))
    return decays, [(decay * scores).astype(BF16) for decay in decays]


def conv_forward(padded_ref, taps, rows):
    total = taps[KCONV : KCONV + 1, :]
    for k in range(KCONV):
        start = RIM - (KCONV - 1) + k
        total = total + taps[k : k + 1, :] * padded_ref[start : start + rows, :]
    return total


def forward_kernel(
    inner,
    tokens_ref,
    gain_ref,
    weight_ref,
    taps_ref,
    heads_ref,
    skip_ref,
    low_ref,
    rest_ref,
    mixed_ref,
    incoming_ref,
    padded,
    state,
):
    rows = tokens_ref.shape[1]
    conv = inner + 2 * NS
    @pl.when(pl.program_id(1) == 0)
    def _():
        padded[0:RIM, :] = jnp.zeros((RIM, conv), F32)
        state[...] = jnp.zeros_like(state)

    @pl.when(pl.program_id(1) > 0)
    def _():
        padded[0:RIM, :] = padded[rows : rows + RIM, :]

    tokens = tokens_ref[0].astype(F32)
    scale = lax.rsqrt(jnp.mean(tokens * tokens, axis=1, keepdims=True) + NORM_EPS)
    low = (tokens * scale * gain_ref[...]).astype(BF16)
    low_ref[0] = low
    projected = dot(low, weight_ref[...])
    rest_ref[0] = projected
    padded[RIM : RIM + rows, :] = projected[:, :conv]
    conv_out = conv_forward(padded, taps_ref[...], rows)
    active = conv_out * sigmoid(conv_out)
    heads = heads_ref[...]
    step_all = softplus(projected[:, conv:] + heads[0:1, :])
    rate_all = heads[1:2, :] * step_all
    skip = skip_ref[...]
    spread = expander(inner)
    tri = lower_ones()
    for c in range(rows // CHUNK):
        part = slice(c * CHUNK, (c + 1) * CHUNK)
        values = active[part, :inner]
        in_b = active[part, inner : inner + NS].astype(BF16)
        out_c = active[part, inner + NS :].astype(BF16)
        cum, cum_t, step_x, grown, remain = decay_terms(
            step_all[part], rate_all[part], spread, tri
        )
        stepped = values * step_x
        stepped_low = stepped.astype(BF16)
        scores = dot(out_c, in_b, ROW_ROW) * tri
        inside = []
        for pair in range(inner // LANES):
            lanes = slice(pair * LANES, (pair + 1) * LANES)
            _, mixing = pair_mixing(cum, cum_t, scores, pair)
            inside.append(
                dot(jnp.concatenate(mixing, axis=1), side_by_side(stepped_low[:, lanes]))
            )
        before = state[...]
        before_low = before.astype(BF16)
        incoming_ref[0, c] = before_low
        outer = grown * dot(out_c, before_low)
        mixed_ref[0, part, :] = jnp.concatenate(inside, axis=1) + outer + skip * values
        state[...] = grown[CHUNK - 1 : CHUNK, :] * before + dot(
            in_b, (remain * stepped).astype(BF16), COL_COL
        )


def stats_kernel(
    place_ref, up_ref, low_ref, weight_gate_ref, mixed_ref, gain_ref, *refs
):
    *block_refs, gate_ref, d_out_ref, stats_ref, weight_ref = refs

    @pl.when((pl.program_id(0) == 0) & (pl.program_id(1) == 0))
    def _():
        deep = block_refs[0].shape[0]
        for k, block_ref in enumerate(block_refs):
            start = pl.multiple_of((place_ref[0] ^ k) * deep, deep)
            weight_ref[pl.ds(start, deep), :] = block_ref[...]

    d_out = dot(up_ref[0], weight_ref[...], ROW_ROW)
    d_out_ref[0] = d_out
    gate = dot(low_ref[0], weight_gate_ref[...])
    gate_ref[0] = gate
    gated = mixed_ref[0] * gate * sigmoid(gate)
    stats_ref[0, 0:1, :] = row_sums(gated * gated)
    stats_ref[0, 1:2, :] = row_sums(d_out * gain_ref[...] * gated)


def row_to_lanes(row):
    return jnp.broadcast_to(row, (LANES, row.shape[1])).T[:, 0:1]


def keep_or_send(refs, step, value):
    if len(refs) == 1:
        refs[0][0] = value
        return

    @pl.when(step < 2)
    def _():
        refs[0][0] = value

    @pl.when(step >= 2)
    def _():
        refs[1][0] = value


def gate_back_kernel(
    order_ref, up_ref, weight_ref, gate_ref, mixed_ref, gain_ref, d_out_ref, stats_ref, *refs
):
    *branch_refs, grad_ref, d_mixed_ref, d_gate_ref, d_gain_ref, total = refs
    first = (pl.program_id(0) == 0) & (pl.program_id(1) == 0)
    last_one = pl.program_id(0) == pl.num_programs(0) - 1
    last_two = pl.program_id(1) == pl.num_programs(1) - 1

    @pl.when(first)
    def _():
        total[...] = jnp.zeros_like(total)
        d_gain_ref[...] = jnp.zeros_like(d_gain_ref)

    stats = stats_ref[0, 0]
    for k in range(1, stats_ref.shape[0]):
        stats = stats + stats_ref[k, 0]
    squares = row_to_lanes(stats[0:1])
    products = row_to_lanes(stats[1:2])
    scale = lax.rsqrt(squares * (1.0 / DI) + NORM_EPS)
    gate = gate_ref[0]
    mixed = mixed_ref[0]
    gain = gain_ref[...]
    d_out = d_out_ref[0]
    sig = sigmoid(gate)
    silu = gate * sig
    gated = mixed * silu
    unit = gated * scale
    low = (unit * gain).astype(BF16)
    keep_or_send(branch_refs, pl.program_id(1), dot(low, weight_ref[...]).astype(BF16))
    total[...] += dot(low, up_ref[0], COL_COL)
    d_gain_ref[...] += jnp.sum(d_out * unit, axis=0, keepdims=True)
    d_gated = scale * (gain * d_out - unit * (scale * products * (1.0 / DI)))
    d_mixed_ref[0] = d_gated * silu
    d_gate_ref[0] = (d_gated * mixed * (sig + silu * (1.0 - sig))).astype(BF16)

    @pl.when(last_one & last_two)
    def _():
        grad_ref[...] = total[...].astype(BF16)


def mixer_back_kernel(
    inner,
    rest_ref,
    rim_ref,
    mixed_ref,
    d_mixed_ref,
    incoming_ref,
    taps_ref,
    heads_ref,
    skip_ref,
    after_ref,
    d_rest_ref,
    d_taps_ref,
    d_heads_ref,
    d_skip_ref,
    padded,
    later,
    carried,
    d_active,
):
    rows = rest_ref.shape[1]
    conv = inner + 2 * NS
    block = pl.num_programs(0) - 1 - pl.program_id(0)

    @pl.when(pl.program_id(0) == 0)
    def _():
        d_taps_ref[...] = jnp.zeros_like(d_taps_ref)
        d_heads_ref[...] = jnp.zeros_like(d_heads_ref)
        d_skip_ref[...] = jnp.zeros_like(d_skip_ref)
        carried[...] = jnp.zeros_like(carried)
        later[rows : rows + RIM, :] = jnp.zeros((RIM, conv), F32)

    @pl.when(pl.program_id(0) > 0)
    def _():
        later[rows : rows + RIM, :] = later[0:RIM, :]

    rim = rim_ref[0][:, :conv]
    padded[0:RIM, :] = jnp.where(block > 0, rim, jnp.zeros_like(rim))
    padded[RIM : RIM + rows, :] = rest_ref[0][:, :conv]
    taps = taps_ref[...]
    conv_out = conv_forward(padded, taps, rows)
    sig = sigmoid(conv_out)
    active = conv_out * sig
    slope = sig + active * (1.0 - sig)
    heads = heads_ref[...]
    raw = rest_ref[0][:, conv:] + heads[0:1, :]
    step_all = softplus(raw)
    rate_all = heads[1:2, :] * step_all
    skip = skip_ref[...]
    spread = expander(inner)
    tri = lower_ones()
    upper = tri.T.astype(BF16)
    for c in reversed(range(rows // CHUNK)):
        part = slice(c * CHUNK, (c + 1) * CHUNK)
        values = active[part, :inner]
        in_b = active[part, inner : inner + NS].astype(BF16)
        out_c = active[part, inner + NS :].astype(BF16)
        step = step_all[part]
        rate = rate_all[part]
        cum, cum_t, step_x, grown, remain = decay_terms(step, rate, spread, tri)
        stepped = values * step_x
        stepped_low = stepped.astype(BF16)
        scores = dot(out_c, in_b, ROW_ROW) * tri
        d_mixed = d_mixed_ref[0, part, :]
        d_low = d_mixed.astype(BF16)
        d_scores = jnp.zeros((CHUNK, CHUNK), F32)
        inside = []
        for pair in range(inner // LANES):
            lanes = slice(pair * LANES, (pair + 1) * LANES)
            decays, mixing = pair_mixing(cum, cum_t, scores, pair)
            d_two = side_by_side(d_low[:, lanes])
            d_mixing = dot(d_two, stepped_low[:, lanes], ROW_ROW)
            d_scores += decays[0] * d_mixing[:CHUNK] + decays[1] * d_mixing[CHUNK:]
            inside.append(dot(jnp.concatenate(mixing, axis=0), d_two, COL_COL))
        before = incoming_ref[0, c]
        ahead = carried[...]
        ahead_low = ahead.astype(BF16)
        through = remain * dot(in_b, ahead_low)
        outer = (grown * d_mixed).astype(BF16)
        d_scores_low = (d_scores * tri).astype(BF16)
        d_in_b = dot((remain * stepped).astype(BF16), ahead_low, ROW_ROW) + dot(
            d_scores_low, out_c, COL_COL
        )
        d_out_c = dot(outer, before, ROW_ROW) + dot(d_scores_low, in_b)
        d_stepped = jnp.concatenate(inside, axis=1) + through
        stepped_near = stepped_low.astype(F32)
        both = d_low.astype(F32) * (mixed_ref[0, part, :] - skip * values)
        d_cum_x = both - stepped_near * d_stepped
        d_step_x = d_stepped * values
        grown_total = grown[CHUNK - 1 : CHUNK, :]
        d_total_x = jnp.sum(stepped_near * through, axis=0, keepdims=True) + grown_total * jnp.sum(
            ahead * before.astype(F32), axis=0, keepdims=True
        )
        gathered = jnp.concatenate(
            [d_cum_x, d_step_x, jnp.broadcast_to(d_total_x, (16, inner))], axis=0
        )
        narrow = sum(dot(part, spread, ROW_ROW) for part in terms(gathered, 2))
        d_rate = sum_dot(upper, narrow[:CHUNK], 2) + narrow[2 * CHUNK : 2 * CHUNK + 1]
        d_raw = (narrow[CHUNK : 2 * CHUNK] + heads[1:2, :] * d_rate) * sigmoid(raw[part])
        d_heads_ref[0:1, :] += jnp.sum(d_raw, axis=0, keepdims=True)
        d_heads_ref[1:2, :] += jnp.sum(d_rate * rate, axis=0, keepdims=True)
        d_skip_ref[...] += jnp.sum(d_mixed * values, axis=0, keepdims=True)
        d_rest_ref[0, part, conv:] = d_raw.astype(BF16)
        d_active[part, :inner] = d_stepped * step_x + skip * d_mixed
        d_active[part, inner : inner + NS] = d_in_b
        d_active[part, inner + NS :] = d_out_c
        carried[...] = grown_total * ahead + dot(out_c, outer, COL_COL)
    d_conv_out = d_active[...] * slope
    later[0:rows, :] = d_conv_out
    d_conv_in = jnp.zeros((rows, conv), F32)
    for k in range(KCONV):
        ahead_rows = KCONV - 1 - k
        start = RIM - (KCONV - 1) + k
        d_conv_in += taps[k : k + 1, :] * later[ahead_rows : ahead_rows + rows, :]
        d_taps_ref[k : k + 1, :] += jnp.sum(
            d_conv_out * padded[start : start + rows, :], axis=0, keepdims=True
        )
    d_taps_ref[KCONV : KCONV + 1, :] += jnp.sum(d_conv_out, axis=0, keepdims=True)
    d_rest_ref[0, :, :conv] = d_conv_in.astype(BF16)


def norm_back_kernel(
    order_ref, d_gate_ref, d_rest_ref, weight_gate_ref, weight_rest_ref, tokens_ref, after_ref, *refs
):
    *d_normed_refs, d_gain_ref = refs

    @pl.when(pl.program_id(0) == 0)
    def _():
        d_gain_ref[...] = jnp.zeros_like(d_gain_ref)

    d_normed = dot(d_gate_ref[0], weight_gate_ref[...], ROW_ROW) + dot(
        d_rest_ref[0], weight_rest_ref[...], ROW_ROW
    )
    tokens = tokens_ref[0].astype(F32)
    scale = lax.rsqrt(jnp.mean(tokens * tokens, axis=1, keepdims=True) + NORM_EPS)
    d_gain_ref[...] += jnp.sum(d_normed * (tokens * scale), axis=0, keepdims=True)
    keep_or_send(d_normed_refs, pl.program_id(0), d_normed.astype(BF16))


def whole(shape):
    return pl.BlockSpec(shape, lambda *_: (0,) * len(shape))


def by_rows(width):
    return pl.BlockSpec((1, ROWS, width), lambda s, b, *_: (s, b, 0))


def by_order(width):
    return pl.BlockSpec((1, ROWS, width), lambda s, b, order: (s, order[b], 0))


def left_alone():
    return pl.BlockSpec(memory_space=pl.ANY)


def cost(micros):
    return pl.CostEstimate(
        flops=int(micros * 1.1e9), bytes_accessed=int(micros * 2e6), transcendentals=0
    )


def params():
    return pltpu.CompilerParams(
        vmem_limit_bytes=VMEM_BYTES
    )


def shaped(shape, dtype=F32):
    return jax.ShapeDtypeStruct(shape, dtype)


def run_forward(tokens, norm_gain, weight, taps, heads, skip):
    count, length, _ = tokens.shape
    inner = skip.shape[1]
    rest = weight.shape[1]
    conv = inner + 2 * NS
    chunks = ROWS // CHUNK
    return pl.pallas_call(
        functools.partial(forward_kernel, inner),
        grid=(count, length // ROWS),
        in_specs=[
            by_rows(D),
            whole((1, D)),
            whole((D, rest)),
            whole((RIM, conv)),
            whole((8, LANES)),
            whole((1, inner)),
        ],
        out_specs=[
            by_rows(D),
            by_rows(rest),
            by_rows(inner),
            pl.BlockSpec((1, chunks, NS, inner), lambda s, b: (s, b, 0, 0)),
        ],
        out_shape=[
            shaped((count, length, D), BF16),
            shaped((count, length, rest)),
            shaped((count, length, inner)),
            shaped((count, length // CHUNK, NS, inner), BF16),
        ],
        scratch_shapes=[pltpu.VMEM((RIM + ROWS, conv), F32), pltpu.VMEM((NS, inner), F32)],
        compiler_params=params(),
        cost_estimate=cost(22),
        name="forward_mixer",
    )(tokens, norm_gain, weight, taps, heads, skip)


def run_stats(place, upstream, low, weight_gate, mixed, gate_gain, blocks):
    count, length, inner = mixed.shape
    return pl.pallas_call(
        stats_kernel,
        grid_spec=pltpu.PrefetchScalarGridSpec(
            num_scalar_prefetch=1,
            grid=(count, length // ROWS),
            in_specs=[
                by_rows(D),
                by_rows(D),
                whole((D, inner)),
                by_rows(inner),
                whole((1, inner)),
            ]
            + [whole(block.shape) for block in blocks],
            out_specs=[
                by_rows(inner),
                by_rows(inner),
                pl.BlockSpec((1, 2, ROWS), lambda s, b, *_: (s, 0, b)),
                whole((inner, D)),
            ],
        ),
        out_shape=[
            shaped((count, length, inner)),
            shaped((count, length, inner)),
            shaped((count, 2, length)),
            shaped((inner, D), BF16),
        ],
        compiler_params=params(),
        cost_estimate=cost(11),
        name="gate_stats",
    )(place, upstream, low, weight_gate, mixed, gate_gain, *blocks)


def kept_and_sent(split, count, length, place):
    if not split:
        return [place(lambda order, b: order[b])], [shaped((count, length, D), BF16)]
    specs = [
        place(lambda order, b: jnp.minimum(b, 1)),
        place(lambda order, b: jnp.maximum(b - 2, 0)),
    ]
    return specs, [shaped((count, 2 * ROWS, D), BF16)] * 2


def run_gate_back(split, order, upstream, weight, gate, mixed, gate_gain, d_out, stats):
    count, length, inner = gate.shape

    def place(group):
        return pl.BlockSpec((1, ROWS, D), lambda s, b, order: (s, group(order, b), 0))

    branch_specs, branch_shapes = kept_and_sent(split, count, length, place)
    return pl.pallas_call(
        gate_back_kernel,
        grid_spec=pltpu.PrefetchScalarGridSpec(
            num_scalar_prefetch=1,
            grid=(count, length // ROWS),
            in_specs=[
                by_order(D),
                whole((inner, D)),
                by_order(inner),
                by_order(inner),
                whole((1, inner)),
                by_order(inner),
                pl.BlockSpec(
                    (stats.shape[0], 1, 2, ROWS), lambda s, b, order: (0, s, 0, order[b])
                ),
            ],
            out_specs=branch_specs
            + [whole((inner, D)), by_order(inner), by_order(inner), whole((1, inner))],
            scratch_shapes=[pltpu.VMEM((inner, D), F32)],
        ),
        out_shape=branch_shapes
        + [
            shaped((inner, D), BF16),
            shaped((count, length, inner)),
            shaped((count, length, inner), BF16),
            shaped((1, inner)),
        ],
        compiler_params=params(),
        cost_estimate=cost(13),
        name="gate_back",
    )(order, upstream, weight, gate, mixed, gate_gain, d_out, stats)


def run_mixer_back(s, rest, mixed, d_mixed, incoming, taps, heads, skip, after):
    _, length, inner = mixed.shape
    conv = inner + 2 * NS
    last = length // ROWS - 1
    chunks = ROWS // CHUNK
    width = rest.shape[2]

    def rows(width, s=s):
        return pl.BlockSpec((1, ROWS, width), lambda b: (s, last - b, 0))

    return pl.pallas_call(
        functools.partial(mixer_back_kernel, inner),
        grid=(length // ROWS,),
        in_specs=[
            rows(width),
            pl.BlockSpec(
                (1, RIM, width),
                lambda b: (s, jnp.maximum((last - b) * (ROWS // RIM) - 1, 0), 0),
            ),
            rows(inner),
            rows(inner),
            pl.BlockSpec((1, chunks, NS, inner), lambda b: (s, last - b, 0, 0)),
            whole((RIM, conv)),
            whole((8, LANES)),
            whole((1, inner)),
            left_alone(),
        ],
        out_specs=[rows(width, 0), whole((RIM, conv)), whole((8, LANES)), whole((1, inner))],
        scratch_shapes=[
            pltpu.VMEM((RIM + ROWS, conv), F32),
            pltpu.VMEM((RIM + ROWS, conv), F32),
            pltpu.VMEM((NS, inner), F32),
            pltpu.VMEM((ROWS, conv), F32),
        ],
        out_shape=[
            shaped((1, length, width), BF16),
            shaped((RIM, conv)),
            shaped((8, LANES)),
            shaped((1, inner)),
        ],
        compiler_params=params(),
        cost_estimate=cost(19),
        name="mixer_back",
    )(rest, rest, mixed, d_mixed, incoming, taps, heads, skip, after)


def run_norm_back(split, s, order, d_gate, d_rest, weight_gate, weight_rest, tokens, after):
    _, length, inner = d_gate.shape
    width = d_rest.shape[2]

    def rows(width, s):
        return pl.BlockSpec((1, ROWS, width), lambda b, order: (s, order[b], 0))

    def place(group):
        return pl.BlockSpec((1, ROWS, D), lambda b, order: (0, group(order, b), 0))

    specs, shapes = kept_and_sent(split, 1, length, place)
    return pl.pallas_call(
        norm_back_kernel,
        grid_spec=pltpu.PrefetchScalarGridSpec(
            num_scalar_prefetch=1,
            grid=(length // ROWS,),
            in_specs=[
                rows(inner, s),
                rows(width, 0),
                whole(weight_gate.shape),
                whole(weight_rest.shape),
                rows(D, s),
                left_alone(),
            ],
            out_specs=specs + [whole((1, D))],
        ),
        out_shape=shapes + [shaped((1, D))],
        compiler_params=params(),
        cost_estimate=cost(6),
        name="norm_back",
    )(order, d_gate, d_rest, weight_gate, weight_rest, tokens, after)


BOTH = ("dp", "ctx")


def swapped(value, axis, mask):
    count = lax.axis_size(axis)
    return lax.ppermute(value, axis, [(a, a ^ mask) for a in range(count)])


def gather_blocks(block):
    if lax.axis_size("dp") != 8:
        return [lax.all_gather(block, "dp", axis=0, tiled=True)]
    far, near, side = (swapped(block, "dp", mask) for mask in (4, 2, 1))
    far_near, far_side = swapped(far, "dp", 2), swapped(far, "dp", 1)
    near_side = swapped(near, "dp", 1)
    every = swapped(far_near, "dp", 1)
    return [block, side, near, near_side, far, far_side, far_near, every]


def chip_sums(parts):
    if len(parts) == 1:
        total = lax.psum_scatter(parts[0], "ctx", scatter_dimension=1, tiled=True)
        return total.astype(F32), None
    kept, sent = parts
    got = swapped(sent, "ctx", 1)
    own = kept[:, :ROWS].astype(F32) + got[:, :ROWS].astype(F32)
    return own, (kept[:, ROWS:].astype(F32) + got[:, ROWS:].astype(F32)).astype(BF16)


def across_sums(own, sent):
    if sent is None:
        return own
    return own + swapped(sent, "ctx", 2).astype(F32)


def sum_over_dp(value):
    if lax.axis_size("dp") != 8:
        return lax.psum(value, "dp")
    for mask in (1, 2, 4):
        value = value + swapped(value, "dp", mask)
    return value


def adam_step(weight, first_old, second_old, gradient, step_rate):
    first_new = BETA_ONE * first_old + (1.0 - BETA_ONE) * gradient
    second_new = BETA_TWO * second_old + (1.0 - BETA_TWO) * gradient * gradient
    first_hat = first_new / (1.0 - BETA_ONE**STEP)
    second_hat = second_new / (1.0 - BETA_TWO**STEP)
    weight_new = weight - step_rate * (
        first_hat / (jnp.sqrt(second_hat) + ADAM_EPS) + DECAY_WEIGHT * weight
    )
    return (second_new, weight_new)


def pad_lanes(value, width):
    return jnp.pad(value, [(0, 0)] * (value.ndim - 1) + [(0, width - value.shape[-1])])


def shards(
    block_in,
    out_grad,
    w_in,
    w_in_m,
    w_in_v,
    w_out,
    w_out_m,
    w_out_v,
    small_params,
    small_m,
    small_v,
):
    n_dp, n_ctx = lax.axis_size("dp"), lax.axis_size("ctx")
    rank = lax.axis_index("ctx")
    heads = HEADS // n_ctx
    inner = heads * HD
    conv = inner + 2 * NS
    count = block_in.shape[0]

    moves = []
    for block in range(n_dp * n_ctx):
        moves.append((block, (block % n_dp) * n_ctx + block // n_dp))
    mine_out = lax.ppermute(w_out.astype(BF16), BOTH, moves)
    w_in_low = w_in.astype(BF16)
    slices = []
    for r in range(n_ctx):
        first = DI + CHANNELS + r * heads
        slices.append(
            jnp.concatenate(
                [
                    w_in_low[:, DI + r * inner : DI + (r + 1) * inner],
                    w_in_low[:, 2 * DI : 2 * DI + 2 * NS],
                    pad_lanes(w_in_low[:, first : first + heads], LANES),
                ],
                axis=1,
            )
        )

    def to_ranks(slices):
        stacked = jnp.stack(slices)
        sent = jnp.broadcast_to(stacked[None], (n_dp,) + stacked.shape)
        sent = sent.reshape(-1, stacked.shape[2])
        return lax.all_to_all(sent, BOTH, split_axis=0, concat_axis=0, tiled=True)

    tokens = lax.all_gather(block_in, "ctx", axis=1, tiled=True)
    upstream = lax.all_gather(out_grad, "ctx", axis=1, tiled=True)
    weight_rest = to_ranks(slices)
    weight_gate = to_ranks([w_in_low[:, r * inner : (r + 1) * inner] for r in range(n_ctx)])
    blocks_out = gather_blocks(mine_out)

    offset = 0
    pieces = []
    for amount in (D, DI, KCONV * CHANNELS, CHANNELS, HEADS, HEADS, HEADS):
        pieces.append(small_params[offset : offset + amount])
        offset = offset + amount
    norm_gain = pieces[0].reshape(1, D)
    gate_gain = lax.dynamic_slice(pieces[1], (rank * inner,), (inner,)).reshape(1, inner)
    taps_all = jnp.concatenate([pieces[2].reshape(KCONV, CHANNELS), pieces[3][None]], axis=0)
    taps = jnp.concatenate(
        [lax.dynamic_slice(taps_all, (0, rank * inner), (KCONV + 1, inner)), taps_all[:, DI:]],
        axis=1,
    )
    taps = jnp.pad(taps, ((0, RIM - KCONV - 1), (0, 0)))
    dt_bias = lax.dynamic_slice(pieces[4], (rank * heads,), (heads,))
    decay = -jnp.exp(lax.dynamic_slice(pieces[5], (rank * heads,), (heads,)))
    head_rows = jnp.pad(jnp.stack([dt_bias, decay]), ((0, 6), (0, LANES - heads)))
    skip = jnp.repeat(lax.dynamic_slice(pieces[6], (rank * heads,), (heads,)), HD).reshape(1, inner)

    split = n_ctx == 4 and block_in.shape[1] == ROWS
    place = lax.axis_index("dp") if len(blocks_out) > 1 else rank * 0
    place = place.astype(jnp.int32).reshape(1)
    order = jnp.arange(n_ctx * block_in.shape[1] // ROWS, dtype=jnp.int32)
    if split:
        order = rank.astype(jnp.int32) ^ jnp.array([0, 2, 1, 3], jnp.int32)
    low, rest, mixed, incoming = run_forward(tokens, norm_gain, weight_rest, taps, head_rows, skip)
    gate, d_out, stats, weight_out = run_stats(
        place, upstream, low, weight_gate, mixed, gate_gain, blocks_out
    )
    stats = lax.all_gather(stats, "ctx")
    *branch, grad_out, d_mixed, d_gate, d_gate_gain = run_gate_back(
        split, order, upstream, weight_out, gate, mixed, gate_gain, d_out, stats
    )
    grad_out = lax.all_to_all(grad_out, "dp", split_axis=0, concat_axis=0, tiled=True)
    branch, branch_sent = chip_sums(branch)

    def to_owners(grad):
        return lax.all_to_all(grad.astype(BF16), BOTH, split_axis=0, concat_axis=0, tiled=True)

    def summed(got):
        return jnp.sum(got.astype(F32).reshape(n_dp, n_ctx, -1, got.shape[1]), axis=0)

    grad_gate = dot(low.reshape(-1, D), d_gate.reshape(-1, inner), COL_COL).astype(BF16)
    after = grad_gate if branch_sent is None else branch_sent
    branch = across_sums(branch, branch_sent)
    grad_rest = 0.0
    smalls = []
    normeds = []
    for s in range(count):
        d_rest, *small = run_mixer_back(
            s, rest, mixed, d_mixed, incoming, taps, head_rows, skip, after
        )
        grad_rest = grad_rest + dot(low[s], d_rest[0], COL_COL)
        if s == 0:
            after = grad_out
            grad_gate = to_owners(grad_gate)
        if s == count - 1:
            grad_rest = grad_rest.astype(BF16)
            after = grad_rest
            grad_rest = to_owners(grad_rest)
        *d_normed, d_gain = run_norm_back(
            split, s, order, d_gate, d_rest, weight_gate, weight_rest, tokens, after
        )
        smalls.append([d_gain] + small)
        d_normed, normed_sent = chip_sums(d_normed)
        after = d_normed if normed_sent is None else normed_sent
        normeds.append(across_sums(d_normed, normed_sent))
    d_normed = jnp.concatenate(normeds, axis=0)
    d_norm_gain, d_taps, d_heads, d_skip = (sum(parts) for parts in zip(*smalls))
    grad_out = jnp.sum(grad_out.astype(F32).reshape(n_dp, -1, D), axis=0)
    grad_out = lax.ppermute(grad_out, BOTH, [(b, a) for a, b in moves])
    grad_gate = summed(grad_gate)
    grad_rest = summed(grad_rest)
    columns = [grad_gate[r] for r in range(n_ctx)]
    columns += [grad_rest[r, :, :inner] for r in range(n_ctx)]
    columns += [jnp.sum(grad_rest[:, :, inner:conv], axis=0)]
    columns += [grad_rest[r, :, conv : conv + heads] for r in range(n_ctx)]
    grad_in = jnp.concatenate(columns, axis=1)

    parts = (
        d_norm_gain.reshape(-1),
        d_gate_gain.reshape(-1),
        d_taps[: KCONV + 1].reshape(-1),
        d_heads[0, :heads],
        d_heads[1, :heads],
        jnp.sum(d_skip.reshape(heads, HD), axis=1),
    )
    mine = jnp.concatenate(parts)
    mine = jnp.pad(mine, (0, -mine.shape[0] % (8 * LANES))).reshape(-1, LANES)
    every = lax.all_gather(sum_over_dp(mine), "ctx", axis=0).reshape(n_ctx, -1)
    offset = 0
    found = []
    for part in parts:
        found.append(every[:, offset : offset + part.shape[0]])
        offset = offset + part.shape[0]
    taps_found = found[2].reshape(n_ctx, KCONV + 1, conv)
    taps_found = jnp.concatenate(
        [
            jnp.swapaxes(taps_found[:, :, :inner], 0, 1).reshape(KCONV + 1, DI),
            jnp.sum(taps_found[:, :, inner:], axis=0),
        ],
        axis=1,
    )
    grad_small = jnp.concatenate(
        [jnp.sum(found[0], axis=0), found[1].reshape(-1), taps_found.reshape(-1)]
        + [found[k].reshape(-1) for k in (3, 4, 5)]
    )

    own = block_in.astype(F32)
    block_out = (own + branch.astype(F32)).astype(BF16)
    scale = lax.rsqrt(jnp.mean(own * own, axis=-1, keepdims=True) + NORM_EPS)
    d_scaled = d_normed * norm_gain
    d_own = scale * (
        d_scaled - own * scale * scale * jnp.mean(d_scaled * own, axis=-1, keepdims=True)
    )
    input_grad = (out_grad.astype(F32) + d_own).astype(BF16)
    in_second, in_new = adam_step(w_in, w_in_m, w_in_v, grad_in, RATE_BIG)
    out_second, out_new = adam_step(w_out, w_out_m, w_out_v, grad_out, RATE_BIG)
    small_second, small_updated = adam_step(small_params, small_m, small_v, grad_small, RATE_SMALL)
    return (
        block_out,
        input_grad,
        grad_in,
        in_second,
        in_new,
        grad_out,
        out_second,
        out_new,
        grad_small,
        small_second,
        small_updated,
    )


def solution(mesh):
    rows = P(("dp", "ctx"), None)
    spread = P("dp", "ctx", None)
    return jax.shard_map(
        shards,
        mesh=mesh,
        in_specs=(spread, spread) + (rows,) * 6 + (P(),) * 3,
        out_specs=(spread, spread) + (rows,) * 6 + (P(),) * 3,
        check_vma=False,
    )
```

```python
import functools

import jax
import jax.numpy as jnp
import numpy as np
from jax import lax
from jax.experimental import pallas as pl
from jax.experimental.pallas import tpu as pltpu
from jax.sharding import Mesh
from jax.sharding import PartitionSpec as P

D = 1024
HEADS = 32
HD = 64
NS = 128
KCONV = 4
STEP = 10
DI = 2048
CHANNELS = DI + 2 * NS

CHUNK = 128
LANES = 128
RIM = 8
ROWS = 256

NORM_EPS = 1e-05
ADAM_EPS = 1e-08
BETA_ONE = 0.9
BETA_TWO = 0.999
RATE_BIG = 0.03
RATE_SMALL = 0.3
DECAY_WEIGHT = 0.01

F32 = jnp.float32
BF16 = jnp.bfloat16
VMEM_BYTES = 48 * 1024 * 1024


def dot(a, b, contract=((1,), (0,))):
    return lax.dot_general(a, b, (contract, ((), ())), preferred_element_type=F32)


def terms(a, count):
    parts = []
    for _ in range(count):
        part = a.astype(BF16)
        parts.append(part)
        a = a - part.astype(F32)
    return parts


def spread_dot(a, spread):
    return dot(
        jnp.concatenate(terms(a, 2), axis=1), jnp.concatenate([spread, spread], axis=0)
    )


def sum_dot(ones, a, count):
    return sum(dot(ones, part) for part in terms(a, count))


ROW_ROW = ((1,), (1,))
COL_COL = ((0,), (0,))


def sigmoid(v):
    return 1.0 / (1.0 + jnp.exp(-v))


def softplus(v):
    return jnp.maximum(v, 0.0) + jnp.log1p(jnp.exp(-jnp.abs(v)))


def expander(inner):
    head = lax.broadcasted_iota(jnp.int32, (LANES, inner), 0)
    column = lax.broadcasted_iota(jnp.int32, (LANES, inner), 1)
    inside = (column >= head * HD) & (column < (head + 1) * HD)
    return jnp.where(inside, 1.0, 0.0).astype(BF16)


def lower_ones():
    row = lax.broadcasted_iota(jnp.int32, (CHUNK, CHUNK), 0)
    column = lax.broadcasted_iota(jnp.int32, (CHUNK, CHUNK), 1)
    return jnp.where(row >= column, 1.0, 0.0)


def row_sums(a):
    lanes = a[:, :LANES]
    for start in range(LANES, a.shape[1], LANES):
        lanes = lanes + a[:, start : start + LANES]
    return jnp.sum(lanes.T, axis=0, keepdims=True)


def side_by_side(pair):
    lane = lax.broadcasted_iota(jnp.int32, pair.shape, 1)
    zero = jnp.zeros_like(pair)
    return jnp.concatenate(
        [jnp.where(lane < HD, pair, zero), jnp.where(lane < HD, zero, pair)], axis=0
    )


def decay_terms(step, rate, spread, tri):
    cum = sum_dot(tri.astype(BF16), rate, 3)
    total = cum[CHUNK - 1 : CHUNK, :]
    wide = spread_dot(
        jnp.concatenate([step, jnp.exp(cum), jnp.exp(total - cum)], axis=0), spread
    )
    return cum, cum.T, wide[:CHUNK], wide[CHUNK : 2 * CHUNK], wide[2 * CHUNK :]


def pair_mixing(cum, cum_t, scores, pair):
    decays = []
    for head in (2 * pair, 2 * pair + 1):
        differ = cum[:, head : head + 1] - cum_t[head : head + 1, :]
        decays.append(jnp.exp(jnp.minimum(differ, 0.0)))
    return decays, [(decay * scores).astype(BF16) for decay in decays]


def conv_forward(padded_ref, taps, rows):
    total = taps[KCONV : KCONV + 1, :]
    for k in range(KCONV):
        start = RIM - (KCONV - 1) + k
        total = total + taps[k : k + 1, :] * padded_ref[start : start + rows, :]
    return total


def forward_kernel(
    inner,
    order_ref,
    tokens_ref,
    gain_ref,
    taps_ref,
    heads_ref,
    skip_ref,
    mine_ref,
    other_ref,
    low_ref,
    rest_ref,
    mixed_ref,
    incoming_ref,
    weight_ref,
    padded,
    state,
):
    rows = tokens_ref.shape[1]
    conv = inner + 2 * NS

    @pl.when((pl.program_id(0) == 0) & (pl.program_id(1) == 0))
    def _():
        if mine_ref.shape[0] == D:
            weight_ref[...] = mine_ref[...]
        else:
            mine = pl.multiple_of(order_ref[0] * (D // 2), D // 2)
            other = pl.multiple_of((1 - order_ref[0]) * (D // 2), D // 2)
            weight_ref[pl.ds(mine, D // 2), :] = mine_ref[...]
            weight_ref[pl.ds(other, D // 2), :] = other_ref[...]

    @pl.when(pl.program_id(1) == 0)
    def _():
        padded[0:RIM, :] = jnp.zeros((RIM, conv), F32)
        state[...] = jnp.zeros_like(state)

    @pl.when(pl.program_id(1) > 0)
    def _():
        padded[0:RIM, :] = padded[rows : rows + RIM, :]

    tokens_low = tokens_ref[0]
    tokens = tokens_low.astype(F32)
    scale = lax.rsqrt(jnp.mean(tokens * tokens, axis=1, keepdims=True) + NORM_EPS)
    low = (tokens * scale * gain_ref[...]).astype(BF16)
    low_ref[0] = low
    projected = dot(low, weight_ref[...])
    rest_ref[0] = projected
    padded[RIM : RIM + rows, :] = projected[:, :conv]
    conv_out = conv_forward(padded, taps_ref[...], rows)
    active = conv_out * sigmoid(conv_out)
    heads = heads_ref[...]
    step_all = softplus(projected[:, conv:] + heads[0:1, :])
    rate_all = heads[1:2, :] * step_all
    skip = skip_ref[...]
    spread = expander(inner)
    tri = lower_ones()
    for c in range(rows // CHUNK):
        part = slice(c * CHUNK, (c + 1) * CHUNK)
        values = active[part, :inner]
        in_b = active[part, inner : inner + NS].astype(BF16)
        out_c = active[part, inner + NS :].astype(BF16)
        cum, cum_t, step_x, grown, remain = decay_terms(
            step_all[part], rate_all[part], spread, tri
        )
        stepped = values * step_x
        stepped_low = stepped.astype(BF16)
        scores = dot(out_c, in_b, ROW_ROW) * tri
        inside = []
        for pair in range(inner // LANES):
            lanes = slice(pair * LANES, (pair + 1) * LANES)
            _, mixing = pair_mixing(cum, cum_t, scores, pair)
            inside.append(
                dot(jnp.concatenate(mixing, axis=1), side_by_side(stepped_low[:, lanes]))
            )
        before = state[...]
        before_low = before.astype(BF16)
        incoming_ref[0, c] = before_low
        outer = grown * dot(out_c, before_low)
        mixed_ref[0, part, :] = jnp.concatenate(inside, axis=1) + outer + skip * values
        state[...] = grown[CHUNK - 1 : CHUNK, :] * before + dot(
            in_b, (remain * stepped).astype(BF16), COL_COL
        )


def stats_kernel(joined, order_ref, up_ref, low_ref, mixed_ref, gain_ref, *refs):
    if joined:
        both_ref, weight_out_ref, weight_gate_ref, gate_ref, d_out_ref, stats_ref = refs
        inner = gate_ref.shape[2]

        @pl.when((pl.program_id(0) == 0) & (pl.program_id(1) == 0))
        def _():
            deep, tall = D // 8, inner // 8
            place = 0
            for quarter in range(4):
                for half in (order_ref[0], 1 - order_ref[0]):
                    block = half * 4 + quarter
                    rows = pl.ds(pl.multiple_of(block * deep, deep), deep)
                    weight_gate_ref[rows, :] = both_ref[place : place + deep, :]
                    place = place + deep
                    rows = pl.ds(pl.multiple_of(block * tall, tall), tall)
                    for k in range(D // inner):
                        columns = slice(k * inner, (k + 1) * inner)
                        weight_out_ref[rows, columns] = both_ref[place : place + tall, :]
                        place = place + tall

    else:
        weight_out_ref, weight_gate_ref, gate_ref, d_out_ref, stats_ref = refs
    d_out = dot(up_ref[0], weight_out_ref[...], ROW_ROW)
    d_out_ref[0] = d_out
    gate = dot(low_ref[0], weight_gate_ref[...])
    gate_ref[0] = gate
    gated = mixed_ref[0] * gate * sigmoid(gate)
    stats_ref[0, 0:1, :] = row_sums(gated * gated)
    stats_ref[0, 1:2, :] = row_sums(d_out * gain_ref[...] * gated)


def row_to_lanes(row):
    return jnp.broadcast_to(row, (LANES, row.shape[1])).T[:, 0:1]


def keep_or_send(refs, step, value):
    if len(refs) == 1:
        refs[0][0] = value
        return

    @pl.when(step < 2)
    def _():
        refs[0][0] = value

    @pl.when(step >= 2)
    def _():
        refs[1][0] = value


def gate_back_kernel(
    order_ref, up_ref, weight_ref, gate_ref, mixed_ref, gain_ref, d_out_ref, stats_ref, *refs
):
    *branch_refs, grad_ref, d_mixed_ref, d_gate_ref, d_gain_ref, total = refs
    first = (pl.program_id(0) == 0) & (pl.program_id(1) == 0)
    last_one = pl.program_id(0) == pl.num_programs(0) - 1
    last_two = pl.program_id(1) == pl.num_programs(1) - 1

    @pl.when(first)
    def _():
        total[...] = jnp.zeros_like(total)
        d_gain_ref[...] = jnp.zeros_like(d_gain_ref)

    stats = stats_ref[0, 0]
    for k in range(1, stats_ref.shape[0]):
        stats = stats + stats_ref[k, 0]
    squares = row_to_lanes(stats[0:1])
    products = row_to_lanes(stats[1:2])
    scale = lax.rsqrt(squares * (1.0 / DI) + NORM_EPS)
    gate = gate_ref[0]
    mixed = mixed_ref[0]
    gain = gain_ref[...]
    d_out = d_out_ref[0]
    sig = sigmoid(gate)
    silu = gate * sig
    gated = mixed * silu
    unit = gated * scale
    low = (unit * gain).astype(BF16)
    keep_or_send(branch_refs, pl.program_id(1), dot(low, weight_ref[...]).astype(BF16))
    total[...] += dot(low, up_ref[0], COL_COL)
    d_gain_ref[...] += jnp.sum(d_out * unit, axis=0, keepdims=True)
    d_gated = scale * (gain * d_out - unit * (scale * products * (1.0 / DI)))
    d_mixed_ref[0] = d_gated * silu
    d_gate_ref[0] = (d_gated * mixed * (sig + silu * (1.0 - sig))).astype(BF16)

    @pl.when(last_one & last_two)
    def _():
        grad_ref[...] = total[...].astype(BF16)


def mixer_back_kernel(
    inner,
    rest_ref,
    rim_ref,
    mixed_ref,
    d_mixed_ref,
    incoming_ref,
    taps_ref,
    heads_ref,
    skip_ref,
    after_ref,
    before_ref,
    d_rest_ref,
    d_taps_ref,
    d_heads_ref,
    d_skip_ref,
    padded,
    later,
    carried,
    d_active,
):
    rows = rest_ref.shape[1]
    conv = inner + 2 * NS
    block = pl.num_programs(0) - 1 - pl.program_id(0)

    @pl.when(pl.program_id(0) == 0)
    def _():
        d_taps_ref[...] = jnp.zeros_like(d_taps_ref)
        d_heads_ref[...] = jnp.zeros_like(d_heads_ref)
        d_skip_ref[...] = jnp.zeros_like(d_skip_ref)
        carried[...] = jnp.zeros_like(carried)
        later[rows : rows + RIM, :] = jnp.zeros((RIM, conv), F32)

    @pl.when(pl.program_id(0) > 0)
    def _():
        later[rows : rows + RIM, :] = later[0:RIM, :]

    rim = rim_ref[0][:, :conv]
    padded[0:RIM, :] = jnp.where(block > 0, rim, jnp.zeros_like(rim))
    padded[RIM : RIM + rows, :] = rest_ref[0][:, :conv]
    taps = taps_ref[...]
    conv_out = conv_forward(padded, taps, rows)
    sig = sigmoid(conv_out)
    active = conv_out * sig
    slope = sig + active * (1.0 - sig)
    heads = heads_ref[...]
    raw = rest_ref[0][:, conv:] + heads[0:1, :]
    step_all = softplus(raw)
    rate_all = heads[1:2, :] * step_all
    skip = skip_ref[...]
    spread = expander(inner)
    tri = lower_ones()
    upper = tri.T.astype(BF16)
    for c in reversed(range(rows // CHUNK)):
        part = slice(c * CHUNK, (c + 1) * CHUNK)
        values = active[part, :inner]
        in_b = active[part, inner : inner + NS].astype(BF16)
        out_c = active[part, inner + NS :].astype(BF16)
        step = step_all[part]
        rate = rate_all[part]
        cum, cum_t, step_x, grown, remain = decay_terms(step, rate, spread, tri)
        stepped = values * step_x
        stepped_low = stepped.astype(BF16)
        scores = dot(out_c, in_b, ROW_ROW) * tri
        d_mixed = d_mixed_ref[0, part, :]
        d_low = d_mixed.astype(BF16)
        d_scores = jnp.zeros((CHUNK, CHUNK), F32)
        inside = []
        for pair in range(inner // LANES):
            lanes = slice(pair * LANES, (pair + 1) * LANES)
            decays, mixing = pair_mixing(cum, cum_t, scores, pair)
            d_two = side_by_side(d_low[:, lanes])
            d_mixing = dot(d_two, stepped_low[:, lanes], ROW_ROW)
            d_scores += decays[0] * d_mixing[:CHUNK] + decays[1] * d_mixing[CHUNK:]
            inside.append(dot(jnp.concatenate(mixing, axis=0), d_two, COL_COL))
        before = incoming_ref[0, c]
        ahead = carried[...]
        ahead_low = ahead.astype(BF16)
        through = remain * dot(in_b, ahead_low)
        outer = (grown * d_mixed).astype(BF16)
        d_scores_low = (d_scores * tri).astype(BF16)
        d_in_b = dot((remain * stepped).astype(BF16), ahead_low, ROW_ROW) + dot(
            d_scores_low, out_c, COL_COL
        )
        d_out_c = dot(outer, before, ROW_ROW) + dot(d_scores_low, in_b)
        d_stepped = jnp.concatenate(inside, axis=1) + through
        stepped_near = stepped_low.astype(F32)
        both = d_low.astype(F32) * (mixed_ref[0, part, :] - skip * values)
        d_cum_x = both - stepped_near * d_stepped
        d_step_x = d_stepped * values
        grown_total = grown[CHUNK - 1 : CHUNK, :]
        d_total_x = jnp.sum(stepped_near * through, axis=0, keepdims=True) + grown_total * jnp.sum(
            ahead * before.astype(F32), axis=0, keepdims=True
        )
        gathered = jnp.concatenate(
            [d_cum_x, d_step_x, jnp.broadcast_to(d_total_x, (16, inner))], axis=0
        )
        narrow = sum(dot(part, spread, ROW_ROW) for part in terms(gathered, 2))
        d_rate = sum_dot(upper, narrow[:CHUNK], 2) + narrow[2 * CHUNK : 2 * CHUNK + 1]
        d_raw = (narrow[CHUNK : 2 * CHUNK] + heads[1:2, :] * d_rate) * sigmoid(raw[part])
        d_heads_ref[0:1, :] += jnp.sum(d_raw, axis=0, keepdims=True)
        d_heads_ref[1:2, :] += jnp.sum(d_rate * rate, axis=0, keepdims=True)
        d_skip_ref[...] += jnp.sum(d_mixed * values, axis=0, keepdims=True)
        d_rest_ref[0, part, conv:] = d_raw.astype(BF16)
        d_active[part, :inner] = d_stepped * step_x + skip * d_mixed
        d_active[part, inner : inner + NS] = d_in_b
        d_active[part, inner + NS :] = d_out_c
        carried[...] = grown_total * ahead + dot(out_c, outer, COL_COL)
    d_conv_out = d_active[...] * slope
    later[0:rows, :] = d_conv_out
    d_conv_in = jnp.zeros((rows, conv), F32)
    for k in range(KCONV):
        ahead_rows = KCONV - 1 - k
        start = RIM - (KCONV - 1) + k
        d_conv_in += taps[k : k + 1, :] * later[ahead_rows : ahead_rows + rows, :]
        d_taps_ref[k : k + 1, :] += jnp.sum(
            d_conv_out * padded[start : start + rows, :], axis=0, keepdims=True
        )
    d_taps_ref[KCONV : KCONV + 1, :] += jnp.sum(d_conv_out, axis=0, keepdims=True)
    d_rest_ref[0, :, :conv] = d_conv_in.astype(BF16)


def norm_back_kernel(
    order_ref, d_gate_ref, d_rest_ref, weight_gate_ref, weight_rest_ref, tokens_ref, after_ref, *refs
):
    *d_normed_refs, d_gain_ref = refs

    @pl.when(pl.program_id(0) == 0)
    def _():
        d_gain_ref[...] = jnp.zeros_like(d_gain_ref)

    d_normed = dot(d_gate_ref[0], weight_gate_ref[...], ROW_ROW) + dot(
        d_rest_ref[0], weight_rest_ref[...], ROW_ROW
    )
    tokens = tokens_ref[0].astype(F32)
    scale = lax.rsqrt(jnp.mean(tokens * tokens, axis=1, keepdims=True) + NORM_EPS)
    d_gain_ref[...] += jnp.sum(d_normed * (tokens * scale), axis=0, keepdims=True)
    keep_or_send(d_normed_refs, pl.program_id(0), d_normed.astype(BF16))


def whole(shape):
    return pl.BlockSpec(shape, lambda *_: (0,) * len(shape))


def by_rows(width):
    return pl.BlockSpec((1, ROWS, width), lambda s, b, *_: (s, b, 0))


def by_order(width):
    return pl.BlockSpec((1, ROWS, width), lambda s, b, order: (s, order[b], 0))


def left_alone():
    return pl.BlockSpec(memory_space=pl.ANY)


def cost(micros):
    return pl.CostEstimate(
        flops=int(micros * 1.1e9), bytes_accessed=int(micros * 2e6), transcendentals=0
    )


def params():
    return pltpu.CompilerParams(
        vmem_limit_bytes=VMEM_BYTES
    )


def shaped(shape, dtype=F32):
    return jax.ShapeDtypeStruct(shape, dtype)


def run_forward(order, tokens, norm_gain, halves, taps, heads, skip):
    count, length, _ = tokens.shape
    inner = skip.shape[1]
    rest = halves[0].shape[1]
    conv = inner + 2 * NS
    chunks = ROWS // CHUNK
    fixed = [norm_gain, taps, heads, skip, halves[0], halves[-1]]
    return pl.pallas_call(
        functools.partial(forward_kernel, inner),
        grid_spec=pltpu.PrefetchScalarGridSpec(
            num_scalar_prefetch=1,
            grid=(count, length // ROWS),
            in_specs=[by_rows(D)] + [whole(value.shape) for value in fixed],
            out_specs=[
                by_rows(D),
                by_rows(rest),
                by_rows(inner),
                pl.BlockSpec((1, chunks, NS, inner), lambda s, b, *_: (s, b, 0, 0)),
                whole((D, rest)),
            ],
            scratch_shapes=[pltpu.VMEM((RIM + ROWS, conv), F32), pltpu.VMEM((NS, inner), F32)],
        ),
        out_shape=[
            shaped((count, length, D), BF16),
            shaped((count, length, rest)),
            shaped((count, length, inner)),
            shaped((count, length // CHUNK, NS, inner), BF16),
            shaped((D, rest), BF16),
        ],
        compiler_params=params(),
        cost_estimate=cost(1),
        name="forward_mixer",
    )(order, tokens, *fixed)


def run_stats(order, upstream, low, mixed, gate_gain, weights):
    count, length, inner = mixed.shape
    joined = len(weights) == 1
    found_specs = [whole((inner, D)), whole((D, inner))] * joined
    found_shapes = [shaped((inner, D), BF16), shaped((D, inner), BF16)] * joined
    found = pl.pallas_call(
        functools.partial(stats_kernel, joined),
        grid_spec=pltpu.PrefetchScalarGridSpec(
            num_scalar_prefetch=1,
            grid=(count, length // ROWS),
            in_specs=[by_rows(D), by_rows(D), by_rows(inner), whole((1, inner))]
            + [whole(weight.shape) for weight in weights],
            out_specs=found_specs
            + [
                by_rows(inner),
                by_rows(inner),
                pl.BlockSpec((1, 2, ROWS), lambda s, b, *_: (s, 0, b)),
            ],
        ),
        out_shape=found_shapes
        + [
            shaped((count, length, inner)),
            shaped((count, length, inner)),
            shaped((count, 2, length)),
        ],
        compiler_params=params(),
        cost_estimate=cost(1),
        name="gate_stats",
    )(order, upstream, low, mixed, gate_gain, *weights)
    return found if joined else [*weights, *found]


def kept_and_sent(split, count, length, place):
    if not split:
        return [place(lambda order, b: order[b])], [shaped((count, length, D), BF16)]
    specs = [
        place(lambda order, b: jnp.minimum(b, 1)),
        place(lambda order, b: jnp.maximum(b - 2, 0)),
    ]
    return specs, [shaped((count, 2 * ROWS, D), BF16)] * 2


def run_gate_back(split, order, upstream, weight, gate, mixed, gate_gain, d_out, stats):
    count, length, inner = gate.shape

    def place(group):
        return pl.BlockSpec((1, ROWS, D), lambda s, b, order: (s, group(order, b), 0))

    branch_specs, branch_shapes = kept_and_sent(split, count, length, place)
    return pl.pallas_call(
        gate_back_kernel,
        grid_spec=pltpu.PrefetchScalarGridSpec(
            num_scalar_prefetch=1,
            grid=(count, length // ROWS),
            in_specs=[
                by_order(D),
                whole((inner, D)),
                by_order(inner),
                by_order(inner),
                whole((1, inner)),
                by_order(inner),
                pl.BlockSpec(
                    (stats.shape[0], 1, 2, ROWS), lambda s, b, order: (0, s, 0, order[b])
                ),
            ],
            out_specs=branch_specs
            + [whole((inner, D)), by_order(inner), by_order(inner), whole((1, inner))],
            scratch_shapes=[pltpu.VMEM((inner, D), F32)],
        ),
        out_shape=branch_shapes
        + [
            shaped((inner, D), BF16),
            shaped((count, length, inner)),
            shaped((count, length, inner), BF16),
            shaped((1, inner)),
        ],
        compiler_params=params(),
        cost_estimate=cost(1),
        name="gate_back",
    )(order, upstream, weight, gate, mixed, gate_gain, d_out, stats)


def run_mixer_back(s, rest, mixed, d_mixed, incoming, taps, heads, skip, after, before):
    count, length, inner = mixed.shape
    conv = inner + 2 * NS
    last = length // ROWS - 1
    chunks = ROWS // CHUNK
    width = rest.shape[2]

    def rows(width):
        return pl.BlockSpec((1, ROWS, width), lambda b: (s, last - b, 0))

    return pl.pallas_call(
        functools.partial(mixer_back_kernel, inner),
        grid=(length // ROWS,),
        in_specs=[
            rows(width),
            pl.BlockSpec(
                (1, RIM, width),
                lambda b: (s, jnp.maximum((last - b) * (ROWS // RIM) - 1, 0), 0),
            ),
            rows(inner),
            rows(inner),
            pl.BlockSpec((1, chunks, NS, inner), lambda b: (s, last - b, 0, 0)),
            whole((RIM, conv)),
            whole((8, LANES)),
            whole((1, inner)),
            left_alone(),
            left_alone(),
        ],
        out_specs=[rows(width), whole((RIM, conv)), whole((8, LANES)), whole((1, inner))],
        scratch_shapes=[
            pltpu.VMEM((RIM + ROWS, conv), F32),
            pltpu.VMEM((RIM + ROWS, conv), F32),
            pltpu.VMEM((NS, inner), F32),
            pltpu.VMEM((ROWS, conv), F32),
        ],
        out_shape=[
            shaped((count, length, width), BF16),
            shaped((RIM, conv)),
            shaped((8, LANES)),
            shaped((1, inner)),
        ],
        input_output_aliases={9: 0} if s > 0 else {},
        compiler_params=params(),
        cost_estimate=cost(1),
        name="mixer_back",
    )(rest, rest, mixed, d_mixed, incoming, taps, heads, skip, after, before)


def run_norm_back(split, s, order, d_gate, d_rest, weight_gate, weight_rest, tokens, after):
    _, length, inner = d_gate.shape
    width = d_rest.shape[2]

    def rows(width, s):
        return pl.BlockSpec((1, ROWS, width), lambda b, order: (s, order[b], 0))

    def place(group):
        return pl.BlockSpec((1, ROWS, D), lambda b, order: (0, group(order, b), 0))

    specs, shapes = kept_and_sent(split, 1, length, place)
    return pl.pallas_call(
        norm_back_kernel,
        grid_spec=pltpu.PrefetchScalarGridSpec(
            num_scalar_prefetch=1,
            grid=(length // ROWS,),
            in_specs=[
                rows(inner, s),
                rows(width, s),
                whole(weight_gate.shape),
                whole(weight_rest.shape),
                rows(D, s),
                left_alone(),
            ],
            out_specs=specs + [whole((1, D))],
        ),
        out_shape=shapes + [shaped((1, D))],
        compiler_params=params(),
        cost_estimate=cost(1),
        name="norm_back",
    )(order, d_gate, d_rest, weight_gate, weight_rest, tokens, after)


def swapped(value, axis, mask=1):
    count = lax.axis_size(axis)
    return lax.ppermute(value, axis, [(a, a ^ mask) for a in range(count)])


def chip_sums(parts):
    if len(parts) == 1:
        total = lax.psum_scatter(parts[0], "ctx", scatter_dimension=1, tiled=True)
        return total.astype(F32), None
    kept, sent = parts
    got = swapped(sent, "ctx", 1)
    own = kept[:, :ROWS].astype(F32) + got[:, :ROWS].astype(F32)
    return own, (kept[:, ROWS:].astype(F32) + got[:, ROWS:].astype(F32)).astype(BF16)


def across_sums(own, sent):
    if sent is None:
        return own
    return own + swapped(sent, "ctx", 2).astype(F32)


def sum_over(value, axes):
    if len(axes) == 1:
        return lax.psum(value, axes)
    for axis in axes:
        value = value + swapped(value, axis)
    return value


def to_all(value, axes):
    return lax.all_to_all(value, axes, split_axis=0, concat_axis=0, tiled=True)


def to_every(value, axes):
    times = 1
    for axis in axes:
        times = times * lax.axis_size(axis)
    return to_all(jnp.broadcast_to(value[None], (times,) + value.shape).reshape(-1, value.shape[1]), axes)


def adam_step(weight, first_old, second_old, gradient, step_rate):
    first_new = BETA_ONE * first_old + (1.0 - BETA_ONE) * gradient
    second_new = BETA_TWO * second_old + (1.0 - BETA_TWO) * gradient * gradient
    first_hat = first_new / (1.0 - BETA_ONE**STEP)
    second_hat = second_new / (1.0 - BETA_TWO**STEP)
    weight_new = weight - step_rate * (
        first_hat / (jnp.sqrt(second_hat) + ADAM_EPS) + DECAY_WEIGHT * weight
    )
    return (second_new, weight_new)


def pad_lanes(value, width):
    return jnp.pad(value, [(0, 0)] * (value.ndim - 1) + [(0, width - value.shape[-1])])


def shards(
    dp,
    block_in,
    out_grad,
    w_in,
    w_in_m,
    w_in_v,
    w_out,
    w_out_m,
    w_out_v,
    small_params,
    small_m,
    small_v,
):
    axes = dp + ("ctx",)
    n_dp, n_ctx = lax.axis_size(dp), lax.axis_size("ctx")
    rank = lax.axis_index("ctx")
    heads = HEADS // n_ctx
    inner = heads * HD
    conv = inner + 2 * NS
    count = block_in.shape[0]

    moves = []
    for block in range(n_dp * n_ctx):
        moves.append((block, (block % n_dp) * n_ctx + block // n_dp))
    mine_out = lax.ppermute(w_out.astype(BF16), axes, moves)
    tokens = lax.all_gather(block_in, "ctx", axis=1, tiled=True)
    upstream = lax.all_gather(out_grad, "ctx", axis=1, tiled=True)
    w_in_low = w_in.astype(BF16)
    slices = []
    for r in range(n_ctx):
        first = DI + CHANNELS + r * heads
        slices.append(
            jnp.concatenate(
                [
                    w_in_low[:, DI + r * inner : DI + (r + 1) * inner],
                    w_in_low[:, 2 * DI : 2 * DI + 2 * NS],
                    pad_lanes(w_in_low[:, first : first + heads], LANES),
                    w_in_low[:, r * inner : (r + 1) * inner],
                ],
                axis=1,
            )
        )
    rest = conv + LANES
    mine_in = to_all(jnp.concatenate(slices, axis=0), "ctx")
    mine_rest = mine_in[:, :rest]
    if len(dp) > 1:
        columns = [mine_out[:, k * inner : (k + 1) * inner] for k in range(D // inner)]
        mine_both = jnp.concatenate([mine_in[:, rest:]] + columns, axis=0)
        other_rest = swapped(mine_rest, dp[0])
        other_both = swapped(mine_both, dp[0])
        weight_halves = [to_every(mine_rest, dp[1:]), to_every(other_rest, dp[1:])]
        both = jnp.concatenate([mine_both, other_both], axis=0)
        both, *weight_halves = lax.optimization_barrier((both, *weight_halves))
        weights = [to_every(both, dp[1:])]
    else:
        weight_halves = [lax.all_gather(mine_rest, dp, axis=0, tiled=True)]
        weights = [
            lax.all_gather(value, dp, axis=0, tiled=True)
            for value in (mine_out, mine_in[:, rest:])
        ]

    offset = 0
    pieces = []
    for amount in (D, DI, KCONV * CHANNELS, CHANNELS, HEADS, HEADS, HEADS):
        pieces.append(small_params[offset : offset + amount])
        offset = offset + amount
    norm_gain = pieces[0].reshape(1, D)
    gate_gain = lax.dynamic_slice(pieces[1], (rank * inner,), (inner,)).reshape(1, inner)
    taps_all = jnp.concatenate([pieces[2].reshape(KCONV, CHANNELS), pieces[3][None]], axis=0)
    taps = jnp.concatenate(
        [lax.dynamic_slice(taps_all, (0, rank * inner), (KCONV + 1, inner)), taps_all[:, DI:]],
        axis=1,
    )
    taps = jnp.pad(taps, ((0, RIM - KCONV - 1), (0, 0)))
    dt_bias = lax.dynamic_slice(pieces[4], (rank * heads,), (heads,))
    decay = -jnp.exp(lax.dynamic_slice(pieces[5], (rank * heads,), (heads,)))
    head_rows = jnp.pad(jnp.stack([dt_bias, decay]), ((0, 6), (0, LANES - heads)))
    skip = jnp.repeat(lax.dynamic_slice(pieces[6], (rank * heads,), (heads,)), HD).reshape(1, inner)

    split = n_ctx == 4 and block_in.shape[1] == ROWS
    order = jnp.arange(n_ctx * block_in.shape[1] // ROWS, dtype=jnp.int32)
    if split:
        order = rank.astype(jnp.int32) ^ jnp.array([0, 2, 1, 3], jnp.int32)
    high = lax.axis_index(dp[0]) if len(dp) > 1 else rank * 0
    high = high.astype(jnp.int32).reshape(1)
    low, rest, mixed, incoming, weight_rest = run_forward(
        high, tokens, norm_gain, weight_halves, taps, head_rows, skip
    )
    weight_out, weight_gate, gate, d_out, stats = run_stats(
        high, upstream, low, mixed, gate_gain, weights
    )
    stats = lax.all_gather(stats, "ctx")
    *branch, grad_out, d_mixed, d_gate, d_gate_gain = run_gate_back(
        split, order, upstream, weight_out, gate, mixed, gate_gain, d_out, stats
    )
    grad_out = to_all(grad_out, dp)
    branch, branch_sent = chip_sums(branch)

    own_rows = w_in.shape[0]

    def summed(got):
        return jnp.sum(got.astype(F32).reshape(-1, n_ctx, own_rows, got.shape[1]), axis=0)

    grad_gate = dot(low.reshape(-1, D), d_gate.reshape(-1, inner), COL_COL).astype(BF16)
    after = grad_gate if branch_sent is None else branch_sent
    branch = across_sums(branch, branch_sent)
    d_rest = after
    smalls = []
    normeds = []
    for s in range(count):
        d_rest, *small = run_mixer_back(
            s, rest, mixed, d_mixed, incoming, taps, head_rows, skip, after, d_rest
        )
        after = grad_out
        if s == 0:
            grad_gate = to_all(grad_gate, axes)
        if s == count - 1:
            grad_rest = dot(
                low.reshape(-1, D), d_rest.reshape(-1, d_rest.shape[2]), COL_COL
            ).astype(BF16)
            after = grad_gate[:16, :LANES] + grad_rest[:16, :LANES]
            grad_rest = to_all(grad_rest, axes)
        *d_normed, d_gain = run_norm_back(
            split, s, order, d_gate, d_rest, weight_gate, weight_rest, tokens, after
        )
        smalls.append([d_gain] + small)
        d_normed, normed_sent = chip_sums(d_normed)
        after = d_normed if normed_sent is None else normed_sent
        normeds.append(across_sums(d_normed, normed_sent))
    d_normed = jnp.concatenate(normeds, axis=0)
    d_norm_gain, d_taps, d_heads, d_skip = (sum(parts) for parts in zip(*smalls))
    grad_out = jnp.sum(grad_out.astype(F32).reshape(n_dp, -1, D), axis=0)
    grad_out = lax.ppermute(grad_out, axes, [(b, a) for a, b in moves])
    grad_gate = summed(grad_gate)
    grad_rest = summed(grad_rest)
    columns = [grad_gate[r] for r in range(n_ctx)]
    columns += [grad_rest[r, :, :inner] for r in range(n_ctx)]
    columns += [jnp.sum(grad_rest[:, :, inner:conv], axis=0)]
    columns += [grad_rest[r, :, conv : conv + heads] for r in range(n_ctx)]
    grad_in = jnp.concatenate(columns, axis=1)

    parts = (
        d_norm_gain.reshape(-1),
        d_gate_gain.reshape(-1),
        d_taps[: KCONV + 1].reshape(-1),
        d_heads[0, :heads],
        d_heads[1, :heads],
        jnp.sum(d_skip.reshape(heads, HD), axis=1),
    )
    mine = jnp.concatenate(parts)
    mine = jnp.pad(mine, (0, -mine.shape[0] % (8 * LANES))).reshape(-1, LANES)
    every = lax.all_gather(sum_over(mine, dp), "ctx", axis=0).reshape(n_ctx, -1)
    offset = 0
    found = []
    for part in parts:
        found.append(every[:, offset : offset + part.shape[0]])
        offset = offset + part.shape[0]
    taps_found = found[2].reshape(n_ctx, KCONV + 1, conv)
    taps_found = jnp.concatenate(
        [
            jnp.swapaxes(taps_found[:, :, :inner], 0, 1).reshape(KCONV + 1, DI),
            jnp.sum(taps_found[:, :, inner:], axis=0),
        ],
        axis=1,
    )
    grad_small = jnp.concatenate(
        [jnp.sum(found[0], axis=0), found[1].reshape(-1), taps_found.reshape(-1)]
        + [found[k].reshape(-1) for k in (3, 4, 5)]
    )

    own = block_in.astype(F32)
    block_out = (own + branch.astype(F32)).astype(BF16)
    scale = lax.rsqrt(jnp.mean(own * own, axis=-1, keepdims=True) + NORM_EPS)
    d_scaled = d_normed * norm_gain
    d_own = scale * (
        d_scaled - own * scale * scale * jnp.mean(d_scaled * own, axis=-1, keepdims=True)
    )
    input_grad = (out_grad.astype(F32) + d_own).astype(BF16)
    in_second, in_new = adam_step(w_in, w_in_m, w_in_v, grad_in, RATE_BIG)
    out_second, out_new = adam_step(w_out, w_out_m, w_out_v, grad_out, RATE_BIG)
    small_second, small_updated = adam_step(small_params, small_m, small_v, grad_small, RATE_SMALL)
    return (
        block_out,
        input_grad,
        grad_in,
        in_second,
        in_new,
        grad_out,
        out_second,
        out_new,
        grad_small,
        small_second,
        small_updated,
    )


def solution(mesh):
    dp = ("dp",)
    if mesh.shape["dp"] == 8 and mesh.shape["ctx"] == 4:
        dp = ("high", "low", "side")
        mesh = Mesh(np.asarray(mesh.devices).reshape(2, 2, 2, 4), dp + ("ctx",))
    rows = P(dp + ("ctx",), None)
    spread = P(dp, "ctx", None)
    return jax.shard_map(
        functools.partial(shards, dp),
        mesh=mesh,
        in_specs=(spread, spread) + (rows,) * 6 + (P(),) * 3,
        out_specs=(spread, spread) + (rows,) * 6 + (P(),) * 3,
        check_vma=False,
    )
```

```python
import functools

import jax
import jax.numpy as jnp
import numpy as np
from jax import lax
from jax.experimental import pallas as pl
from jax.experimental.pallas import tpu as pltpu
from jax.sharding import Mesh
from jax.sharding import PartitionSpec as P

D = 1024
HEADS = 32
HD = 64
NS = 128
KCONV = 4
STEP = 10
DI = 2048
CHANNELS = DI + 2 * NS

CHUNK = 128
LANES = 128
RIM = 8
ROWS = 256

NORM_EPS = 1e-05
ADAM_EPS = 1e-08
BETA_ONE = 0.9
BETA_TWO = 0.999
RATE_BIG = 0.03
RATE_SMALL = 0.3
DECAY_WEIGHT = 0.01

F32 = jnp.float32
BF16 = jnp.bfloat16
VMEM_BYTES = 48 * 1024 * 1024


def dot(a, b, contract=((1,), (0,))):
    return lax.dot_general(a, b, (contract, ((), ())), preferred_element_type=F32)


def terms(a, count):
    parts = []
    for _ in range(count):
        part = a.astype(BF16)
        parts.append(part)
        a = a - part.astype(F32)
    return parts


def spread_dot(a, spread):
    return dot(
        jnp.concatenate(terms(a, 2), axis=1), jnp.concatenate([spread, spread], axis=0)
    )


def sum_dot(ones, a, count):
    return sum(dot(ones, part) for part in terms(a, count))


ROW_ROW = ((1,), (1,))
COL_COL = ((0,), (0,))


def sigmoid(v):
    return 1.0 / (1.0 + jnp.exp(-v))


def softplus(v):
    return jnp.maximum(v, 0.0) + jnp.log1p(jnp.exp(-jnp.abs(v)))


def expander(inner):
    head = lax.broadcasted_iota(jnp.int32, (LANES, inner), 0)
    column = lax.broadcasted_iota(jnp.int32, (LANES, inner), 1)
    inside = (column >= head * HD) & (column < (head + 1) * HD)
    return jnp.where(inside, 1.0, 0.0).astype(BF16)


def lower_ones():
    row = lax.broadcasted_iota(jnp.int32, (CHUNK, CHUNK), 0)
    column = lax.broadcasted_iota(jnp.int32, (CHUNK, CHUNK), 1)
    return jnp.where(row >= column, 1.0, 0.0)


def row_sums(a):
    lanes = a[:, :LANES]
    for start in range(LANES, a.shape[1], LANES):
        lanes = lanes + a[:, start : start + LANES]
    return jnp.sum(lanes.T, axis=0, keepdims=True)


def side_by_side(pair):
    lane = lax.broadcasted_iota(jnp.int32, pair.shape, 1)
    zero = jnp.zeros_like(pair)
    return jnp.concatenate(
        [jnp.where(lane < HD, pair, zero), jnp.where(lane < HD, zero, pair)], axis=0
    )


def decay_terms(step, rate, spread, tri):
    cum = sum_dot(tri.astype(BF16), rate, 3)
    total = cum[CHUNK - 1 : CHUNK, :]
    wide = spread_dot(
        jnp.concatenate([step, jnp.exp(cum), jnp.exp(total - cum)], axis=0), spread
    )
    return cum, cum.T, wide[:CHUNK], wide[CHUNK : 2 * CHUNK], wide[2 * CHUNK :]


def pair_mixing(cum, cum_t, scores, pair):
    decays = []
    for head in (2 * pair, 2 * pair + 1):
        differ = cum[:, head : head + 1] - cum_t[head : head + 1, :]
        decays.append(jnp.exp(jnp.minimum(differ, 0.0)))
    return decays, [(decay * scores).astype(BF16) for decay in decays]


def conv_forward(padded_ref, taps, rows):
    total = taps[KCONV : KCONV + 1, :]
    for k in range(KCONV):
        start = RIM - (KCONV - 1) + k
        total = total + taps[k : k + 1, :] * padded_ref[start : start + rows, :]
    return total


def forward_kernel(
    inner,
    order_ref,
    tokens_ref,
    gain_ref,
    taps_ref,
    heads_ref,
    skip_ref,
    mine_ref,
    other_ref,
    low_ref,
    rest_ref,
    mixed_ref,
    incoming_ref,
    weight_ref,
    padded,
    state,
):
    rows = tokens_ref.shape[1]
    conv = inner + 2 * NS

    @pl.when((pl.program_id(0) == 0) & (pl.program_id(1) == 0))
    def _():
        if mine_ref.shape[0] == D:
            weight_ref[...] = mine_ref[...]
        else:
            mine = pl.multiple_of(order_ref[0] * (D // 2), D // 2)
            other = pl.multiple_of((1 - order_ref[0]) * (D // 2), D // 2)
            weight_ref[pl.ds(mine, D // 2), :] = mine_ref[...]
            weight_ref[pl.ds(other, D // 2), :] = other_ref[...]

    @pl.when(pl.program_id(1) == 0)
    def _():
        padded[0:RIM, :] = jnp.zeros((RIM, conv), F32)
        state[...] = jnp.zeros_like(state)

    @pl.when(pl.program_id(1) > 0)
    def _():
        padded[0:RIM, :] = padded[rows : rows + RIM, :]

    tokens_low = tokens_ref[0]
    tokens = tokens_low.astype(F32)
    scale = lax.rsqrt(jnp.mean(tokens * tokens, axis=1, keepdims=True) + NORM_EPS)
    low = (tokens * scale * gain_ref[...]).astype(BF16)
    low_ref[0] = low
    projected = dot(low, weight_ref[...])
    rest_ref[0] = projected
    padded[RIM : RIM + rows, :] = projected[:, :conv]
    conv_out = conv_forward(padded, taps_ref[...], rows)
    active = conv_out * sigmoid(conv_out)
    heads = heads_ref[...]
    step_all = softplus(projected[:, conv:] + heads[0:1, :])
    rate_all = heads[1:2, :] * step_all
    skip = skip_ref[...]
    spread = expander(inner)
    tri = lower_ones()
    for c in range(rows // CHUNK):
        part = slice(c * CHUNK, (c + 1) * CHUNK)
        values = active[part, :inner]
        in_b = active[part, inner : inner + NS].astype(BF16)
        out_c = active[part, inner + NS :].astype(BF16)
        cum, cum_t, step_x, grown, remain = decay_terms(
            step_all[part], rate_all[part], spread, tri
        )
        stepped = values * step_x
        stepped_low = stepped.astype(BF16)
        scores = dot(out_c, in_b, ROW_ROW) * tri
        inside = []
        for pair in range(inner // LANES):
            lanes = slice(pair * LANES, (pair + 1) * LANES)
            _, mixing = pair_mixing(cum, cum_t, scores, pair)
            inside.append(
                dot(jnp.concatenate(mixing, axis=1), side_by_side(stepped_low[:, lanes]))
            )
        before = state[...]
        before_low = before.astype(BF16)
        incoming_ref[0, c] = before_low
        outer = grown * dot(out_c, before_low)
        mixed_ref[0, part, :] = jnp.concatenate(inside, axis=1) + outer + skip * values
        state[...] = grown[CHUNK - 1 : CHUNK, :] * before + dot(
            in_b, (remain * stepped).astype(BF16), COL_COL
        )


def stats_kernel(joined, order_ref, up_ref, low_ref, mixed_ref, gain_ref, *refs):
    if joined:
        both_ref, weight_out_ref, weight_gate_ref, gate_ref, d_out_ref, stats_ref = refs
        inner = gate_ref.shape[2]

        @pl.when((pl.program_id(0) == 0) & (pl.program_id(1) == 0))
        def _():
            deep, tall = D // 8, inner // 8
            place = 0
            for quarter in range(4):
                for half in (order_ref[0], 1 - order_ref[0]):
                    block = half * 4 + quarter
                    rows = pl.ds(pl.multiple_of(block * deep, deep), deep)
                    weight_gate_ref[rows, :] = both_ref[place : place + deep, :]
                    place = place + deep
                    rows = pl.ds(pl.multiple_of(block * tall, tall), tall)
                    for k in range(D // inner):
                        columns = slice(k * inner, (k + 1) * inner)
                        weight_out_ref[rows, columns] = both_ref[place : place + tall, :]
                        place = place + tall

    else:
        weight_out_ref, weight_gate_ref, gate_ref, d_out_ref, stats_ref = refs
    d_out = dot(up_ref[0], weight_out_ref[...], ROW_ROW)
    d_out_ref[0] = d_out.astype(BF16)
    gate = dot(low_ref[0], weight_gate_ref[...])
    gate_ref[0] = gate
    gated = mixed_ref[0] * gate * sigmoid(gate)
    stats_ref[0, 0:1, :] = row_sums(gated * gated)
    stats_ref[0, 1:2, :] = row_sums(d_out * gain_ref[...] * gated)


def row_to_lanes(row):
    return jnp.broadcast_to(row, (LANES, row.shape[1])).T[:, 0:1]


def keep_or_send(refs, step, value):
    if len(refs) == 1:
        refs[0][0] = value
        return

    @pl.when(step < 2)
    def _():
        refs[0][0] = value

    @pl.when(step >= 2)
    def _():
        refs[1][0] = value


def gate_back_kernel(
    order_ref,
    up_ref,
    weight_ref,
    gate_ref,
    mixed_ref,
    gain_ref,
    d_out_ref,
    stats_ref,
    low_ref,
    *refs,
):
    *branch_refs, grad_ref, grad_gate_ref, d_mixed_ref, d_gate_ref, d_gain_ref = refs[:-2]
    total, total_gate = refs[-2:]
    first = (pl.program_id(0) == 0) & (pl.program_id(1) == 0)
    last_one = pl.program_id(0) == pl.num_programs(0) - 1
    last_two = pl.program_id(1) == pl.num_programs(1) - 1

    @pl.when(first)
    def _():
        total[...] = jnp.zeros_like(total)
        total_gate[...] = jnp.zeros_like(total_gate)
        d_gain_ref[...] = jnp.zeros_like(d_gain_ref)

    stats = stats_ref[0, 0]
    for k in range(1, stats_ref.shape[0]):
        stats = stats + stats_ref[k, 0]
    squares = row_to_lanes(stats[0:1])
    products = row_to_lanes(stats[1:2])
    scale = lax.rsqrt(squares * (1.0 / DI) + NORM_EPS)
    gate = gate_ref[0]
    mixed = mixed_ref[0]
    gain = gain_ref[...]
    d_out = d_out_ref[0].astype(F32)
    sig = sigmoid(gate)
    silu = gate * sig
    gated = mixed * silu
    unit = gated * scale
    low = (unit * gain).astype(BF16)
    keep_or_send(branch_refs, pl.program_id(1), dot(low, weight_ref[...]).astype(BF16))
    total[...] += dot(low, up_ref[0], COL_COL)
    d_gain_ref[...] += jnp.sum(d_out * unit, axis=0, keepdims=True)
    d_gated = scale * (gain * d_out - unit * (scale * products * (1.0 / DI)))
    d_mixed_ref[0] = (d_gated * silu).astype(BF16)
    d_gate = (d_gated * mixed * (sig + silu * (1.0 - sig))).astype(BF16)
    d_gate_ref[0] = d_gate
    total_gate[...] += dot(low_ref[0], d_gate, COL_COL)

    @pl.when(last_one & last_two)
    def _():
        grad_ref[...] = total[...].astype(BF16)
        grad_gate_ref[...] = total_gate[...].astype(BF16)


def mixer_back_kernel(
    inner,
    first,
    rest_ref,
    rim_ref,
    mixed_ref,
    d_mixed_ref,
    incoming_ref,
    taps_ref,
    heads_ref,
    skip_ref,
    low_ref,
    after_ref,
    before_ref,
    part_ref,
    d_rest_ref,
    grad_ref,
    d_taps_ref,
    d_heads_ref,
    d_skip_ref,
    padded,
    later,
    carried,
    d_active,
    total,
):
    rows = rest_ref.shape[1]
    conv = inner + 2 * NS
    block = pl.num_programs(0) - 1 - pl.program_id(0)

    @pl.when(pl.program_id(0) == 0)
    def _():
        d_taps_ref[...] = jnp.zeros_like(d_taps_ref)
        d_heads_ref[...] = jnp.zeros_like(d_heads_ref)
        d_skip_ref[...] = jnp.zeros_like(d_skip_ref)
        if first:
            total[...] = jnp.zeros_like(total)
        else:
            pltpu.sync_copy(part_ref, total)
        carried[...] = jnp.zeros_like(carried)
        later[rows : rows + RIM, :] = jnp.zeros((RIM, conv), F32)

    @pl.when(pl.program_id(0) > 0)
    def _():
        later[rows : rows + RIM, :] = later[0:RIM, :]

    rim = rim_ref[0][:, :conv]
    padded[0:RIM, :] = jnp.where(block > 0, rim, jnp.zeros_like(rim))
    padded[RIM : RIM + rows, :] = rest_ref[0][:, :conv]
    taps = taps_ref[...]
    conv_out = conv_forward(padded, taps, rows)
    sig = sigmoid(conv_out)
    active = conv_out * sig
    slope = sig + active * (1.0 - sig)
    heads = heads_ref[...]
    raw = rest_ref[0][:, conv:] + heads[0:1, :]
    step_all = softplus(raw)
    rate_all = heads[1:2, :] * step_all
    skip = skip_ref[...]
    spread = expander(inner)
    tri = lower_ones()
    upper = tri.T.astype(BF16)
    for c in reversed(range(rows // CHUNK)):
        part = slice(c * CHUNK, (c + 1) * CHUNK)
        values = active[part, :inner]
        in_b = active[part, inner : inner + NS].astype(BF16)
        out_c = active[part, inner + NS :].astype(BF16)
        step = step_all[part]
        rate = rate_all[part]
        cum, cum_t, step_x, grown, remain = decay_terms(step, rate, spread, tri)
        stepped = values * step_x
        stepped_low = stepped.astype(BF16)
        scores = dot(out_c, in_b, ROW_ROW) * tri
        d_low = d_mixed_ref[0, part, :]
        d_mixed = d_low.astype(F32)
        d_scores = jnp.zeros((CHUNK, CHUNK), F32)
        inside = []
        for pair in range(inner // LANES):
            lanes = slice(pair * LANES, (pair + 1) * LANES)
            decays, mixing = pair_mixing(cum, cum_t, scores, pair)
            d_two = side_by_side(d_low[:, lanes])
            d_mixing = dot(d_two, stepped_low[:, lanes], ROW_ROW)
            d_scores += decays[0] * d_mixing[:CHUNK] + decays[1] * d_mixing[CHUNK:]
            inside.append(dot(jnp.concatenate(mixing, axis=0), d_two, COL_COL))
        before = incoming_ref[0, c]
        ahead = carried[...]
        ahead_low = ahead.astype(BF16)
        through = remain * dot(in_b, ahead_low)
        outer = (grown * d_mixed).astype(BF16)
        d_scores_low = (d_scores * tri).astype(BF16)
        d_in_b = dot((remain * stepped).astype(BF16), ahead_low, ROW_ROW) + dot(
            d_scores_low, out_c, COL_COL
        )
        d_out_c = dot(outer, before, ROW_ROW) + dot(d_scores_low, in_b)
        d_stepped = jnp.concatenate(inside, axis=1) + through
        stepped_near = stepped_low.astype(F32)
        both = d_mixed * (mixed_ref[0, part, :] - skip * values)
        d_cum_x = both - stepped_near * d_stepped
        d_step_x = d_stepped * values
        grown_total = grown[CHUNK - 1 : CHUNK, :]
        d_total_x = jnp.sum(stepped_near * through, axis=0, keepdims=True) + grown_total * jnp.sum(
            ahead * before.astype(F32), axis=0, keepdims=True
        )
        gathered = jnp.concatenate(
            [d_cum_x, d_step_x, jnp.broadcast_to(d_total_x, (16, inner))], axis=0
        )
        narrow = sum(dot(part, spread, ROW_ROW) for part in terms(gathered, 2))
        d_rate = sum_dot(upper, narrow[:CHUNK], 2) + narrow[2 * CHUNK : 2 * CHUNK + 1]
        d_raw = (narrow[CHUNK : 2 * CHUNK] + heads[1:2, :] * d_rate) * sigmoid(raw[part])
        d_heads_ref[0:1, :] += jnp.sum(d_raw, axis=0, keepdims=True)
        d_heads_ref[1:2, :] += jnp.sum(d_rate * rate, axis=0, keepdims=True)
        d_skip_ref[...] += jnp.sum(d_mixed * values, axis=0, keepdims=True)
        d_rest_ref[0, part, conv:] = d_raw.astype(BF16)
        d_active[part, :inner] = d_stepped * step_x + skip * d_mixed
        d_active[part, inner : inner + NS] = d_in_b
        d_active[part, inner + NS :] = d_out_c
        carried[...] = grown_total * ahead + dot(out_c, outer, COL_COL)
    d_conv_out = d_active[...] * slope
    later[0:rows, :] = d_conv_out
    d_conv_in = jnp.zeros((rows, conv), F32)
    for k in range(KCONV):
        ahead_rows = KCONV - 1 - k
        start = RIM - (KCONV - 1) + k
        d_conv_in += taps[k : k + 1, :] * later[ahead_rows : ahead_rows + rows, :]
        d_taps_ref[k : k + 1, :] += jnp.sum(
            d_conv_out * padded[start : start + rows, :], axis=0, keepdims=True
        )
    d_taps_ref[KCONV : KCONV + 1, :] += jnp.sum(d_conv_out, axis=0, keepdims=True)
    d_rest_ref[0, :, :conv] = d_conv_in.astype(BF16)
    total[...] += dot(low_ref[0], d_rest_ref[0], COL_COL)

    @pl.when(block == 0)
    def _():
        grad_ref[...] = total[...].astype(grad_ref.dtype)


def norm_back_kernel(
    order_ref, d_gate_ref, d_rest_ref, weight_gate_ref, weight_rest_ref, tokens_ref, after_ref, *refs
):
    *d_normed_refs, d_gain_ref = refs

    @pl.when(pl.program_id(0) == 0)
    def _():
        d_gain_ref[...] = jnp.zeros_like(d_gain_ref)

    d_normed = dot(d_gate_ref[0], weight_gate_ref[...], ROW_ROW) + dot(
        d_rest_ref[0], weight_rest_ref[...], ROW_ROW
    )
    tokens = tokens_ref[0].astype(F32)
    scale = lax.rsqrt(jnp.mean(tokens * tokens, axis=1, keepdims=True) + NORM_EPS)
    d_gain_ref[...] += jnp.sum(d_normed * (tokens * scale), axis=0, keepdims=True)
    keep_or_send(d_normed_refs, pl.program_id(0), d_normed.astype(BF16))


def whole(shape):
    return pl.BlockSpec(shape, lambda *_: (0,) * len(shape))


def by_rows(width):
    return pl.BlockSpec((1, ROWS, width), lambda s, b, *_: (s, b, 0))


def by_order(width):
    return pl.BlockSpec((1, ROWS, width), lambda s, b, order: (s, order[b], 0))


def left_alone():
    return pl.BlockSpec(memory_space=pl.ANY)


def cost(micros):
    return pl.CostEstimate(
        flops=int(micros * 1.1e9), bytes_accessed=int(micros * 2e6), transcendentals=0
    )


def params():
    return pltpu.CompilerParams(
        vmem_limit_bytes=VMEM_BYTES
    )


def shaped(shape, dtype=F32):
    return jax.ShapeDtypeStruct(shape, dtype)


def run_forward(order, tokens, norm_gain, halves, taps, heads, skip):
    count, length, _ = tokens.shape
    inner = skip.shape[1]
    rest = halves[0].shape[1]
    conv = inner + 2 * NS
    chunks = ROWS // CHUNK
    fixed = [norm_gain, taps, heads, skip, halves[0], halves[-1]]
    return pl.pallas_call(
        functools.partial(forward_kernel, inner),
        grid_spec=pltpu.PrefetchScalarGridSpec(
            num_scalar_prefetch=1,
            grid=(count, length // ROWS),
            in_specs=[by_rows(D)] + [whole(value.shape) for value in fixed],
            out_specs=[
                by_rows(D),
                by_rows(rest),
                by_rows(inner),
                pl.BlockSpec((1, chunks, NS, inner), lambda s, b, *_: (s, b, 0, 0)),
                whole((D, rest)),
            ],
            scratch_shapes=[pltpu.VMEM((RIM + ROWS, conv), F32), pltpu.VMEM((NS, inner), F32)],
        ),
        out_shape=[
            shaped((count, length, D), BF16),
            shaped((count, length, rest)),
            shaped((count, length, inner)),
            shaped((count, length // CHUNK, NS, inner), BF16),
            shaped((D, rest), BF16),
        ],
        compiler_params=params(),
        cost_estimate=cost(1),
        name="forward_mixer",
    )(order, tokens, *fixed)


def run_stats(order, upstream, low, mixed, gate_gain, weights):
    count, length, inner = mixed.shape
    joined = len(weights) == 1
    found_specs = [whole((inner, D)), whole((D, inner))] * joined
    found_shapes = [shaped((inner, D), BF16), shaped((D, inner), BF16)] * joined
    found = pl.pallas_call(
        functools.partial(stats_kernel, joined),
        grid_spec=pltpu.PrefetchScalarGridSpec(
            num_scalar_prefetch=1,
            grid=(count, length // ROWS),
            in_specs=[by_rows(D), by_rows(D), by_rows(inner), whole((1, inner))]
            + [whole(weight.shape) for weight in weights],
            out_specs=found_specs
            + [
                by_rows(inner),
                by_rows(inner),
                pl.BlockSpec((1, 2, ROWS), lambda s, b, *_: (s, 0, b)),
            ],
        ),
        out_shape=found_shapes
        + [
            shaped((count, length, inner)),
            shaped((count, length, inner), BF16),
            shaped((count, 2, length)),
        ],
        compiler_params=params(),
        cost_estimate=cost(1),
        name="gate_stats",
    )(order, upstream, low, mixed, gate_gain, *weights)
    return found if joined else [*weights, *found]


def kept_and_sent(split, count, length, place):
    if not split:
        return [place(lambda order, b: order[b])], [shaped((count, length, D), BF16)]
    specs = [
        place(lambda order, b: jnp.minimum(b, 1)),
        place(lambda order, b: jnp.maximum(b - 2, 0)),
    ]
    return specs, [shaped((count, 2 * ROWS, D), BF16)] * 2


def run_gate_back(split, order, upstream, weight, gate, mixed, gate_gain, d_out, stats, low):
    count, length, inner = gate.shape

    def place(group):
        return pl.BlockSpec((1, ROWS, D), lambda s, b, order: (s, group(order, b), 0))

    branch_specs, branch_shapes = kept_and_sent(split, count, length, place)
    return pl.pallas_call(
        gate_back_kernel,
        grid_spec=pltpu.PrefetchScalarGridSpec(
            num_scalar_prefetch=1,
            grid=(count, length // ROWS),
            in_specs=[
                by_order(D),
                whole((inner, D)),
                by_order(inner),
                by_order(inner),
                whole((1, inner)),
                by_order(inner),
                pl.BlockSpec(
                    (stats.shape[0], 1, 2, ROWS), lambda s, b, order: (0, s, 0, order[b])
                ),
                by_order(D),
            ],
            out_specs=branch_specs
            + [
                whole((inner, D)),
                whole((D, inner)),
                by_order(inner),
                by_order(inner),
                whole((1, inner)),
            ],
            scratch_shapes=[pltpu.VMEM((inner, D), F32), pltpu.VMEM((D, inner), F32)],
        ),
        out_shape=branch_shapes
        + [
            shaped((inner, D), BF16),
            shaped((D, inner), BF16),
            shaped((count, length, inner), BF16),
            shaped((count, length, inner), BF16),
            shaped((1, inner)),
        ],
        compiler_params=params(),
        cost_estimate=cost(1),
        name="gate_back",
    )(order, upstream, weight, gate, mixed, gate_gain, d_out, stats, low)


def run_mixer_back(s, rest, mixed, d_mixed, incoming, taps, heads, skip, low, after, before, part):
    count, length, inner = mixed.shape
    conv = inner + 2 * NS
    last = length // ROWS - 1
    chunks = ROWS // CHUNK
    width = rest.shape[2]

    def rows(width):
        return pl.BlockSpec((1, ROWS, width), lambda b: (s, last - b, 0))

    return pl.pallas_call(
        functools.partial(mixer_back_kernel, inner, s == 0),
        grid=(length // ROWS,),
        in_specs=[
            rows(width),
            pl.BlockSpec(
                (1, RIM, width),
                lambda b: (s, jnp.maximum((last - b) * (ROWS // RIM) - 1, 0), 0),
            ),
            rows(inner),
            rows(inner),
            pl.BlockSpec((1, chunks, NS, inner), lambda b: (s, last - b, 0, 0)),
            whole((RIM, conv)),
            whole((8, LANES)),
            whole((1, inner)),
            rows(D),
            left_alone(),
            left_alone(),
            left_alone(),
        ],
        out_specs=[
            rows(width),
            whole((D, width)),
            whole((RIM, conv)),
            whole((8, LANES)),
            whole((1, inner)),
        ],
        scratch_shapes=[
            pltpu.VMEM((RIM + ROWS, conv), F32),
            pltpu.VMEM((RIM + ROWS, conv), F32),
            pltpu.VMEM((NS, inner), F32),
            pltpu.VMEM((ROWS, conv), F32),
            pltpu.VMEM((D, width), F32),
        ],
        out_shape=[
            shaped((count, length, width), BF16),
            shaped((D, width), BF16 if s == count - 1 else F32),
            shaped((RIM, conv)),
            shaped((8, LANES)),
            shaped((1, inner)),
        ],
        input_output_aliases={10: 0} if s > 0 else {},
        compiler_params=params(),
        cost_estimate=cost(1),
        name="mixer_back",
    )(rest, rest, mixed, d_mixed, incoming, taps, heads, skip, low, after, before, part)


def run_norm_back(split, s, order, d_gate, d_rest, weight_gate, weight_rest, tokens, after):
    _, length, inner = d_gate.shape
    width = d_rest.shape[2]

    def rows(width, s):
        return pl.BlockSpec((1, ROWS, width), lambda b, order: (s, order[b], 0))

    def place(group):
        return pl.BlockSpec((1, ROWS, D), lambda b, order: (0, group(order, b), 0))

    specs, shapes = kept_and_sent(split, 1, length, place)
    return pl.pallas_call(
        norm_back_kernel,
        grid_spec=pltpu.PrefetchScalarGridSpec(
            num_scalar_prefetch=1,
            grid=(length // ROWS,),
            in_specs=[
                rows(inner, s),
                rows(width, s),
                whole(weight_gate.shape),
                whole(weight_rest.shape),
                rows(D, s),
                left_alone(),
            ],
            out_specs=specs + [whole((1, D))],
        ),
        out_shape=shapes + [shaped((1, D))],
        compiler_params=params(),
        cost_estimate=cost(1),
        name="norm_back",
    )(order, d_gate, d_rest, weight_gate, weight_rest, tokens, after)


def swapped(value, axis, mask=1):
    count = lax.axis_size(axis)
    return lax.ppermute(value, axis, [(a, a ^ mask) for a in range(count)])


def chip_sums(parts):
    if len(parts) == 1:
        total = lax.psum_scatter(parts[0], "ctx", scatter_dimension=1, tiled=True)
        return total.astype(F32), None
    kept, sent = parts
    got = swapped(sent, "ctx", 1)
    own = kept[:, :ROWS].astype(F32) + got[:, :ROWS].astype(F32)
    return own, (kept[:, ROWS:].astype(F32) + got[:, ROWS:].astype(F32)).astype(BF16)


def across_sums(own, sent):
    if sent is None:
        return own
    return own + swapped(sent, "ctx", 2).astype(F32)


def sum_over(value, axes):
    if len(axes) == 1:
        return lax.psum(value, axes)
    for axis in axes:
        value = value + swapped(value, axis)
    return value


def by_rank(value):
    if lax.axis_size("ctx") != 4:
        return lax.all_gather(value, "ctx", axis=0)
    rank = lax.axis_index("ctx")
    near, across = swapped(value, "ctx", 1), swapped(value, "ctx", 2)
    found = [value, near, across, swapped(across, "ctx", 1)]
    odd, high = (rank & 1) == 1, rank >= 2
    found = [jnp.where(odd, found[k ^ 1], found[k]) for k in range(4)]
    return jnp.stack([jnp.where(high, found[k ^ 2], found[k]) for k in range(4)])


def to_all(value, axes):
    return lax.all_to_all(value, axes, split_axis=0, concat_axis=0, tiled=True)


def to_every(value, axes):
    times = 1
    for axis in axes:
        times = times * lax.axis_size(axis)
    return to_all(jnp.broadcast_to(value[None], (times,) + value.shape).reshape(-1, value.shape[1]), axes)


def adam_step(weight, first_old, second_old, gradient, step_rate):
    first_new = BETA_ONE * first_old + (1.0 - BETA_ONE) * gradient
    second_new = BETA_TWO * second_old + (1.0 - BETA_TWO) * gradient * gradient
    first_hat = first_new / (1.0 - BETA_ONE**STEP)
    second_hat = second_new / (1.0 - BETA_TWO**STEP)
    weight_new = weight - step_rate * (
        first_hat / (jnp.sqrt(second_hat) + ADAM_EPS) + DECAY_WEIGHT * weight
    )
    return (second_new, weight_new)


def pad_lanes(value, width):
    return jnp.pad(value, [(0, 0)] * (value.ndim - 1) + [(0, width - value.shape[-1])])


def shards(
    dp,
    block_in,
    out_grad,
    w_in,
    w_in_m,
    w_in_v,
    w_out,
    w_out_m,
    w_out_v,
    small_params,
    small_m,
    small_v,
):
    axes = dp + ("ctx",)
    n_dp, n_ctx = lax.axis_size(dp), lax.axis_size("ctx")
    rank = lax.axis_index("ctx")
    heads = HEADS // n_ctx
    inner = heads * HD
    conv = inner + 2 * NS
    count = block_in.shape[0]

    moves = []
    for block in range(n_dp * n_ctx):
        moves.append((block, (block % n_dp) * n_ctx + block // n_dp))
    mine_out = lax.ppermute(w_out.astype(BF16), axes, moves)
    tokens = lax.all_gather(block_in, "ctx", axis=1, tiled=True)
    upstream = lax.all_gather(out_grad, "ctx", axis=1, tiled=True)
    w_in_low = w_in.astype(BF16)
    slices = []
    for r in range(n_ctx):
        first = DI + CHANNELS + r * heads
        slices.append(
            jnp.concatenate(
                [
                    w_in_low[:, DI + r * inner : DI + (r + 1) * inner],
                    w_in_low[:, 2 * DI : 2 * DI + 2 * NS],
                    pad_lanes(w_in_low[:, first : first + heads], LANES),
                    w_in_low[:, r * inner : (r + 1) * inner],
                ],
                axis=1,
            )
        )
    rest = conv + LANES
    sent = jnp.concatenate(slices, axis=0)
    mine_in = to_all(sent, "ctx")
    mine_rest = mine_in[:, :rest]
    if len(dp) > 1:
        columns = [mine_out[:, k * inner : (k + 1) * inner] for k in range(D // inner)]
        mine_both = jnp.concatenate([mine_in[:, rest:]] + columns, axis=0)
        other_rest = swapped(mine_rest, dp[0])
        other_both = swapped(mine_both, dp[0])
        mine_rest, mine_out = lax.optimization_barrier((mine_rest, mine_out))
        other_rest, other_both = lax.optimization_barrier((other_rest, other_both))
        weight_halves = [to_every(mine_rest, dp[1:]), to_every(other_rest, dp[1:])]
        both = jnp.concatenate([mine_both, other_both], axis=0)
        both, *weight_halves = lax.optimization_barrier((both, *weight_halves))
        weights = [to_every(both, dp[1:])]
    else:
        weight_halves = [lax.all_gather(mine_rest, dp, axis=0, tiled=True)]
        weights = [
            lax.all_gather(value, dp, axis=0, tiled=True)
            for value in (mine_out, mine_in[:, rest:])
        ]

    offset = 0
    pieces = []
    for amount in (D, DI, KCONV * CHANNELS, CHANNELS, HEADS, HEADS, HEADS):
        pieces.append(small_params[offset : offset + amount])
        offset = offset + amount
    norm_gain = pieces[0].reshape(1, D)
    gate_gain = lax.dynamic_slice(pieces[1], (rank * inner,), (inner,)).reshape(1, inner)
    taps_all = jnp.concatenate([pieces[2].reshape(KCONV, CHANNELS), pieces[3][None]], axis=0)
    taps = jnp.concatenate(
        [lax.dynamic_slice(taps_all, (0, rank * inner), (KCONV + 1, inner)), taps_all[:, DI:]],
        axis=1,
    )
    taps = jnp.pad(taps, ((0, RIM - KCONV - 1), (0, 0)))
    dt_bias = lax.dynamic_slice(pieces[4], (rank * heads,), (heads,))
    decay = -jnp.exp(lax.dynamic_slice(pieces[5], (rank * heads,), (heads,)))
    head_rows = jnp.pad(jnp.stack([dt_bias, decay]), ((0, 6), (0, LANES - heads)))
    skip = jnp.repeat(lax.dynamic_slice(pieces[6], (rank * heads,), (heads,)), HD).reshape(1, inner)

    split = n_ctx == 4 and block_in.shape[1] == ROWS
    order = jnp.arange(n_ctx * block_in.shape[1] // ROWS, dtype=jnp.int32)
    if split:
        order = rank.astype(jnp.int32) ^ jnp.array([0, 2, 1, 3], jnp.int32)
    high = lax.axis_index(dp[0]) if len(dp) > 1 else rank * 0
    high = high.astype(jnp.int32).reshape(1)
    low, rest, mixed, incoming, weight_rest = run_forward(
        high, tokens, norm_gain, weight_halves, taps, head_rows, skip
    )
    weight_out, weight_gate, gate, d_out, stats = run_stats(
        high, upstream, low, mixed, gate_gain, weights
    )
    stats = lax.all_gather(stats, "ctx")
    *branch, grad_out, grad_gate, d_mixed, d_gate, d_gate_gain = run_gate_back(
        split, order, upstream, weight_out, gate, mixed, gate_gain, d_out, stats, low
    )
    grad_out = to_all(grad_out, dp)
    branch, branch_sent = chip_sums(branch)

    own_rows = w_in.shape[0]

    def summed(got):
        return jnp.sum(got.astype(F32).reshape(-1, n_ctx, own_rows, got.shape[1]), axis=0)

    after = grad_gate if branch_sent is None else branch_sent
    branch = across_sums(branch, branch_sent)
    d_rest = grad_rest = after
    smalls = []
    normeds = []
    for s in range(count):
        d_rest, grad_rest, *small = run_mixer_back(
            s, rest, mixed, d_mixed, incoming, taps, head_rows, skip, low, after, d_rest, grad_rest
        )
        after = grad_out
        if s == 0:
            grad_gate, small[0] = lax.optimization_barrier((grad_gate, small[0]))
            grad_gate = to_all(grad_gate, axes)
        if s == count - 1:
            after = grad_gate
        *d_normed, d_gain = run_norm_back(
            split, s, order, d_gate, d_rest, weight_gate, weight_rest, tokens, after
        )
        smalls.append([d_gain] + small)
        d_normed, normed_sent = chip_sums(d_normed)
        after = d_normed if normed_sent is None else normed_sent
        normeds.append(across_sums(d_normed, normed_sent))
    d_norm_gain, d_taps, d_heads, d_skip = (sum(parts) for parts in zip(*smalls))
    parts = (
        d_norm_gain.reshape(-1),
        d_gate_gain.reshape(-1),
        d_taps[: KCONV + 1].reshape(-1),
        d_heads[0, :heads],
        d_heads[1, :heads],
        jnp.sum(d_skip.reshape(heads, HD), axis=1),
    )
    mine = jnp.concatenate(parts)
    mine = jnp.pad(mine, (0, -mine.shape[0] % (8 * LANES))).reshape(-1, LANES)
    mine = sum_over(mine, dp)
    grad_rest = to_all(grad_rest, axes)
    d_normed = jnp.concatenate(normeds, axis=0)
    grad_out = jnp.sum(grad_out.astype(F32).reshape(n_dp, -1, D), axis=0)
    grad_out = lax.ppermute(grad_out, axes, [(b, a) for a, b in moves])
    grad_gate = summed(grad_gate)
    grad_rest = summed(grad_rest)
    columns = [grad_gate[r] for r in range(n_ctx)]
    columns += [grad_rest[r, :, :inner] for r in range(n_ctx)]
    columns += [jnp.sum(grad_rest[:, :, inner:conv], axis=0)]
    columns += [grad_rest[r, :, conv : conv + heads] for r in range(n_ctx)]
    grad_in = jnp.concatenate(columns, axis=1)

    every = by_rank(mine).reshape(n_ctx, -1)
    offset = 0
    found = []
    for part in parts:
        found.append(every[:, offset : offset + part.shape[0]])
        offset = offset + part.shape[0]
    taps_found = found[2].reshape(n_ctx, KCONV + 1, conv)
    taps_found = jnp.concatenate(
        [
            jnp.swapaxes(taps_found[:, :, :inner], 0, 1).reshape(KCONV + 1, DI),
            jnp.sum(taps_found[:, :, inner:], axis=0),
        ],
        axis=1,
    )
    grad_small = jnp.concatenate(
        [jnp.sum(found[0], axis=0), found[1].reshape(-1), taps_found.reshape(-1)]
        + [found[k].reshape(-1) for k in (3, 4, 5)]
    )

    own = block_in.astype(F32)
    block_out = (own + branch.astype(F32)).astype(BF16)
    scale = lax.rsqrt(jnp.mean(own * own, axis=-1, keepdims=True) + NORM_EPS)
    d_scaled = d_normed * norm_gain
    d_own = scale * (
        d_scaled - own * scale * scale * jnp.mean(d_scaled * own, axis=-1, keepdims=True)
    )
    input_grad = (out_grad.astype(F32) + d_own).astype(BF16)
    in_second, in_new = adam_step(w_in, w_in_m, w_in_v, grad_in, RATE_BIG)
    out_second, out_new = adam_step(w_out, w_out_m, w_out_v, grad_out, RATE_BIG)
    small_second, small_updated = adam_step(small_params, small_m, small_v, grad_small, RATE_SMALL)
    return (
        block_out,
        input_grad,
        grad_in,
        in_second,
        in_new,
        grad_out,
        out_second,
        out_new,
        grad_small,
        small_second,
        small_updated,
    )


def solution(mesh):
    dp = ("dp",)
    if mesh.shape["dp"] == 8 and mesh.shape["ctx"] == 4:
        dp = ("high", "low", "side")
        mesh = Mesh(np.asarray(mesh.devices).reshape(2, 2, 2, 4), dp + ("ctx",))
    rows = P(dp + ("ctx",), None)
    spread = P(dp, "ctx", None)
    return jax.shard_map(
        functools.partial(shards, dp),
        mesh=mesh,
        in_specs=(spread, spread) + (rows,) * 6 + (P(),) * 3,
        out_specs=(spread, spread) + (rows,) * 6 + (P(),) * 3,
        check_vma=False,
    )
```

```python
import functools

import jax
import jax.numpy as jnp
import numpy as np
from jax import lax
from jax.experimental import pallas as pl
from jax.experimental.pallas import tpu as pltpu
from jax.sharding import Mesh
from jax.sharding import PartitionSpec as P

D = 1024
HEADS = 32
HD = 64
NS = 128
KCONV = 4
STEP = 10
DI = 2048
CHANNELS = DI + 2 * NS

CHUNK = 128
LANES = 128
RIM = 8
ROWS = 256

NORM_EPS = 1e-05
ADAM_EPS = 1e-08
BETA_ONE = 0.9
BETA_TWO = 0.999
RATE_BIG = 0.03
RATE_SMALL = 0.3
DECAY_WEIGHT = 0.01

F32 = jnp.float32
BF16 = jnp.bfloat16
VMEM_BYTES = 60 * 1024 * 1024


def dot(a, b, contract=((1,), (0,))):
    return lax.dot_general(a, b, (contract, ((), ())), preferred_element_type=F32)


def terms(a, count):
    parts = []
    for _ in range(count):
        part = a.astype(BF16)
        parts.append(part)
        a = a - part.astype(F32)
    return parts


def spread_dot(a, spread):
    return dot(
        jnp.concatenate(terms(a, 2), axis=1), jnp.concatenate([spread, spread], axis=0)
    )


def sum_dot(ones, a, count):
    return sum(dot(ones, part) for part in terms(a, count))


ROW_ROW = ((1,), (1,))
COL_COL = ((0,), (0,))


def sigmoid(v):
    return 1.0 / (1.0 + jnp.exp(-v))


def softplus(v):
    return jnp.maximum(v, 0.0) + jnp.log1p(jnp.exp(-jnp.abs(v)))


def expander(inner):
    head = lax.broadcasted_iota(jnp.int32, (LANES, inner), 0)
    column = lax.broadcasted_iota(jnp.int32, (LANES, inner), 1)
    inside = (column >= head * HD) & (column < (head + 1) * HD)
    return jnp.where(inside, 1.0, 0.0).astype(BF16)


def lower_ones():
    row = lax.broadcasted_iota(jnp.int32, (CHUNK, CHUNK), 0)
    column = lax.broadcasted_iota(jnp.int32, (CHUNK, CHUNK), 1)
    return jnp.where(row >= column, 1.0, 0.0)


def row_sums(a):
    lanes = a[:, :LANES]
    for start in range(LANES, a.shape[1], LANES):
        lanes = lanes + a[:, start : start + LANES]
    return jnp.sum(lanes.T, axis=0, keepdims=True)


def side_by_side(pair):
    lane = lax.broadcasted_iota(jnp.int32, pair.shape, 1)
    zero = jnp.zeros_like(pair)
    return jnp.concatenate(
        [jnp.where(lane < HD, pair, zero), jnp.where(lane < HD, zero, pair)], axis=0
    )


def decay_terms(step, rate, spread, tri):
    cum = sum_dot(tri.astype(BF16), rate, 3)
    total = cum[CHUNK - 1 : CHUNK, :]
    wide = spread_dot(
        jnp.concatenate([step, jnp.exp(cum), jnp.exp(total - cum)], axis=0), spread
    )
    return cum, cum.T, wide[:CHUNK], wide[CHUNK : 2 * CHUNK], wide[2 * CHUNK :]


def pair_mixing(cum, cum_t, scores, pair):
    decays = []
    for head in (2 * pair, 2 * pair + 1):
        differ = cum[:, head : head + 1] - cum_t[head : head + 1, :]
        decays.append(jnp.exp(jnp.minimum(differ, 0.0)))
    return decays, [(decay * scores).astype(BF16) for decay in decays]


def conv_forward(padded_ref, taps, rows):
    total = taps[KCONV : KCONV + 1, :]
    for k in range(KCONV):
        start = RIM - (KCONV - 1) + k
        total = total + taps[k : k + 1, :] * padded_ref[start : start + rows, :]
    return total


def forward_kernel(
    inner,
    order_ref,
    tokens_ref,
    gain_ref,
    taps_ref,
    heads_ref,
    skip_ref,
    mine_ref,
    other_ref,
    low_ref,
    rest_ref,
    mixed_ref,
    incoming_ref,
    weight_ref,
    padded,
    state,
):
    rows = tokens_ref.shape[1]
    conv = inner + 2 * NS

    @pl.when((pl.program_id(0) == 0) & (pl.program_id(1) == 0))
    def _():
        if mine_ref.shape[0] == D:
            weight_ref[...] = mine_ref[...]
        else:
            mine = pl.multiple_of(order_ref[0] * (D // 2), D // 2)
            other = pl.multiple_of((1 - order_ref[0]) * (D // 2), D // 2)
            weight_ref[pl.ds(mine, D // 2), :] = mine_ref[...]
            weight_ref[pl.ds(other, D // 2), :] = other_ref[...]

    @pl.when(pl.program_id(1) == 0)
    def _():
        padded[0:RIM, :] = jnp.zeros((RIM, conv), F32)
        state[...] = jnp.zeros_like(state)

    @pl.when(pl.program_id(1) > 0)
    def _():
        padded[0:RIM, :] = padded[rows : rows + RIM, :]

    tokens_low = tokens_ref[0]
    tokens = tokens_low.astype(F32)
    scale = lax.rsqrt(jnp.mean(tokens * tokens, axis=1, keepdims=True) + NORM_EPS)
    low = (tokens * scale * gain_ref[...]).astype(BF16)
    low_ref[0] = low
    projected = dot(low, weight_ref[...])
    rest_ref[0] = projected
    padded[RIM : RIM + rows, :] = projected[:, :conv]
    conv_out = conv_forward(padded, taps_ref[...], rows)
    active = conv_out * sigmoid(conv_out)
    heads = heads_ref[...]
    step_all = softplus(projected[:, conv:] + heads[0:1, :])
    rate_all = heads[1:2, :] * step_all
    skip = skip_ref[...]
    spread = expander(inner)
    tri = lower_ones()
    for c in range(rows // CHUNK):
        part = slice(c * CHUNK, (c + 1) * CHUNK)
        values = active[part, :inner]
        in_b = active[part, inner : inner + NS].astype(BF16)
        out_c = active[part, inner + NS :].astype(BF16)
        cum, cum_t, step_x, grown, remain = decay_terms(
            step_all[part], rate_all[part], spread, tri
        )
        stepped = values * step_x
        stepped_low = stepped.astype(BF16)
        scores = dot(out_c, in_b, ROW_ROW) * tri
        inside = []
        for pair in range(inner // LANES):
            lanes = slice(pair * LANES, (pair + 1) * LANES)
            _, mixing = pair_mixing(cum, cum_t, scores, pair)
            inside.append(
                dot(jnp.concatenate(mixing, axis=1), side_by_side(stepped_low[:, lanes]))
            )
        before = state[...]
        before_low = before.astype(BF16)
        incoming_ref[0, c] = before_low
        outer = grown * dot(out_c, before_low)
        mixed_ref[0, part, :] = jnp.concatenate(inside, axis=1) + outer + skip * values
        state[...] = grown[CHUNK - 1 : CHUNK, :] * before + dot(
            in_b, (remain * stepped).astype(BF16), COL_COL
        )


def stats_kernel(joined, order_ref, up_ref, low_ref, mixed_ref, gain_ref, *refs):
    if joined:
        both_ref, weight_out_ref, weight_gate_ref, gate_ref, d_out_ref, stats_ref = refs
        inner = gate_ref.shape[2]

        @pl.when((pl.program_id(0) == 0) & (pl.program_id(1) == 0))
        def _():
            deep, tall = D // 8, inner // 8
            place = 0
            for quarter in range(4):
                for half in (order_ref[0], 1 - order_ref[0]):
                    block = half * 4 + quarter
                    rows = pl.ds(pl.multiple_of(block * deep, deep), deep)
                    weight_gate_ref[rows, :] = both_ref[place : place + deep, :]
                    place = place + deep
                    rows = pl.ds(pl.multiple_of(block * tall, tall), tall)
                    for k in range(D // inner):
                        columns = slice(k * inner, (k + 1) * inner)
                        weight_out_ref[rows, columns] = both_ref[place : place + tall, :]
                        place = place + tall

    else:
        weight_out_ref, weight_gate_ref, gate_ref, d_out_ref, stats_ref = refs
    d_out = dot(up_ref[0], weight_out_ref[...], ROW_ROW)
    d_out_ref[0] = d_out.astype(BF16)
    gate = dot(low_ref[0], weight_gate_ref[...])
    gate_ref[0] = gate
    gated = mixed_ref[0] * gate * sigmoid(gate)
    stats_ref[0, 0:1, :] = row_sums(gated * gated)
    stats_ref[0, 1:2, :] = row_sums(d_out * gain_ref[...] * gated)


def row_to_lanes(row):
    return jnp.broadcast_to(row, (LANES, row.shape[1])).T[:, 0:1]


def keep_or_send(refs, kept, value):
    if len(refs) == 1:
        refs[0][0] = value
        return

    @pl.when(kept)
    def _():
        refs[0][0] = value

    @pl.when(jnp.logical_not(kept))
    def _():
        refs[1][0] = value


def gate_back_kernel(
    order_ref,
    up_ref,
    weight_ref,
    gate_ref,
    mixed_ref,
    gain_ref,
    d_out_ref,
    stats_ref,
    low_ref,
    *refs,
):
    *branch_refs, grad_ref, grad_gate_ref, d_mixed_ref, d_gate_ref, d_gain_ref = refs[:-2]
    total, total_gate = refs[-2:]
    first = (pl.program_id(0) == 0) & (pl.program_id(1) == 0)
    last_one = pl.program_id(0) == pl.num_programs(0) - 1
    last_two = pl.program_id(1) == pl.num_programs(1) - 1

    @pl.when(first)
    def _():
        total[...] = jnp.zeros_like(total)
        total_gate[...] = jnp.zeros_like(total_gate)
        d_gain_ref[...] = jnp.zeros_like(d_gain_ref)

    stats = stats_ref[0, 0]
    for k in range(1, stats_ref.shape[0]):
        stats = stats + stats_ref[k, 0]
    squares = row_to_lanes(stats[0:1])
    products = row_to_lanes(stats[1:2])
    scale = lax.rsqrt(squares * (1.0 / DI) + NORM_EPS)
    gate = gate_ref[0]
    mixed = mixed_ref[0]
    gain = gain_ref[...]
    d_out = d_out_ref[0].astype(F32)
    sig = sigmoid(gate)
    silu = gate * sig
    gated = mixed * silu
    unit = gated * scale
    low = (unit * gain).astype(BF16)
    keep_or_send(branch_refs, pl.program_id(1) < 2, dot(low, weight_ref[...]).astype(BF16))
    total[...] += dot(low, up_ref[0], COL_COL)
    d_gain_ref[...] += jnp.sum(d_out * unit, axis=0, keepdims=True)
    d_gated = scale * (gain * d_out - unit * (scale * products * (1.0 / DI)))
    d_mixed_ref[0] = (d_gated * silu).astype(BF16)
    d_gate = (d_gated * mixed * (sig + silu * (1.0 - sig))).astype(BF16)
    d_gate_ref[0] = d_gate
    total_gate[...] += dot(low_ref[0], d_gate, COL_COL)

    @pl.when(last_one & last_two)
    def _():
        grad_ref[...] = total[...].astype(BF16)
        grad_gate_ref[...] = total_gate[...].astype(BF16)


def mixer_back_kernel(
    inner,
    first,
    table_ref,
    rest_ref,
    rim_ref,
    mixed_ref,
    d_mixed_ref,
    incoming_ref,
    taps_ref,
    heads_ref,
    skip_ref,
    low_ref,
    d_gate_ref,
    tokens_ref,
    weight_gate_ref,
    weight_rest_ref,
    after_ref,
    part_ref,
    *refs,
):
    *normed_refs, d_gain_ref, grad_ref, d_taps_ref, d_heads_ref, d_skip_ref = refs[:-6]
    padded, later, carried, d_active, total, d_rest_ref = refs[-6:]
    rows = rest_ref.shape[1]
    conv = inner + 2 * NS
    block = pl.num_programs(0) - 1 - pl.program_id(0)

    @pl.when(pl.program_id(0) == 0)
    def _():
        d_taps_ref[...] = jnp.zeros_like(d_taps_ref)
        d_heads_ref[...] = jnp.zeros_like(d_heads_ref)
        d_skip_ref[...] = jnp.zeros_like(d_skip_ref)
        d_gain_ref[...] = jnp.zeros_like(d_gain_ref)
        if first:
            total[...] = jnp.zeros_like(total)
        else:
            pltpu.sync_copy(part_ref, total)
        carried[...] = jnp.zeros_like(carried)
        later[rows : rows + RIM, :] = jnp.zeros((RIM, conv), F32)

    @pl.when(pl.program_id(0) > 0)
    def _():
        later[rows : rows + RIM, :] = later[0:RIM, :]

    rim = rim_ref[0][:, :conv]
    padded[0:RIM, :] = jnp.where(block > 0, rim, jnp.zeros_like(rim))
    padded[RIM : RIM + rows, :] = rest_ref[0][:, :conv]
    taps = taps_ref[...]
    conv_out = conv_forward(padded, taps, rows)
    sig = sigmoid(conv_out)
    active = conv_out * sig
    slope = sig + active * (1.0 - sig)
    heads = heads_ref[...]
    raw = rest_ref[0][:, conv:] + heads[0:1, :]
    step_all = softplus(raw)
    rate_all = heads[1:2, :] * step_all
    skip = skip_ref[...]
    spread = expander(inner)
    tri = lower_ones()
    upper = tri.T.astype(BF16)
    for c in reversed(range(rows // CHUNK)):
        part = slice(c * CHUNK, (c + 1) * CHUNK)
        values = active[part, :inner]
        in_b = active[part, inner : inner + NS].astype(BF16)
        out_c = active[part, inner + NS :].astype(BF16)
        step = step_all[part]
        rate = rate_all[part]
        cum, cum_t, step_x, grown, remain = decay_terms(step, rate, spread, tri)
        stepped = values * step_x
        stepped_low = stepped.astype(BF16)
        scores = dot(out_c, in_b, ROW_ROW) * tri
        d_low = d_mixed_ref[0, part, :]
        d_mixed = d_low.astype(F32)
        d_scores = jnp.zeros((CHUNK, CHUNK), F32)
        inside = []
        for pair in range(inner // LANES):
            lanes = slice(pair * LANES, (pair + 1) * LANES)
            decays, mixing = pair_mixing(cum, cum_t, scores, pair)
            d_two = side_by_side(d_low[:, lanes])
            d_mixing = dot(d_two, stepped_low[:, lanes], ROW_ROW)
            d_scores += decays[0] * d_mixing[:CHUNK] + decays[1] * d_mixing[CHUNK:]
            inside.append(dot(jnp.concatenate(mixing, axis=0), d_two, COL_COL))
        before = incoming_ref[0, c]
        ahead = carried[...]
        ahead_low = ahead.astype(BF16)
        through = remain * dot(in_b, ahead_low)
        outer = (grown * d_mixed).astype(BF16)
        d_scores_low = (d_scores * tri).astype(BF16)
        d_in_b = dot((remain * stepped).astype(BF16), ahead_low, ROW_ROW) + dot(
            d_scores_low, out_c, COL_COL
        )
        d_out_c = dot(outer, before, ROW_ROW) + dot(d_scores_low, in_b)
        d_stepped = jnp.concatenate(inside, axis=1) + through
        stepped_near = stepped_low.astype(F32)
        both = d_mixed * (mixed_ref[0, part, :] - skip * values)
        d_cum_x = both - stepped_near * d_stepped
        d_step_x = d_stepped * values
        grown_total = grown[CHUNK - 1 : CHUNK, :]
        d_total_x = jnp.sum(stepped_near * through, axis=0, keepdims=True) + grown_total * jnp.sum(
            ahead * before.astype(F32), axis=0, keepdims=True
        )
        gathered = jnp.concatenate(
            [d_cum_x, d_step_x, jnp.broadcast_to(d_total_x, (16, inner))], axis=0
        )
        narrow = sum(dot(part, spread, ROW_ROW) for part in terms(gathered, 2))
        d_rate = sum_dot(upper, narrow[:CHUNK], 2) + narrow[2 * CHUNK : 2 * CHUNK + 1]
        d_raw = (narrow[CHUNK : 2 * CHUNK] + heads[1:2, :] * d_rate) * sigmoid(raw[part])
        d_heads_ref[0:1, :] += jnp.sum(d_raw, axis=0, keepdims=True)
        d_heads_ref[1:2, :] += jnp.sum(d_rate * rate, axis=0, keepdims=True)
        d_skip_ref[...] += jnp.sum(d_mixed * values, axis=0, keepdims=True)
        d_rest_ref[part, conv:] = d_raw.astype(BF16)
        d_active[part, :inner] = d_stepped * step_x + skip * d_mixed
        d_active[part, inner : inner + NS] = d_in_b
        d_active[part, inner + NS :] = d_out_c
        carried[...] = grown_total * ahead + dot(out_c, outer, COL_COL)
    d_conv_out = d_active[...] * slope
    later[0:rows, :] = d_conv_out
    d_conv_in = jnp.zeros((rows, conv), F32)
    for k in range(KCONV):
        ahead_rows = KCONV - 1 - k
        start = RIM - (KCONV - 1) + k
        d_conv_in += taps[k : k + 1, :] * later[ahead_rows : ahead_rows + rows, :]
        d_taps_ref[k : k + 1, :] += jnp.sum(
            d_conv_out * padded[start : start + rows, :], axis=0, keepdims=True
        )
    d_taps_ref[KCONV : KCONV + 1, :] += jnp.sum(d_conv_out, axis=0, keepdims=True)
    d_rest_ref[:, :conv] = d_conv_in.astype(BF16)
    d_rest = d_rest_ref[...]
    total[...] += dot(low_ref[0], d_rest, COL_COL)
    d_normed = dot(d_gate_ref[0], weight_gate_ref[...], ROW_ROW) + dot(
        d_rest, weight_rest_ref[...], ROW_ROW
    )
    tokens = tokens_ref[0].astype(F32)
    scale = lax.rsqrt(jnp.mean(tokens * tokens, axis=1, keepdims=True) + NORM_EPS)
    d_gain_ref[...] += jnp.sum(d_normed * (tokens * scale), axis=0, keepdims=True)
    keep_or_send(normed_refs, table_ref[pl.program_id(0)] == 1, d_normed.astype(BF16))

    @pl.when(block == 0)
    def _():
        grad_ref[...] = total[...].astype(grad_ref.dtype)


def whole(shape):
    return pl.BlockSpec(shape, lambda *_: (0,) * len(shape))


def by_rows(width):
    return pl.BlockSpec((1, ROWS, width), lambda s, b, *_: (s, b, 0))


def by_order(width):
    return pl.BlockSpec((1, ROWS, width), lambda s, b, order: (s, order[b], 0))


def left_alone():
    return pl.BlockSpec(memory_space=pl.ANY)


def cost(micros):
    return pl.CostEstimate(
        flops=int(micros * 1.1e9), bytes_accessed=int(micros * 2e6), transcendentals=0
    )


def params():
    return pltpu.CompilerParams(
        vmem_limit_bytes=VMEM_BYTES
    )


def shaped(shape, dtype=F32):
    return jax.ShapeDtypeStruct(shape, dtype)


def run_forward(order, tokens, norm_gain, halves, taps, heads, skip):
    count, length, _ = tokens.shape
    inner = skip.shape[1]
    rest = halves[0].shape[1]
    conv = inner + 2 * NS
    chunks = ROWS // CHUNK
    fixed = [norm_gain, taps, heads, skip, halves[0], halves[-1]]
    return pl.pallas_call(
        functools.partial(forward_kernel, inner),
        grid_spec=pltpu.PrefetchScalarGridSpec(
            num_scalar_prefetch=1,
            grid=(count, length // ROWS),
            in_specs=[by_rows(D)] + [whole(value.shape) for value in fixed],
            out_specs=[
                by_rows(D),
                by_rows(rest),
                by_rows(inner),
                pl.BlockSpec((1, chunks, NS, inner), lambda s, b, *_: (s, b, 0, 0)),
                whole((D, rest)),
            ],
            scratch_shapes=[pltpu.VMEM((RIM + ROWS, conv), F32), pltpu.VMEM((NS, inner), F32)],
        ),
        out_shape=[
            shaped((count, length, D), BF16),
            shaped((count, length, rest)),
            shaped((count, length, inner)),
            shaped((count, length // CHUNK, NS, inner), BF16),
            shaped((D, rest), BF16),
        ],
        compiler_params=params(),
        cost_estimate=cost(1),
        name="forward_mixer",
    )(order, tokens, *fixed)


def run_stats(order, upstream, low, mixed, gate_gain, weights):
    count, length, inner = mixed.shape
    joined = len(weights) == 1
    found_specs = [whole((inner, D)), whole((D, inner))] * joined
    found_shapes = [shaped((inner, D), BF16), shaped((D, inner), BF16)] * joined
    found = pl.pallas_call(
        functools.partial(stats_kernel, joined),
        grid_spec=pltpu.PrefetchScalarGridSpec(
            num_scalar_prefetch=1,
            grid=(count, length // ROWS),
            in_specs=[by_rows(D), by_rows(D), by_rows(inner), whole((1, inner))]
            + [whole(weight.shape) for weight in weights],
            out_specs=found_specs
            + [
                by_rows(inner),
                by_rows(inner),
                pl.BlockSpec((1, 2, ROWS), lambda s, b, *_: (s, 0, b)),
            ],
        ),
        out_shape=found_shapes
        + [
            shaped((count, length, inner)),
            shaped((count, length, inner), BF16),
            shaped((count, 2, length)),
        ],
        compiler_params=params(),
        cost_estimate=cost(1),
        name="gate_stats",
    )(order, upstream, low, mixed, gate_gain, *weights)
    return found if joined else [*weights, *found]


def kept_and_sent(split, count, length, place):
    if not split:
        return [place(lambda order, b: order[b])], [shaped((count, length, D), BF16)]
    specs = [
        place(lambda order, b: jnp.minimum(b, 1)),
        place(lambda order, b: jnp.maximum(b - 2, 0)),
    ]
    return specs, [shaped((count, 2 * ROWS, D), BF16)] * 2


def run_gate_back(split, order, upstream, weight, gate, mixed, gate_gain, d_out, stats, low):
    count, length, inner = gate.shape

    def place(group):
        return pl.BlockSpec((1, ROWS, D), lambda s, b, order: (s, group(order, b), 0))

    branch_specs, branch_shapes = kept_and_sent(split, count, length, place)
    return pl.pallas_call(
        gate_back_kernel,
        grid_spec=pltpu.PrefetchScalarGridSpec(
            num_scalar_prefetch=1,
            grid=(count, length // ROWS),
            in_specs=[
                by_order(D),
                whole((inner, D)),
                by_order(inner),
                by_order(inner),
                whole((1, inner)),
                by_order(inner),
                pl.BlockSpec(
                    (stats.shape[0], 1, 2, ROWS), lambda s, b, order: (0, s, 0, order[b])
                ),
                by_order(D),
            ],
            out_specs=branch_specs
            + [
                whole((inner, D)),
                whole((D, inner)),
                by_order(inner),
                by_order(inner),
                whole((1, inner)),
            ],
            scratch_shapes=[pltpu.VMEM((inner, D), F32), pltpu.VMEM((D, inner), F32)],
        ),
        out_shape=branch_shapes
        + [
            shaped((inner, D), BF16),
            shaped((D, inner), BF16),
            shaped((count, length, inner), BF16),
            shaped((count, length, inner), BF16),
            shaped((1, inner)),
        ],
        compiler_params=params(),
        cost_estimate=cost(1),
        name="gate_back",
    )(order, upstream, weight, gate, mixed, gate_gain, d_out, stats, low)


def run_mixer_back(split, s, table, saved, fixed, weights, after, part):
    rest, mixed, d_mixed, incoming, low, d_gate, tokens = saved
    taps, heads, skip = fixed
    count, length, inner = mixed.shape
    conv = inner + 2 * NS
    last = length // ROWS - 1
    chunks = ROWS // CHUNK
    width = rest.shape[2]

    def rows(width):
        return pl.BlockSpec((1, ROWS, width), lambda b, table: (s, last - b, 0))

    if split:
        normed_specs = [
            pl.BlockSpec((1, ROWS, D), lambda b, table: (0, table[4 + b], 0)),
            pl.BlockSpec((1, ROWS, D), lambda b, table: (0, table[8 + b], 0)),
        ]
        normed_shapes = [shaped((1, 2 * ROWS, D), BF16)] * 2
    else:
        normed_specs = [pl.BlockSpec((1, ROWS, D), lambda b, table: (0, last - b, 0))]
        normed_shapes = [shaped((1, length, D), BF16)]
    return pl.pallas_call(
        functools.partial(mixer_back_kernel, inner, s == 0),
        grid_spec=pltpu.PrefetchScalarGridSpec(
            num_scalar_prefetch=1,
            grid=(length // ROWS,),
            in_specs=[
                rows(width),
                pl.BlockSpec(
                    (1, RIM, width),
                    lambda b, table: (s, jnp.maximum((last - b) * (ROWS // RIM) - 1, 0), 0),
                ),
                rows(inner),
                rows(inner),
                pl.BlockSpec((1, chunks, NS, inner), lambda b, table: (s, last - b, 0, 0)),
                whole((RIM, conv)),
                whole((8, LANES)),
                whole((1, inner)),
                rows(D),
                rows(inner),
                rows(D),
                whole((D, inner)),
                whole((D, width)),
                left_alone(),
                left_alone(),
            ],
            out_specs=normed_specs
            + [
                whole((1, D)),
                whole((D, width)),
                whole((RIM, conv)),
                whole((8, LANES)),
                whole((1, inner)),
            ],
            scratch_shapes=[
                pltpu.VMEM((RIM + ROWS, conv), F32),
                pltpu.VMEM((RIM + ROWS, conv), F32),
                pltpu.VMEM((NS, inner), F32),
                pltpu.VMEM((ROWS, conv), F32),
                pltpu.VMEM((D, width), F32),
                pltpu.VMEM((ROWS, width), BF16),
            ],
        ),
        out_shape=normed_shapes
        + [
            shaped((1, D)),
            shaped((D, width), BF16 if s == count - 1 else F32),
            shaped((RIM, conv)),
            shaped((8, LANES)),
            shaped((1, inner)),
        ],
        compiler_params=params(),
        cost_estimate=cost(1),
        name="mixer_back",
    )(table, rest, rest, mixed, d_mixed, incoming, *fixed, low, d_gate, tokens, *weights, after, part)


def swapped(value, axis, mask=1):
    count = lax.axis_size(axis)
    return lax.ppermute(value, axis, [(a, a ^ mask) for a in range(count)])


def chip_sums(parts):
    if len(parts) == 1:
        total = lax.psum_scatter(parts[0], "ctx", scatter_dimension=1, tiled=True)
        return total.astype(F32), None
    kept, sent = parts
    got = swapped(sent, "ctx", 1)
    own = kept[:, :ROWS].astype(F32) + got[:, :ROWS].astype(F32)
    return own, (kept[:, ROWS:].astype(F32) + got[:, ROWS:].astype(F32)).astype(BF16)


def across_sums(own, sent):
    if sent is None:
        return own
    return own + swapped(sent, "ctx", 2).astype(F32)


def sum_over(value, axes):
    if len(axes) == 1:
        return lax.psum(value, axes)
    for axis in axes:
        value = value + swapped(value, axis)
    return value


def by_rank(value):
    if lax.axis_size("ctx") != 4:
        return lax.all_gather(value, "ctx", axis=0)
    rank = lax.axis_index("ctx")
    near, across = swapped(value, "ctx", 1), swapped(value, "ctx", 2)
    found = [value, near, across, swapped(across, "ctx", 1)]
    odd, high = (rank & 1) == 1, rank >= 2
    found = [jnp.where(odd, found[k ^ 1], found[k]) for k in range(4)]
    return jnp.stack([jnp.where(high, found[k ^ 2], found[k]) for k in range(4)])


def to_all(value, axes):
    return lax.all_to_all(value, axes, split_axis=0, concat_axis=0, tiled=True)


def to_every(value, axes):
    times = 1
    for axis in axes:
        times = times * lax.axis_size(axis)
    return to_all(jnp.broadcast_to(value[None], (times,) + value.shape).reshape(-1, value.shape[1]), axes)


def adam_step(weight, first_old, second_old, gradient, step_rate):
    first_new = BETA_ONE * first_old + (1.0 - BETA_ONE) * gradient
    second_new = BETA_TWO * second_old + (1.0 - BETA_TWO) * gradient * gradient
    first_hat = first_new / (1.0 - BETA_ONE**STEP)
    second_hat = second_new / (1.0 - BETA_TWO**STEP)
    weight_new = weight - step_rate * (
        first_hat / (jnp.sqrt(second_hat) + ADAM_EPS) + DECAY_WEIGHT * weight
    )
    return (second_new, weight_new)


def pad_lanes(value, width):
    return jnp.pad(value, [(0, 0)] * (value.ndim - 1) + [(0, width - value.shape[-1])])


def shards(
    dp,
    block_in,
    out_grad,
    w_in,
    w_in_m,
    w_in_v,
    w_out,
    w_out_m,
    w_out_v,
    small_params,
    small_m,
    small_v,
):
    axes = dp + ("ctx",)
    n_dp, n_ctx = lax.axis_size(dp), lax.axis_size("ctx")
    rank = lax.axis_index("ctx")
    heads = HEADS // n_ctx
    inner = heads * HD
    conv = inner + 2 * NS
    count = block_in.shape[0]

    moves = []
    for block in range(n_dp * n_ctx):
        moves.append((block, (block % n_dp) * n_ctx + block // n_dp))
    mine_out = lax.ppermute(w_out.astype(BF16), axes, moves)
    tokens = lax.all_gather(block_in, "ctx", axis=1, tiled=True)
    upstream = lax.all_gather(out_grad, "ctx", axis=1, tiled=True)
    w_in_low = w_in.astype(BF16)
    slices = []
    for r in range(n_ctx):
        first = DI + CHANNELS + r * heads
        slices.append(
            jnp.concatenate(
                [
                    w_in_low[:, DI + r * inner : DI + (r + 1) * inner],
                    w_in_low[:, 2 * DI : 2 * DI + 2 * NS],
                    pad_lanes(w_in_low[:, first : first + heads], LANES),
                    w_in_low[:, r * inner : (r + 1) * inner],
                ],
                axis=1,
            )
        )
    rest = conv + LANES
    sent = jnp.concatenate(slices, axis=0)
    mine_in = to_all(sent, "ctx")
    mine_rest = mine_in[:, :rest]
    if len(dp) > 1:
        columns = [mine_out[:, k * inner : (k + 1) * inner] for k in range(D // inner)]
        mine_both = jnp.concatenate([mine_in[:, rest:]] + columns, axis=0)
        other_rest = swapped(mine_rest, dp[0])
        other_both = swapped(mine_both, dp[0])
        mine_rest, mine_out = lax.optimization_barrier((mine_rest, mine_out))
        weight_halves = [to_every(mine_rest, dp[1:]), to_every(other_rest, dp[1:])]
        both = jnp.concatenate([mine_both, other_both], axis=0)
        both, *weight_halves = lax.optimization_barrier((both, *weight_halves))
        weights = [to_every(both, dp[1:])]
    else:
        weight_halves = [lax.all_gather(mine_rest, dp, axis=0, tiled=True)]
        weights = [
            lax.all_gather(value, dp, axis=0, tiled=True)
            for value in (mine_out, mine_in[:, rest:])
        ]

    offset = 0
    pieces = []
    for amount in (D, DI, KCONV * CHANNELS, CHANNELS, HEADS, HEADS, HEADS):
        pieces.append(small_params[offset : offset + amount])
        offset = offset + amount
    norm_gain = pieces[0].reshape(1, D)
    gate_gain = lax.dynamic_slice(pieces[1], (rank * inner,), (inner,)).reshape(1, inner)
    taps_all = jnp.concatenate([pieces[2].reshape(KCONV, CHANNELS), pieces[3][None]], axis=0)
    taps = jnp.concatenate(
        [lax.dynamic_slice(taps_all, (0, rank * inner), (KCONV + 1, inner)), taps_all[:, DI:]],
        axis=1,
    )
    taps = jnp.pad(taps, ((0, RIM - KCONV - 1), (0, 0)))
    dt_bias = lax.dynamic_slice(pieces[4], (rank * heads,), (heads,))
    decay = -jnp.exp(lax.dynamic_slice(pieces[5], (rank * heads,), (heads,)))
    head_rows = jnp.pad(jnp.stack([dt_bias, decay]), ((0, 6), (0, LANES - heads)))
    skip = jnp.repeat(lax.dynamic_slice(pieces[6], (rank * heads,), (heads,)), HD).reshape(1, inner)

    split = n_ctx == 4 and block_in.shape[1] == ROWS
    order = jnp.arange(n_ctx * block_in.shape[1] // ROWS, dtype=jnp.int32)
    if split:
        order = rank.astype(jnp.int32) ^ jnp.array([0, 2, 1, 3], jnp.int32)
    high = lax.axis_index(dp[0]) if len(dp) > 1 else rank * 0
    high = high.astype(jnp.int32).reshape(1)
    low, rest, mixed, incoming, weight_rest = run_forward(
        high, tokens, norm_gain, weight_halves, taps, head_rows, skip
    )
    weight_out, weight_gate, gate, d_out, stats = run_stats(
        high, upstream, low, mixed, gate_gain, weights
    )
    stats = lax.all_gather(stats, "ctx")
    *branch, grad_out, grad_gate, d_mixed, d_gate, d_gate_gain = run_gate_back(
        split, order, upstream, weight_out, gate, mixed, gate_gain, d_out, stats, low
    )
    grad_out = to_all(grad_out, dp)
    branch, branch_sent = chip_sums(branch)

    own_rows = w_in.shape[0]

    def summed(got):
        return jnp.sum(got.astype(F32).reshape(-1, n_ctx, own_rows, got.shape[1]), axis=0)

    after = grad_gate if branch_sent is None else branch_sent
    branch = across_sums(branch, branch_sent)
    table = jnp.zeros((12,), jnp.int32)
    if split:
        masks = rank.astype(jnp.int32) ^ jnp.array([3, 2, 1, 0], jnp.int32)
        kept = 1 - (masks & 1)
        places = masks >> 1
        early, late = places[jnp.array([0, 0, 2, 2])], places[jnp.array([1, 1, 1, 3])]
        one_first = kept[0] == 1
        table = jnp.concatenate(
            [kept, jnp.where(one_first, early, late), jnp.where(one_first, late, early)]
        )
    saved = (rest, mixed, d_mixed, incoming, low, d_gate, tokens)
    fixed = (taps, head_rows, skip)
    weights = (weight_gate, weight_rest)
    grad_rest = after
    smalls = []
    normeds = []
    for s in range(count):
        found = run_mixer_back(split, s, table, saved, fixed, weights, after, grad_rest)
        *d_normed, d_gain, grad_rest, d_taps, d_heads, d_skip = found
        smalls.append([d_gain, d_taps, d_heads, d_skip])
        if s == 0:
            grad_out, *d_normed = lax.optimization_barrier((grad_out, *d_normed))
        else:
            grad_gate, *d_normed = lax.optimization_barrier((grad_gate, *d_normed))
        d_normed, normed_sent = chip_sums(d_normed)
        after = d_normed if normed_sent is None else normed_sent
        if s == 0:
            grad_gate, after = lax.optimization_barrier((grad_gate, after))
            grad_gate = to_all(grad_gate, axes)
        normeds.append(across_sums(d_normed, normed_sent))
    d_norm_gain, d_taps, d_heads, d_skip = (sum(parts) for parts in zip(*smalls))
    parts = (
        d_norm_gain.reshape(-1),
        d_gate_gain.reshape(-1),
        d_taps[: KCONV + 1].reshape(-1),
        d_heads[0, :heads],
        d_heads[1, :heads],
        jnp.sum(d_skip.reshape(heads, HD), axis=1),
    )
    mine = jnp.concatenate(parts)
    mine = jnp.pad(mine, (0, -mine.shape[0] % (8 * LANES))).reshape(-1, LANES)
    every = by_rank(sum_over(mine, dp)).reshape(n_ctx, -1)
    grad_rest, every, *normeds = lax.optimization_barrier((grad_rest, every, *normeds))
    grad_rest = to_all(grad_rest, axes)
    d_normed = jnp.concatenate(normeds, axis=0)
    grad_out = jnp.sum(grad_out.astype(F32).reshape(n_dp, -1, D), axis=0)
    grad_out = lax.ppermute(grad_out, axes, [(b, a) for a, b in moves])
    grad_gate = summed(grad_gate)
    grad_rest = summed(grad_rest)
    columns = [grad_gate[r] for r in range(n_ctx)]
    columns += [grad_rest[r, :, :inner] for r in range(n_ctx)]
    columns += [jnp.sum(grad_rest[:, :, inner:conv], axis=0)]
    columns += [grad_rest[r, :, conv : conv + heads] for r in range(n_ctx)]
    grad_in = jnp.concatenate(columns, axis=1)

    offset = 0
    found = []
    for part in parts:
        found.append(every[:, offset : offset + part.shape[0]])
        offset = offset + part.shape[0]
    taps_found = found[2].reshape(n_ctx, KCONV + 1, conv)
    taps_found = jnp.concatenate(
        [
            jnp.swapaxes(taps_found[:, :, :inner], 0, 1).reshape(KCONV + 1, DI),
            jnp.sum(taps_found[:, :, inner:], axis=0),
        ],
        axis=1,
    )
    grad_small = jnp.concatenate(
        [jnp.sum(found[0], axis=0), found[1].reshape(-1), taps_found.reshape(-1)]
        + [found[k].reshape(-1) for k in (3, 4, 5)]
    )

    own = block_in.astype(F32)
    block_out = (own + branch.astype(F32)).astype(BF16)
    scale = lax.rsqrt(jnp.mean(own * own, axis=-1, keepdims=True) + NORM_EPS)
    d_scaled = d_normed * norm_gain
    d_own = scale * (
        d_scaled - own * scale * scale * jnp.mean(d_scaled * own, axis=-1, keepdims=True)
    )
    input_grad = (out_grad.astype(F32) + d_own).astype(BF16)
    in_second, in_new = adam_step(w_in, w_in_m, w_in_v, grad_in, RATE_BIG)
    out_second, out_new = adam_step(w_out, w_out_m, w_out_v, grad_out, RATE_BIG)
    small_second, small_updated = adam_step(small_params, small_m, small_v, grad_small, RATE_SMALL)
    return (
        block_out,
        input_grad,
        grad_in,
        in_second,
        in_new,
        grad_out,
        out_second,
        out_new,
        grad_small,
        small_second,
        small_updated,
    )


def solution(mesh):
    dp = ("dp",)
    if mesh.shape["dp"] == 8 and mesh.shape["ctx"] == 4:
        dp = ("high", "low", "side")
        mesh = Mesh(np.asarray(mesh.devices).reshape(2, 2, 2, 4), dp + ("ctx",))
    rows = P(dp + ("ctx",), None)
    spread = P(dp, "ctx", None)
    return jax.shard_map(
        functools.partial(shards, dp),
        mesh=mesh,
        in_specs=(spread, spread) + (rows,) * 6 + (P(),) * 3,
        out_specs=(spread, spread) + (rows,) * 6 + (P(),) * 3,
        check_vma=False,
    )
```

```python
import functools

import jax
import jax.numpy as jnp
import numpy as np
from jax import lax
from jax.experimental import pallas as pl
from jax.experimental.pallas import tpu as pltpu
from jax.sharding import Mesh
from jax.sharding import PartitionSpec as P

D = 1024
HEADS = 32
HD = 64
NS = 128
KCONV = 4
STEP = 10
DI = 2048
CHANNELS = DI + 2 * NS

CHUNK = 128
LANES = 128
RIM = 8
ROWS = 256

NORM_EPS = 1e-05
ADAM_EPS = 1e-08
BETA_ONE = 0.9
BETA_TWO = 0.999
RATE_BIG = 0.03
RATE_SMALL = 0.3
DECAY_WEIGHT = 0.01

F32 = jnp.float32
BF16 = jnp.bfloat16
VMEM_BYTES = 60 * 1024 * 1024


def dot(a, b, contract=((1,), (0,))):
    return lax.dot_general(a, b, (contract, ((), ())), preferred_element_type=F32)


def terms(a, count):
    parts = []
    for _ in range(count):
        part = a.astype(BF16)
        parts.append(part)
        a = a - part.astype(F32)
    return parts


def spread_dot(a, spread):
    return dot(
        jnp.concatenate(terms(a, 2), axis=1), jnp.concatenate([spread, spread], axis=0)
    )


def sum_dot(ones, a, count):
    return sum(dot(ones, part) for part in terms(a, count))


ROW_ROW = ((1,), (1,))
COL_COL = ((0,), (0,))


def sigmoid(v):
    return 1.0 / (1.0 + jnp.exp(-v))


def softplus(v):
    return jnp.maximum(v, 0.0) + jnp.log1p(jnp.exp(-jnp.abs(v)))


def expander(inner):
    head = lax.broadcasted_iota(jnp.int32, (LANES, inner), 0)
    column = lax.broadcasted_iota(jnp.int32, (LANES, inner), 1)
    inside = (column >= head * HD) & (column < (head + 1) * HD)
    return jnp.where(inside, 1.0, 0.0).astype(BF16)


def lower_ones():
    row = lax.broadcasted_iota(jnp.int32, (CHUNK, CHUNK), 0)
    column = lax.broadcasted_iota(jnp.int32, (CHUNK, CHUNK), 1)
    return jnp.where(row >= column, 1.0, 0.0)


def row_sums(a):
    lanes = a[:, :LANES]
    for start in range(LANES, a.shape[1], LANES):
        lanes = lanes + a[:, start : start + LANES]
    return jnp.sum(lanes.T, axis=0, keepdims=True)


def side_by_side(pair):
    lane = lax.broadcasted_iota(jnp.int32, pair.shape, 1)
    zero = jnp.zeros_like(pair)
    return jnp.concatenate(
        [jnp.where(lane < HD, pair, zero), jnp.where(lane < HD, zero, pair)], axis=0
    )


def decay_terms(step, rate, spread, tri):
    cum = sum_dot(tri.astype(BF16), rate, 3)
    total = cum[CHUNK - 1 : CHUNK, :]
    wide = spread_dot(
        jnp.concatenate([step, jnp.exp(cum), jnp.exp(total - cum)], axis=0), spread
    )
    return cum, cum.T, wide[:CHUNK], wide[CHUNK : 2 * CHUNK], wide[2 * CHUNK :]


def pair_mixing(cum, cum_t, scores, pair):
    decays = []
    for head in (2 * pair, 2 * pair + 1):
        differ = cum[:, head : head + 1] - cum_t[head : head + 1, :]
        decays.append(jnp.exp(jnp.minimum(differ, 0.0)))
    return decays, [(decay * scores).astype(BF16) for decay in decays]


def conv_forward(padded_ref, taps, rows):
    total = taps[KCONV : KCONV + 1, :]
    for k in range(KCONV):
        start = RIM - (KCONV - 1) + k
        total = total + taps[k : k + 1, :] * padded_ref[start : start + rows, :]
    return total


def forward_kernel(
    inner,
    order_ref,
    tokens_ref,
    gain_ref,
    taps_ref,
    heads_ref,
    skip_ref,
    mine_ref,
    other_ref,
    low_ref,
    rest_ref,
    mixed_ref,
    incoming_ref,
    weight_ref,
    padded,
    state,
):
    rows = tokens_ref.shape[1]
    conv = inner + 2 * NS

    @pl.when((pl.program_id(0) == 0) & (pl.program_id(1) == 0))
    def _():
        if mine_ref.shape[0] == D:
            weight_ref[...] = mine_ref[...]
        else:
            mine = pl.multiple_of(order_ref[0] * (D // 2), D // 2)
            other = pl.multiple_of((1 - order_ref[0]) * (D // 2), D // 2)
            weight_ref[pl.ds(mine, D // 2), :] = mine_ref[...]
            weight_ref[pl.ds(other, D // 2), :] = other_ref[...]

    @pl.when(pl.program_id(1) == 0)
    def _():
        padded[0:RIM, :] = jnp.zeros((RIM, conv), F32)
        state[...] = jnp.zeros_like(state)

    @pl.when(pl.program_id(1) > 0)
    def _():
        padded[0:RIM, :] = padded[rows : rows + RIM, :]

    tokens_low = tokens_ref[0]
    tokens = tokens_low.astype(F32)
    scale = lax.rsqrt(jnp.mean(tokens * tokens, axis=1, keepdims=True) + NORM_EPS)
    low = (tokens * scale * gain_ref[...]).astype(BF16)
    low_ref[0] = low
    projected = dot(low, weight_ref[...])
    rest_ref[0] = projected
    padded[RIM : RIM + rows, :] = projected[:, :conv]
    conv_out = conv_forward(padded, taps_ref[...], rows)
    active = conv_out * sigmoid(conv_out)
    heads = heads_ref[...]
    step_all = softplus(projected[:, conv:] + heads[0:1, :])
    rate_all = heads[1:2, :] * step_all
    skip = skip_ref[...]
    spread = expander(inner)
    tri = lower_ones()
    for c in range(rows // CHUNK):
        part = slice(c * CHUNK, (c + 1) * CHUNK)
        values = active[part, :inner]
        in_b = active[part, inner : inner + NS].astype(BF16)
        out_c = active[part, inner + NS :].astype(BF16)
        cum, cum_t, step_x, grown, remain = decay_terms(
            step_all[part], rate_all[part], spread, tri
        )
        stepped = values * step_x
        stepped_low = stepped.astype(BF16)
        scores = dot(out_c, in_b, ROW_ROW) * tri
        inside = []
        for pair in range(inner // LANES):
            lanes = slice(pair * LANES, (pair + 1) * LANES)
            _, mixing = pair_mixing(cum, cum_t, scores, pair)
            inside.append(
                dot(jnp.concatenate(mixing, axis=1), side_by_side(stepped_low[:, lanes]))
            )
        before = state[...]
        before_low = before.astype(BF16)
        incoming_ref[0, c] = before_low
        outer = grown * dot(out_c, before_low)
        mixed_ref[0, part, :] = jnp.concatenate(inside, axis=1) + outer + skip * values
        state[...] = grown[CHUNK - 1 : CHUNK, :] * before + dot(
            in_b, (remain * stepped).astype(BF16), COL_COL
        )


def stats_kernel(joined, order_ref, up_ref, low_ref, mixed_ref, gain_ref, *refs):
    if joined:
        both_ref, weight_out_ref, weight_gate_ref, gate_ref, d_out_ref, stats_ref = refs
        inner = gate_ref.shape[2]

        @pl.when((pl.program_id(0) == 0) & (pl.program_id(1) == 0))
        def _():
            deep, tall = D // 8, inner // 8
            place = 0
            for quarter in range(4):
                for half in (order_ref[0], 1 - order_ref[0]):
                    block = half * 4 + quarter
                    rows = pl.ds(pl.multiple_of(block * deep, deep), deep)
                    weight_gate_ref[rows, :] = both_ref[place : place + deep, :]
                    place = place + deep
                    rows = pl.ds(pl.multiple_of(block * tall, tall), tall)
                    for k in range(D // inner):
                        columns = slice(k * inner, (k + 1) * inner)
                        weight_out_ref[rows, columns] = both_ref[place : place + tall, :]
                        place = place + tall

    else:
        weight_out_ref, weight_gate_ref, gate_ref, d_out_ref, stats_ref = refs
    d_out = dot(up_ref[0], weight_out_ref[...], ROW_ROW)
    d_out_ref[0] = d_out.astype(BF16)
    gate = dot(low_ref[0], weight_gate_ref[...])
    gate_ref[0] = gate
    gated = mixed_ref[0] * gate * sigmoid(gate)
    stats_ref[0, 0:1, :] = row_sums(gated * gated)
    stats_ref[0, 1:2, :] = row_sums(d_out * gain_ref[...] * gated)


def row_to_lanes(row):
    return jnp.broadcast_to(row, (LANES, row.shape[1])).T[:, 0:1]


def keep_or_send(refs, kept, value):
    if len(refs) == 1:
        refs[0][0] = value
        return

    @pl.when(kept)
    def _():
        refs[0][0] = value

    @pl.when(jnp.logical_not(kept))
    def _():
        refs[1][0] = value


def gate_back_kernel(
    order_ref,
    up_ref,
    weight_ref,
    gate_ref,
    mixed_ref,
    gain_ref,
    d_out_ref,
    stats_ref,
    low_ref,
    *refs,
):
    *branch_refs, grad_ref, grad_gate_ref, d_mixed_ref, d_gate_ref, d_gain_ref = refs[:-2]
    total, total_gate = refs[-2:]
    first = (pl.program_id(0) == 0) & (pl.program_id(1) == 0)
    last_one = pl.program_id(0) == pl.num_programs(0) - 1
    last_two = pl.program_id(1) == pl.num_programs(1) - 1

    @pl.when(first)
    def _():
        total[...] = jnp.zeros_like(total)
        total_gate[...] = jnp.zeros_like(total_gate)
        d_gain_ref[...] = jnp.zeros_like(d_gain_ref)

    stats = stats_ref[0, 0]
    for k in range(1, stats_ref.shape[0]):
        stats = stats + stats_ref[k, 0]
    squares = row_to_lanes(stats[0:1])
    products = row_to_lanes(stats[1:2])
    scale = lax.rsqrt(squares * (1.0 / DI) + NORM_EPS)
    gate = gate_ref[0]
    mixed = mixed_ref[0]
    gain = gain_ref[...]
    d_out = d_out_ref[0].astype(F32)
    sig = sigmoid(gate)
    silu = gate * sig
    gated = mixed * silu
    unit = gated * scale
    low = (unit * gain).astype(BF16)
    keep_or_send(branch_refs, pl.program_id(1) < 2, dot(low, weight_ref[...]).astype(BF16))
    total[...] += dot(low, up_ref[0], COL_COL)
    d_gain_ref[...] += jnp.sum(d_out * unit, axis=0, keepdims=True)
    d_gated = scale * (gain * d_out - unit * (scale * products * (1.0 / DI)))
    d_mixed_ref[0] = (d_gated * silu).astype(BF16)
    d_gate = (d_gated * mixed * (sig + silu * (1.0 - sig))).astype(BF16)
    d_gate_ref[0] = d_gate
    total_gate[...] += dot(low_ref[0], d_gate, COL_COL)

    @pl.when(last_one & last_two)
    def _():
        grad_ref[...] = total[...].astype(BF16)
        grad_gate_ref[...] = total_gate[...].astype(BF16)


def mixer_back_kernel(
    inner,
    first,
    table_ref,
    rest_ref,
    rim_ref,
    mixed_ref,
    d_mixed_ref,
    incoming_ref,
    taps_ref,
    heads_ref,
    skip_ref,
    low_ref,
    d_gate_ref,
    tokens_ref,
    weight_gate_ref,
    weight_rest_ref,
    after_ref,
    part_ref,
    *refs,
):
    *normed_refs, d_gain_ref, grad_ref, d_taps_ref, d_heads_ref, d_skip_ref = refs[:-6]
    padded, later, carried, d_active, total, d_rest_ref = refs[-6:]
    rows = rest_ref.shape[1]
    conv = inner + 2 * NS
    block = pl.num_programs(0) - 1 - pl.program_id(0)

    @pl.when(pl.program_id(0) == 0)
    def _():
        d_taps_ref[...] = jnp.zeros_like(d_taps_ref)
        d_heads_ref[...] = jnp.zeros_like(d_heads_ref)
        d_skip_ref[...] = jnp.zeros_like(d_skip_ref)
        d_gain_ref[...] = jnp.zeros_like(d_gain_ref)
        if first:
            total[...] = jnp.zeros_like(total)
        else:
            pltpu.sync_copy(part_ref, total)
        carried[...] = jnp.zeros_like(carried)
        later[rows : rows + RIM, :] = jnp.zeros((RIM, conv), F32)

    @pl.when(pl.program_id(0) > 0)
    def _():
        later[rows : rows + RIM, :] = later[0:RIM, :]

    rim = rim_ref[0][:, :conv]
    padded[0:RIM, :] = jnp.where(block > 0, rim, jnp.zeros_like(rim))
    padded[RIM : RIM + rows, :] = rest_ref[0][:, :conv]
    taps = taps_ref[...]
    conv_out = conv_forward(padded, taps, rows)
    sig = sigmoid(conv_out)
    active = conv_out * sig
    slope = sig + active * (1.0 - sig)
    heads = heads_ref[...]
    raw = rest_ref[0][:, conv:] + heads[0:1, :]
    step_all = softplus(raw)
    rate_all = heads[1:2, :] * step_all
    skip = skip_ref[...]
    spread = expander(inner)
    tri = lower_ones()
    upper = tri.T.astype(BF16)
    for c in reversed(range(rows // CHUNK)):
        part = slice(c * CHUNK, (c + 1) * CHUNK)
        values = active[part, :inner]
        in_b = active[part, inner : inner + NS].astype(BF16)
        out_c = active[part, inner + NS :].astype(BF16)
        step = step_all[part]
        rate = rate_all[part]
        cum, cum_t, step_x, grown, remain = decay_terms(step, rate, spread, tri)
        stepped = values * step_x
        stepped_low = stepped.astype(BF16)
        scores = dot(out_c, in_b, ROW_ROW) * tri
        d_low = d_mixed_ref[0, part, :]
        d_mixed = d_low.astype(F32)
        d_scores = jnp.zeros((CHUNK, CHUNK), F32)
        inside = []
        for pair in range(inner // LANES):
            lanes = slice(pair * LANES, (pair + 1) * LANES)
            decays, mixing = pair_mixing(cum, cum_t, scores, pair)
            d_two = side_by_side(d_low[:, lanes])
            d_mixing = dot(d_two, stepped_low[:, lanes], ROW_ROW)
            d_scores += decays[0] * d_mixing[:CHUNK] + decays[1] * d_mixing[CHUNK:]
            inside.append(dot(jnp.concatenate(mixing, axis=0), d_two, COL_COL))
        before = incoming_ref[0, c]
        ahead = carried[...]
        ahead_low = ahead.astype(BF16)
        through = remain * dot(in_b, ahead_low)
        outer = (grown * d_mixed).astype(BF16)
        d_scores_low = (d_scores * tri).astype(BF16)
        d_in_b = dot((remain * stepped).astype(BF16), ahead_low, ROW_ROW) + dot(
            d_scores_low, out_c, COL_COL
        )
        d_out_c = dot(outer, before, ROW_ROW) + dot(d_scores_low, in_b)
        d_stepped = jnp.concatenate(inside, axis=1) + through
        stepped_near = stepped_low.astype(F32)
        both = d_mixed * (mixed_ref[0, part, :] - skip * values)
        d_cum_x = both - stepped_near * d_stepped
        d_step_x = d_stepped * values
        grown_total = grown[CHUNK - 1 : CHUNK, :]
        d_total_x = jnp.sum(stepped_near * through, axis=0, keepdims=True) + grown_total * jnp.sum(
            ahead * before.astype(F32), axis=0, keepdims=True
        )
        gathered = jnp.concatenate(
            [d_cum_x, d_step_x, jnp.broadcast_to(d_total_x, (16, inner))], axis=0
        )
        narrow = sum(dot(part, spread, ROW_ROW) for part in terms(gathered, 2))
        d_rate = sum_dot(upper, narrow[:CHUNK], 2) + narrow[2 * CHUNK : 2 * CHUNK + 1]
        d_raw = (narrow[CHUNK : 2 * CHUNK] + heads[1:2, :] * d_rate) * sigmoid(raw[part])
        d_heads_ref[0:1, :] += jnp.sum(d_raw, axis=0, keepdims=True)
        d_heads_ref[1:2, :] += jnp.sum(d_rate * rate, axis=0, keepdims=True)
        d_skip_ref[...] += jnp.sum(d_mixed * values, axis=0, keepdims=True)
        d_rest_ref[part, conv:] = d_raw.astype(BF16)
        d_active[part, :inner] = d_stepped * step_x + skip * d_mixed
        d_active[part, inner : inner + NS] = d_in_b
        d_active[part, inner + NS :] = d_out_c
        carried[...] = grown_total * ahead + dot(out_c, outer, COL_COL)
    d_conv_out = d_active[...] * slope
    later[0:rows, :] = d_conv_out
    d_conv_in = jnp.zeros((rows, conv), F32)
    for k in range(KCONV):
        ahead_rows = KCONV - 1 - k
        start = RIM - (KCONV - 1) + k
        d_conv_in += taps[k : k + 1, :] * later[ahead_rows : ahead_rows + rows, :]
        d_taps_ref[k : k + 1, :] += jnp.sum(
            d_conv_out * padded[start : start + rows, :], axis=0, keepdims=True
        )
    d_taps_ref[KCONV : KCONV + 1, :] += jnp.sum(d_conv_out, axis=0, keepdims=True)
    d_rest_ref[:, :conv] = d_conv_in.astype(BF16)
    d_rest = d_rest_ref[...]
    total[...] += dot(low_ref[0], d_rest, COL_COL)
    d_normed = dot(d_gate_ref[0], weight_gate_ref[...], ROW_ROW) + dot(
        d_rest, weight_rest_ref[...], ROW_ROW
    )
    tokens = tokens_ref[0].astype(F32)
    scale = lax.rsqrt(jnp.mean(tokens * tokens, axis=1, keepdims=True) + NORM_EPS)
    d_gain_ref[...] += jnp.sum(d_normed * (tokens * scale), axis=0, keepdims=True)
    keep_or_send(normed_refs, table_ref[pl.program_id(0)] == 1, d_normed.astype(BF16))

    @pl.when(block == 0)
    def _():
        grad_ref[...] = total[...].astype(grad_ref.dtype)


def whole(shape):
    return pl.BlockSpec(shape, lambda *_: (0,) * len(shape))


def by_rows(width):
    return pl.BlockSpec((1, ROWS, width), lambda s, b, *_: (s, b, 0))


def by_order(width):
    return pl.BlockSpec((1, ROWS, width), lambda s, b, order: (s, order[b], 0))


def left_alone():
    return pl.BlockSpec(memory_space=pl.ANY)


def cost(micros):
    return pl.CostEstimate(
        flops=int(micros * 1.1e9), bytes_accessed=int(micros * 2e6), transcendentals=0
    )


def params():
    return pltpu.CompilerParams(
        vmem_limit_bytes=VMEM_BYTES
    )


def shaped(shape, dtype=F32):
    return jax.ShapeDtypeStruct(shape, dtype)


def run_forward(order, tokens, norm_gain, halves, taps, heads, skip):
    count, length, _ = tokens.shape
    inner = skip.shape[1]
    rest = halves[0].shape[1]
    conv = inner + 2 * NS
    chunks = ROWS // CHUNK
    fixed = [norm_gain, taps, heads, skip, halves[0], halves[-1]]
    return pl.pallas_call(
        functools.partial(forward_kernel, inner),
        grid_spec=pltpu.PrefetchScalarGridSpec(
            num_scalar_prefetch=1,
            grid=(count, length // ROWS),
            in_specs=[by_rows(D)] + [whole(value.shape) for value in fixed],
            out_specs=[
                by_rows(D),
                by_rows(rest),
                by_rows(inner),
                pl.BlockSpec((1, chunks, NS, inner), lambda s, b, *_: (s, b, 0, 0)),
                whole((D, rest)),
            ],
            scratch_shapes=[pltpu.VMEM((RIM + ROWS, conv), F32), pltpu.VMEM((NS, inner), F32)],
        ),
        out_shape=[
            shaped((count, length, D), BF16),
            shaped((count, length, rest)),
            shaped((count, length, inner)),
            shaped((count, length // CHUNK, NS, inner), BF16),
            shaped((D, rest), BF16),
        ],
        compiler_params=params(),
        cost_estimate=cost(1),
        name="forward_mixer",
    )(order, tokens, *fixed)


def run_stats(order, upstream, low, mixed, gate_gain, weights):
    count, length, inner = mixed.shape
    joined = len(weights) == 1
    found_specs = [whole((inner, D)), whole((D, inner))] * joined
    found_shapes = [shaped((inner, D), BF16), shaped((D, inner), BF16)] * joined
    found = pl.pallas_call(
        functools.partial(stats_kernel, joined),
        grid_spec=pltpu.PrefetchScalarGridSpec(
            num_scalar_prefetch=1,
            grid=(count, length // ROWS),
            in_specs=[by_rows(D), by_rows(D), by_rows(inner), whole((1, inner))]
            + [whole(weight.shape) for weight in weights],
            out_specs=found_specs
            + [
                by_rows(inner),
                by_rows(inner),
                pl.BlockSpec((1, 2, ROWS), lambda s, b, *_: (s, 0, b)),
            ],
        ),
        out_shape=found_shapes
        + [
            shaped((count, length, inner)),
            shaped((count, length, inner), BF16),
            shaped((count, 2, length)),
        ],
        compiler_params=params(),
        cost_estimate=cost(1),
        name="gate_stats",
    )(order, upstream, low, mixed, gate_gain, *weights)
    return found if joined else [*weights, *found]


def kept_and_sent(split, count, length, place):
    if not split:
        return [place(lambda order, b: order[b])], [shaped((count, length, D), BF16)]
    specs = [
        place(lambda order, b: jnp.minimum(b, 1)),
        place(lambda order, b: jnp.maximum(b - 2, 0)),
    ]
    return specs, [shaped((count, 2 * ROWS, D), BF16)] * 2


def run_gate_back(split, order, upstream, weight, gate, mixed, gate_gain, d_out, stats, low):
    count, length, inner = gate.shape

    def place(group):
        return pl.BlockSpec((1, ROWS, D), lambda s, b, order: (s, group(order, b), 0))

    branch_specs, branch_shapes = kept_and_sent(split, count, length, place)
    return pl.pallas_call(
        gate_back_kernel,
        grid_spec=pltpu.PrefetchScalarGridSpec(
            num_scalar_prefetch=1,
            grid=(count, length // ROWS),
            in_specs=[
                by_order(D),
                whole((inner, D)),
                by_order(inner),
                by_order(inner),
                whole((1, inner)),
                by_order(inner),
                pl.BlockSpec(
                    (stats.shape[0], 1, 2, ROWS), lambda s, b, order: (0, s, 0, order[b])
                ),
                by_order(D),
            ],
            out_specs=branch_specs
            + [
                whole((inner, D)),
                whole((D, inner)),
                by_order(inner),
                by_order(inner),
                whole((1, inner)),
            ],
            scratch_shapes=[pltpu.VMEM((inner, D), F32), pltpu.VMEM((D, inner), F32)],
        ),
        out_shape=branch_shapes
        + [
            shaped((inner, D), BF16),
            shaped((D, inner), BF16),
            shaped((count, length, inner), BF16),
            shaped((count, length, inner), BF16),
            shaped((1, inner)),
        ],
        compiler_params=params(),
        cost_estimate=cost(1),
        name="gate_back",
    )(order, upstream, weight, gate, mixed, gate_gain, d_out, stats, low)


def run_mixer_back(split, s, table, saved, fixed, weights, after, part):
    rest, mixed, d_mixed, incoming, low, d_gate, tokens = saved
    taps, heads, skip = fixed
    count, length, inner = mixed.shape
    conv = inner + 2 * NS
    last = length // ROWS - 1
    chunks = ROWS // CHUNK
    width = rest.shape[2]

    def rows(width):
        return pl.BlockSpec((1, ROWS, width), lambda b, table: (s, last - b, 0))

    if split:
        normed_specs = [
            pl.BlockSpec((1, ROWS, D), lambda b, table: (0, table[4 + b], 0)),
            pl.BlockSpec((1, ROWS, D), lambda b, table: (0, table[8 + b], 0)),
        ]
        normed_shapes = [shaped((1, 2 * ROWS, D), BF16)] * 2
    else:
        normed_specs = [pl.BlockSpec((1, ROWS, D), lambda b, table: (0, last - b, 0))]
        normed_shapes = [shaped((1, length, D), BF16)]
    return pl.pallas_call(
        functools.partial(mixer_back_kernel, inner, s == 0),
        grid_spec=pltpu.PrefetchScalarGridSpec(
            num_scalar_prefetch=1,
            grid=(length // ROWS,),
            in_specs=[
                rows(width),
                pl.BlockSpec(
                    (1, RIM, width),
                    lambda b, table: (s, jnp.maximum((last - b) * (ROWS // RIM) - 1, 0), 0),
                ),
                rows(inner),
                rows(inner),
                pl.BlockSpec((1, chunks, NS, inner), lambda b, table: (s, last - b, 0, 0)),
                whole((RIM, conv)),
                whole((8, LANES)),
                whole((1, inner)),
                rows(D),
                rows(inner),
                rows(D),
                whole((D, inner)),
                whole((D, width)),
                left_alone(),
                left_alone(),
            ],
            out_specs=normed_specs
            + [
                whole((1, D)),
                whole((D, width)),
                whole((RIM, conv)),
                whole((8, LANES)),
                whole((1, inner)),
            ],
            scratch_shapes=[
                pltpu.VMEM((RIM + ROWS, conv), F32),
                pltpu.VMEM((RIM + ROWS, conv), F32),
                pltpu.VMEM((NS, inner), F32),
                pltpu.VMEM((ROWS, conv), F32),
                pltpu.VMEM((D, width), F32),
                pltpu.VMEM((ROWS, width), BF16),
            ],
        ),
        out_shape=normed_shapes
        + [
            shaped((1, D)),
            shaped((D, width), BF16 if s == count - 1 else F32),
            shaped((RIM, conv)),
            shaped((8, LANES)),
            shaped((1, inner)),
        ],
        compiler_params=params(),
        cost_estimate=cost(1),
        name="mixer_back",
    )(table, rest, rest, mixed, d_mixed, incoming, *fixed, low, d_gate, tokens, *weights, after, part)


def swapped(value, axis, mask=1):
    count = lax.axis_size(axis)
    return lax.ppermute(value, axis, [(a, a ^ mask) for a in range(count)])


def chip_sums(parts):
    if len(parts) == 1:
        total = lax.psum_scatter(parts[0], "ctx", scatter_dimension=1, tiled=True)
        return total.astype(F32), None
    kept, sent = parts
    got = swapped(sent, "ctx", 1)
    own = kept[:, :ROWS].astype(F32) + got[:, :ROWS].astype(F32)
    return own, (kept[:, ROWS:].astype(F32) + got[:, ROWS:].astype(F32)).astype(BF16)


def across(sent):
    return [] if sent is None else [swapped(sent, "ctx", 2)]


def added(own, got):
    return own + got[0].astype(F32) if got else own


def sum_over(value, axes):
    if len(axes) == 1:
        return lax.psum(value, axes)
    for axis in axes:
        value = value + swapped(value, axis)
    return value


def by_rank(value):
    if lax.axis_size("ctx") != 4:
        return lax.all_gather(value, "ctx", axis=0)
    rank = lax.axis_index("ctx")
    near, across = swapped(value, "ctx", 1), swapped(value, "ctx", 2)
    found = [value, near, across, swapped(across, "ctx", 1)]
    odd, high = (rank & 1) == 1, rank >= 2
    found = [jnp.where(odd, found[k ^ 1], found[k]) for k in range(4)]
    return jnp.stack([jnp.where(high, found[k ^ 2], found[k]) for k in range(4)])


def to_all(value, axes):
    return lax.all_to_all(value, axes, split_axis=0, concat_axis=0, tiled=True)


def to_every(value, axes):
    times = 1
    for axis in axes:
        times = times * lax.axis_size(axis)
    return to_all(jnp.broadcast_to(value[None], (times,) + value.shape).reshape(-1, value.shape[1]), axes)


def adam_step(weight, first_old, second_old, gradient, step_rate):
    first_new = BETA_ONE * first_old + (1.0 - BETA_ONE) * gradient
    second_new = BETA_TWO * second_old + (1.0 - BETA_TWO) * gradient * gradient
    first_hat = first_new / (1.0 - BETA_ONE**STEP)
    second_hat = second_new / (1.0 - BETA_TWO**STEP)
    weight_new = weight - step_rate * (
        first_hat / (jnp.sqrt(second_hat) + ADAM_EPS) + DECAY_WEIGHT * weight
    )
    return (second_new, weight_new)


def pad_lanes(value, width):
    return jnp.pad(value, [(0, 0)] * (value.ndim - 1) + [(0, width - value.shape[-1])])


def shards(
    dp,
    block_in,
    out_grad,
    w_in,
    w_in_m,
    w_in_v,
    w_out,
    w_out_m,
    w_out_v,
    small_params,
    small_m,
    small_v,
):
    axes = dp + ("ctx",)
    n_dp, n_ctx = lax.axis_size(dp), lax.axis_size("ctx")
    rank = lax.axis_index("ctx")
    heads = HEADS // n_ctx
    inner = heads * HD
    conv = inner + 2 * NS
    count = block_in.shape[0]

    moves = []
    for block in range(n_dp * n_ctx):
        moves.append((block, (block % n_dp) * n_ctx + block // n_dp))
    mine_out = lax.ppermute(w_out.astype(BF16), axes, moves)
    offset = 0
    pieces = []
    for amount in (D, DI, KCONV * CHANNELS, CHANNELS, HEADS, HEADS, HEADS):
        pieces.append(small_params[offset : offset + amount])
        offset = offset + amount
    norm_gain = pieces[0].reshape(1, D)
    gate_gain = lax.dynamic_slice(pieces[1], (rank * inner,), (inner,)).reshape(1, inner)
    taps_all = jnp.concatenate([pieces[2].reshape(KCONV, CHANNELS), pieces[3][None]], axis=0)
    taps = jnp.concatenate(
        [lax.dynamic_slice(taps_all, (0, rank * inner), (KCONV + 1, inner)), taps_all[:, DI:]],
        axis=1,
    )
    taps = jnp.pad(taps, ((0, RIM - KCONV - 1), (0, 0)))
    dt_bias = lax.dynamic_slice(pieces[4], (rank * heads,), (heads,))
    decay = -jnp.exp(lax.dynamic_slice(pieces[5], (rank * heads,), (heads,)))
    head_rows = jnp.pad(jnp.stack([dt_bias, decay]), ((0, 6), (0, LANES - heads)))
    skip = jnp.repeat(lax.dynamic_slice(pieces[6], (rank * heads,), (heads,)), HD).reshape(1, inner)

    split = n_ctx == 4 and block_in.shape[1] == ROWS
    order = jnp.arange(n_ctx * block_in.shape[1] // ROWS, dtype=jnp.int32)
    if split:
        order = rank.astype(jnp.int32) ^ jnp.array([0, 2, 1, 3], jnp.int32)
    high = lax.axis_index(dp[0]) if len(dp) > 1 else rank * 0
    high = high.astype(jnp.int32).reshape(1)
    table = jnp.zeros((12,), jnp.int32)
    if split:
        masks = rank.astype(jnp.int32) ^ jnp.array([3, 2, 1, 0], jnp.int32)
        kept = 1 - (masks & 1)
        places = masks >> 1
        early, late = places[jnp.array([0, 0, 2, 2])], places[jnp.array([1, 1, 1, 3])]
        one_first = kept[0] == 1
        table = jnp.concatenate(
            [kept, jnp.where(one_first, early, late), jnp.where(one_first, late, early)]
        )
    tokens = lax.all_gather(block_in, "ctx", axis=1, tiled=True)
    upstream = lax.all_gather(out_grad, "ctx", axis=1, tiled=True)
    w_in_low = w_in.astype(BF16)
    slices = []
    for r in range(n_ctx):
        first = DI + CHANNELS + r * heads
        slices.append(
            jnp.concatenate(
                [
                    w_in_low[:, DI + r * inner : DI + (r + 1) * inner],
                    w_in_low[:, 2 * DI : 2 * DI + 2 * NS],
                    pad_lanes(w_in_low[:, first : first + heads], LANES),
                    w_in_low[:, r * inner : (r + 1) * inner],
                ],
                axis=1,
            )
        )
    rest = conv + LANES
    sent = jnp.concatenate(slices, axis=0)
    mine_in = to_all(sent, "ctx")
    mine_rest = mine_in[:, :rest]
    if len(dp) > 1:
        columns = [mine_out[:, k * inner : (k + 1) * inner] for k in range(D // inner)]
        mine_both = jnp.concatenate([mine_in[:, rest:]] + columns, axis=0)
        other_rest = swapped(mine_rest, dp[0])
        other_both = swapped(mine_both, dp[0])
        mine_rest, mine_out = lax.optimization_barrier((mine_rest, mine_out))
        first_half = to_every(mine_rest, dp[1:])
        other_rest, taps, head_rows, skip, norm_gain, gate_gain, order, high, table = (
            lax.optimization_barrier(
                (other_rest, taps, head_rows, skip, norm_gain, gate_gain, order, high, table)
            )
        )
        weight_halves = [first_half, to_every(other_rest, dp[1:])]
        both = jnp.concatenate([mine_both, other_both], axis=0)
        both, *weight_halves = lax.optimization_barrier((both, *weight_halves))
        weights = [to_every(both, dp[1:])]
    else:
        weight_halves = [lax.all_gather(mine_rest, dp, axis=0, tiled=True)]
        weights = [
            lax.all_gather(value, dp, axis=0, tiled=True)
            for value in (mine_out, mine_in[:, rest:])
        ]

    low, rest, mixed, incoming, weight_rest = run_forward(
        high, tokens, norm_gain, weight_halves, taps, head_rows, skip
    )
    weight_out, weight_gate, gate, d_out, stats = run_stats(
        high, upstream, low, mixed, gate_gain, weights
    )
    stats = lax.all_gather(stats, "ctx")
    *branch, grad_out, grad_gate, d_mixed, d_gate, d_gate_gain = run_gate_back(
        split, order, upstream, weight_out, gate, mixed, gate_gain, d_out, stats, low
    )
    grad_out = to_all(grad_out, dp)
    branch, branch_sent = chip_sums(branch)

    own_rows = w_in.shape[0]

    def summed(got):
        return jnp.sum(got.astype(F32).reshape(-1, n_ctx, own_rows, got.shape[1]), axis=0)

    after = grad_gate if branch_sent is None else branch_sent
    branch_got = across(branch_sent)
    saved = (rest, mixed, d_mixed, incoming, low, d_gate, tokens)
    fixed = (taps, head_rows, skip)
    weights = (weight_gate, weight_rest)
    grad_rest = after
    smalls = []
    owns = []
    normeds = []
    for s in range(count):
        found = run_mixer_back(split, s, table, saved, fixed, weights, after, grad_rest)
        *d_normed, d_gain, grad_rest, d_taps, d_heads, d_skip = found
        smalls.append([d_gain, d_taps, d_heads, d_skip])
        if s == 0:
            grad_out, branch_got, d_normed = lax.optimization_barrier(
                (grad_out, branch_got, d_normed)
            )
        else:
            grad_gate, normeds, d_normed = lax.optimization_barrier((grad_gate, normeds, d_normed))
        own, normed_sent = chip_sums(d_normed)
        after = own if normed_sent is None else normed_sent
        if s == 0:
            grad_gate, after = lax.optimization_barrier((grad_gate, after))
            grad_gate = to_all(grad_gate, axes)
        owns.append(own)
        normeds.append(across(normed_sent))
    d_norm_gain, d_taps, d_heads, d_skip = (sum(parts) for parts in zip(*smalls))
    parts = (
        d_norm_gain.reshape(-1),
        d_gate_gain.reshape(-1),
        d_taps[: KCONV + 1].reshape(-1),
        d_heads[0, :heads],
        d_heads[1, :heads],
        jnp.sum(d_skip.reshape(heads, HD), axis=1),
    )
    mine = jnp.concatenate(parts)
    mine = jnp.pad(mine, (0, -mine.shape[0] % (8 * LANES))).reshape(-1, LANES)
    every = by_rank(sum_over(mine, dp)).reshape(n_ctx, -1)
    grad_rest, every, normeds = lax.optimization_barrier((grad_rest, every, normeds))
    grad_rest = to_all(grad_rest, axes)
    d_normed = jnp.concatenate([added(own, got) for own, got in zip(owns, normeds)], axis=0)
    branch = added(branch, branch_got)
    grad_out = jnp.sum(grad_out.astype(F32).reshape(n_dp, -1, D), axis=0)
    grad_out = lax.ppermute(grad_out, axes, [(b, a) for a, b in moves])
    grad_gate = summed(grad_gate)
    grad_rest = summed(grad_rest)
    columns = [grad_gate[r] for r in range(n_ctx)]
    columns += [grad_rest[r, :, :inner] for r in range(n_ctx)]
    columns += [jnp.sum(grad_rest[:, :, inner:conv], axis=0)]
    columns += [grad_rest[r, :, conv : conv + heads] for r in range(n_ctx)]
    grad_in = jnp.concatenate(columns, axis=1)

    offset = 0
    found = []
    for part in parts:
        found.append(every[:, offset : offset + part.shape[0]])
        offset = offset + part.shape[0]
    taps_found = found[2].reshape(n_ctx, KCONV + 1, conv)
    taps_found = jnp.concatenate(
        [
            jnp.swapaxes(taps_found[:, :, :inner], 0, 1).reshape(KCONV + 1, DI),
            jnp.sum(taps_found[:, :, inner:], axis=0),
        ],
        axis=1,
    )
    grad_small = jnp.concatenate(
        [jnp.sum(found[0], axis=0), found[1].reshape(-1), taps_found.reshape(-1)]
        + [found[k].reshape(-1) for k in (3, 4, 5)]
    )

    own = block_in.astype(F32)
    block_out = (own + branch.astype(F32)).astype(BF16)
    scale = lax.rsqrt(jnp.mean(own * own, axis=-1, keepdims=True) + NORM_EPS)
    d_scaled = d_normed * norm_gain
    d_own = scale * (
        d_scaled - own * scale * scale * jnp.mean(d_scaled * own, axis=-1, keepdims=True)
    )
    input_grad = (out_grad.astype(F32) + d_own).astype(BF16)
    in_second, in_new = adam_step(w_in, w_in_m, w_in_v, grad_in, RATE_BIG)
    out_second, out_new = adam_step(w_out, w_out_m, w_out_v, grad_out, RATE_BIG)
    small_second, small_updated = adam_step(small_params, small_m, small_v, grad_small, RATE_SMALL)
    return (
        block_out,
        input_grad,
        grad_in,
        in_second,
        in_new,
        grad_out,
        out_second,
        out_new,
        grad_small,
        small_second,
        small_updated,
    )


def solution(mesh):
    dp = ("dp",)
    if mesh.shape["dp"] == 8 and mesh.shape["ctx"] == 4:
        dp = ("high", "low", "side")
        mesh = Mesh(np.asarray(mesh.devices).reshape(2, 2, 2, 4), dp + ("ctx",))
    rows = P(dp + ("ctx",), None)
    spread = P(dp, "ctx", None)
    return jax.shard_map(
        functools.partial(shards, dp),
        mesh=mesh,
        in_specs=(spread, spread) + (rows,) * 6 + (P(),) * 3,
        out_specs=(spread, spread) + (rows,) * 6 + (P(),) * 3,
        check_vma=False,
    )
```

```python
import functools

import jax
import jax.numpy as jnp
import numpy as np
from jax import lax
from jax.experimental import pallas as pl
from jax.experimental.pallas import tpu as pltpu
from jax.sharding import Mesh
from jax.sharding import PartitionSpec as P

D = 1024
HEADS = 32
HD = 64
NS = 128
KCONV = 4
STEP = 10
DI = 2048
CHANNELS = DI + 2 * NS

CHUNK = 128
LANES = 128
RIM = 8
ROWS = 256
TALL = 512

NORM_EPS = 1e-05
ADAM_EPS = 1e-08
BETA_ONE = 0.9
BETA_TWO = 0.999
RATE_BIG = 0.03
RATE_SMALL = 0.3
DECAY_WEIGHT = 0.01

F32 = jnp.float32
BF16 = jnp.bfloat16
VMEM_BYTES = 60 * 1024 * 1024


def dot(a, b, contract=((1,), (0,))):
    return lax.dot_general(a, b, (contract, ((), ())), preferred_element_type=F32)


def terms(a, count):
    parts = []
    for _ in range(count):
        part = a.astype(BF16)
        parts.append(part)
        a = a - part.astype(F32)
    return parts


def spread_dot(a, spread):
    return dot(
        jnp.concatenate(terms(a, 2), axis=1), jnp.concatenate([spread, spread], axis=0)
    )


def sum_dot(ones, a, count):
    return sum(dot(ones, part) for part in terms(a, count))


ROW_ROW = ((1,), (1,))
COL_COL = ((0,), (0,))


def sigmoid(v):
    return 1.0 / (1.0 + jnp.exp(-v))


def softplus(v):
    return jnp.maximum(v, 0.0) + jnp.log1p(jnp.exp(-jnp.abs(v)))


def expander(inner):
    head = lax.broadcasted_iota(jnp.int32, (LANES, inner), 0)
    column = lax.broadcasted_iota(jnp.int32, (LANES, inner), 1)
    inside = (column >= head * HD) & (column < (head + 1) * HD)
    return jnp.where(inside, 1.0, 0.0).astype(BF16)


def lower_ones():
    row = lax.broadcasted_iota(jnp.int32, (CHUNK, CHUNK), 0)
    column = lax.broadcasted_iota(jnp.int32, (CHUNK, CHUNK), 1)
    return jnp.where(row >= column, 1.0, 0.0)


def row_sums(a):
    lanes = a[:, :LANES]
    for start in range(LANES, a.shape[1], LANES):
        lanes = lanes + a[:, start : start + LANES]
    return jnp.sum(lanes.T, axis=0, keepdims=True)


def side_by_side(pair):
    lane = lax.broadcasted_iota(jnp.int32, pair.shape, 1)
    zero = jnp.zeros_like(pair)
    return jnp.concatenate(
        [jnp.where(lane < HD, pair, zero), jnp.where(lane < HD, zero, pair)], axis=0
    )


def decay_terms(step, rate, spread, tri):
    cum = sum_dot(tri.astype(BF16), rate, 3)
    total = cum[CHUNK - 1 : CHUNK, :]
    wide = spread_dot(
        jnp.concatenate([step, jnp.exp(cum), jnp.exp(total - cum)], axis=0), spread
    )
    return cum, cum.T, wide[:CHUNK], wide[CHUNK : 2 * CHUNK], wide[2 * CHUNK :]


def pair_mixing(cum, cum_t, scores, pair):
    decays = []
    for head in (2 * pair, 2 * pair + 1):
        differ = cum[:, head : head + 1] - cum_t[head : head + 1, :]
        decays.append(jnp.exp(jnp.minimum(differ, 0.0)))
    return decays, [(decay * scores).astype(BF16) for decay in decays]


def conv_forward(padded_ref, taps, rows):
    total = taps[KCONV : KCONV + 1, :]
    for k in range(KCONV):
        start = RIM - (KCONV - 1) + k
        total = total + taps[k : k + 1, :] * padded_ref[start : start + rows, :]
    return total


def forward_kernel(
    inner,
    order_ref,
    tokens_ref,
    gain_ref,
    taps_ref,
    heads_ref,
    skip_ref,
    mine_ref,
    other_ref,
    low_ref,
    rest_ref,
    mixed_ref,
    incoming_ref,
    weight_ref,
    padded,
    state,
):
    rows = tokens_ref.shape[1]
    conv = inner + 2 * NS

    @pl.when((pl.program_id(0) == 0) & (pl.program_id(1) == 0))
    def _():
        if mine_ref.shape[0] == D:
            weight_ref[...] = mine_ref[...]
        else:
            mine = pl.multiple_of(order_ref[0] * (D // 2), D // 2)
            other = pl.multiple_of((1 - order_ref[0]) * (D // 2), D // 2)
            weight_ref[pl.ds(mine, D // 2), :] = mine_ref[...]
            weight_ref[pl.ds(other, D // 2), :] = other_ref[...]

    @pl.when(pl.program_id(1) == 0)
    def _():
        padded[0:RIM, :] = jnp.zeros((RIM, conv), F32)
        state[...] = jnp.zeros_like(state)

    @pl.when(pl.program_id(1) > 0)
    def _():
        padded[0:RIM, :] = padded[rows : rows + RIM, :]

    tokens_low = tokens_ref[0]
    tokens = tokens_low.astype(F32)
    scale = lax.rsqrt(jnp.mean(tokens * tokens, axis=1, keepdims=True) + NORM_EPS)
    low = (tokens * scale * gain_ref[...]).astype(BF16)
    low_ref[0] = low
    projected = dot(low, weight_ref[...])
    rest_ref[0] = projected
    padded[RIM : RIM + rows, :] = projected[:, :conv]
    conv_out = conv_forward(padded, taps_ref[...], rows)
    active = conv_out * sigmoid(conv_out)
    heads = heads_ref[...]
    step_all = softplus(projected[:, conv:] + heads[0:1, :])
    rate_all = heads[1:2, :] * step_all
    skip = skip_ref[...]
    spread = expander(inner)
    tri = lower_ones()
    for c in range(rows // CHUNK):
        part = slice(c * CHUNK, (c + 1) * CHUNK)
        values = active[part, :inner]
        in_b = active[part, inner : inner + NS].astype(BF16)
        out_c = active[part, inner + NS :].astype(BF16)
        cum, cum_t, step_x, grown, remain = decay_terms(
            step_all[part], rate_all[part], spread, tri
        )
        stepped = values * step_x
        stepped_low = stepped.astype(BF16)
        scores = dot(out_c, in_b, ROW_ROW) * tri
        inside = []
        for pair in range(inner // LANES):
            lanes = slice(pair * LANES, (pair + 1) * LANES)
            _, mixing = pair_mixing(cum, cum_t, scores, pair)
            inside.append(
                dot(jnp.concatenate(mixing, axis=1), side_by_side(stepped_low[:, lanes]))
            )
        before = state[...]
        before_low = before.astype(BF16)
        incoming_ref[0, c] = before_low
        outer = grown * dot(out_c, before_low)
        mixed_ref[0, part, :] = jnp.concatenate(inside, axis=1) + outer + skip * values
        state[...] = grown[CHUNK - 1 : CHUNK, :] * before + dot(
            in_b, (remain * stepped).astype(BF16), COL_COL
        )


def stats_kernel(joined, order_ref, up_ref, low_ref, mixed_ref, gain_ref, *refs):
    if joined:
        both_ref, weight_out_ref, weight_gate_ref, gate_ref, d_out_ref, stats_ref = refs
        inner = gate_ref.shape[2]

        @pl.when((pl.program_id(0) == 0) & (pl.program_id(1) == 0))
        def _():
            deep, tall = D // 8, inner // 8
            place = 0
            for quarter in range(4):
                for half in (order_ref[0], 1 - order_ref[0]):
                    block = half * 4 + quarter
                    rows = pl.ds(pl.multiple_of(block * deep, deep), deep)
                    weight_gate_ref[rows, :] = both_ref[place : place + deep, :]
                    place = place + deep
                    rows = pl.ds(pl.multiple_of(block * tall, tall), tall)
                    for k in range(D // inner):
                        columns = slice(k * inner, (k + 1) * inner)
                        weight_out_ref[rows, columns] = both_ref[place : place + tall, :]
                        place = place + tall

    else:
        weight_out_ref, weight_gate_ref, gate_ref, d_out_ref, stats_ref = refs
    d_out = dot(up_ref[0], weight_out_ref[...], ROW_ROW)
    d_out_ref[0] = d_out.astype(BF16)
    gate = dot(low_ref[0], weight_gate_ref[...])
    gate_ref[0] = gate
    gated = mixed_ref[0] * gate * sigmoid(gate)
    stats_ref[0, 0:1, :] = row_sums(gated * gated)
    stats_ref[0, 1:2, :] = row_sums(d_out * gain_ref[...] * gated)


def row_to_lanes(row):
    return jnp.broadcast_to(row, (LANES, row.shape[1])).T[:, 0:1]


def gate_back_kernel(
    up_ref,
    weight_ref,
    gate_ref,
    mixed_ref,
    gain_ref,
    d_out_ref,
    stats_ref,
    low_ref,
    *refs,
):
    *branch_refs, grad_ref, grad_gate_ref, d_mixed_ref, d_gate_ref, d_gain_ref = refs[:-2]
    total, total_gate = refs[-2:]
    first = (pl.program_id(0) == 0) & (pl.program_id(1) == 0)
    last_one = pl.program_id(0) == pl.num_programs(0) - 1
    last_two = pl.program_id(1) == pl.num_programs(1) - 1

    @pl.when(first)
    def _():
        total[...] = jnp.zeros_like(total)
        total_gate[...] = jnp.zeros_like(total_gate)
        d_gain_ref[...] = jnp.zeros_like(d_gain_ref)

    stats = stats_ref[0, 0]
    for k in range(1, stats_ref.shape[0]):
        stats = stats + stats_ref[k, 0]
    squares = row_to_lanes(stats[0:1])
    products = row_to_lanes(stats[1:2])
    scale = lax.rsqrt(squares * (1.0 / DI) + NORM_EPS)
    gate = gate_ref[0]
    mixed = mixed_ref[0]
    gain = gain_ref[...]
    d_out = d_out_ref[0].astype(F32)
    sig = sigmoid(gate)
    silu = gate * sig
    gated = mixed * silu
    unit = gated * scale
    low = (unit * gain).astype(BF16)
    branch = dot(low, weight_ref[...]).astype(BF16)
    for s, branch_ref in enumerate(branch_refs):

        @pl.when(pl.program_id(0) == s)
        def _(branch_ref=branch_ref):
            branch_ref[0] = branch

    total[...] += dot(low, up_ref[0], COL_COL)
    d_gain_ref[...] += jnp.sum(d_out * unit, axis=0, keepdims=True)
    d_gated = scale * (gain * d_out - unit * (scale * products * (1.0 / DI)))
    d_mixed_ref[0] = (d_gated * silu).astype(BF16)
    d_gate = (d_gated * mixed * (sig + silu * (1.0 - sig))).astype(BF16)
    d_gate_ref[0] = d_gate
    total_gate[...] += dot(low_ref[0], d_gate, COL_COL)

    @pl.when(last_one & last_two)
    def _():
        grad_ref[...] = total[...].astype(BF16)
        grad_gate_ref[...] = total_gate[...].astype(BF16)


def mixer_back_kernel(
    inner,
    first,
    rest_ref,
    rim_ref,
    mixed_ref,
    d_mixed_ref,
    incoming_ref,
    taps_ref,
    heads_ref,
    skip_ref,
    low_ref,
    d_gate_ref,
    tokens_ref,
    weight_gate_ref,
    weight_rest_ref,
    after_ref,
    part_ref,
    d_normed_ref,
    d_gain_ref,
    grad_ref,
    d_taps_ref,
    d_heads_ref,
    d_skip_ref,
    padded,
    later,
    carried,
    d_active,
    total,
    d_rest_ref,
):
    rows = rest_ref.shape[1]
    conv = inner + 2 * NS
    block = pl.num_programs(0) - 1 - pl.program_id(0)

    @pl.when(pl.program_id(0) == 0)
    def _():
        d_taps_ref[...] = jnp.zeros_like(d_taps_ref)
        d_heads_ref[...] = jnp.zeros_like(d_heads_ref)
        d_skip_ref[...] = jnp.zeros_like(d_skip_ref)
        d_gain_ref[...] = jnp.zeros_like(d_gain_ref)
        if first:
            total[...] = jnp.zeros_like(total)
        else:
            pltpu.sync_copy(part_ref, total)
        carried[...] = jnp.zeros_like(carried)
        later[rows : rows + RIM, :] = jnp.zeros((RIM, conv), F32)

    @pl.when(pl.program_id(0) > 0)
    def _():
        later[rows : rows + RIM, :] = later[0:RIM, :]

    rim = rim_ref[0][:, :conv]
    padded[0:RIM, :] = jnp.where(block > 0, rim, jnp.zeros_like(rim))
    padded[RIM : RIM + rows, :] = rest_ref[0][:, :conv]
    taps = taps_ref[...]
    conv_out = conv_forward(padded, taps, rows)
    sig = sigmoid(conv_out)
    active = conv_out * sig
    slope = sig + active * (1.0 - sig)
    heads = heads_ref[...]
    raw = rest_ref[0][:, conv:] + heads[0:1, :]
    step_all = softplus(raw)
    rate_all = heads[1:2, :] * step_all
    skip = skip_ref[...]
    spread = expander(inner)
    tri = lower_ones()
    upper = tri.T.astype(BF16)
    for c in reversed(range(rows // CHUNK)):
        part = slice(c * CHUNK, (c + 1) * CHUNK)
        values = active[part, :inner]
        in_b = active[part, inner : inner + NS].astype(BF16)
        out_c = active[part, inner + NS :].astype(BF16)
        step = step_all[part]
        rate = rate_all[part]
        cum, cum_t, step_x, grown, remain = decay_terms(step, rate, spread, tri)
        stepped = values * step_x
        stepped_low = stepped.astype(BF16)
        scores = dot(out_c, in_b, ROW_ROW) * tri
        d_low = d_mixed_ref[0, part, :]
        d_mixed = d_low.astype(F32)
        d_scores = jnp.zeros((CHUNK, CHUNK), F32)
        inside = []
        for pair in range(inner // LANES):
            lanes = slice(pair * LANES, (pair + 1) * LANES)
            decays, mixing = pair_mixing(cum, cum_t, scores, pair)
            d_two = side_by_side(d_low[:, lanes])
            d_mixing = dot(d_two, stepped_low[:, lanes], ROW_ROW)
            d_scores += decays[0] * d_mixing[:CHUNK] + decays[1] * d_mixing[CHUNK:]
            inside.append(dot(jnp.concatenate(mixing, axis=0), d_two, COL_COL))
        before = incoming_ref[0, c]
        ahead = carried[...]
        ahead_low = ahead.astype(BF16)
        through = remain * dot(in_b, ahead_low)
        outer = (grown * d_mixed).astype(BF16)
        d_scores_low = (d_scores * tri).astype(BF16)
        d_in_b = dot((remain * stepped).astype(BF16), ahead_low, ROW_ROW) + dot(
            d_scores_low, out_c, COL_COL
        )
        d_out_c = dot(outer, before, ROW_ROW) + dot(d_scores_low, in_b)
        d_stepped = jnp.concatenate(inside, axis=1) + through
        stepped_near = stepped_low.astype(F32)
        both = d_mixed * (mixed_ref[0, part, :] - skip * values)
        d_cum_x = both - stepped_near * d_stepped
        d_step_x = d_stepped * values
        grown_total = grown[CHUNK - 1 : CHUNK, :]
        d_total_x = jnp.sum(stepped_near * through, axis=0, keepdims=True) + grown_total * jnp.sum(
            ahead * before.astype(F32), axis=0, keepdims=True
        )
        gathered = jnp.concatenate(
            [d_cum_x, d_step_x, jnp.broadcast_to(d_total_x, (16, inner))], axis=0
        )
        narrow = sum(dot(part, spread, ROW_ROW) for part in terms(gathered, 2))
        d_rate = sum_dot(upper, narrow[:CHUNK], 2) + narrow[2 * CHUNK : 2 * CHUNK + 1]
        d_raw = (narrow[CHUNK : 2 * CHUNK] + heads[1:2, :] * d_rate) * sigmoid(raw[part])
        d_heads_ref[0:1, :] += jnp.sum(d_raw, axis=0, keepdims=True)
        d_heads_ref[1:2, :] += jnp.sum(d_rate * rate, axis=0, keepdims=True)
        d_skip_ref[...] += jnp.sum(d_mixed * values, axis=0, keepdims=True)
        d_rest_ref[part, conv:] = d_raw.astype(BF16)
        d_active[part, :inner] = d_stepped * step_x + skip * d_mixed
        d_active[part, inner : inner + NS] = d_in_b
        d_active[part, inner + NS :] = d_out_c
        carried[...] = grown_total * ahead + dot(out_c, outer, COL_COL)
    d_conv_out = d_active[...] * slope
    later[0:rows, :] = d_conv_out
    d_conv_in = jnp.zeros((rows, conv), F32)
    for k in range(KCONV):
        ahead_rows = KCONV - 1 - k
        start = RIM - (KCONV - 1) + k
        d_conv_in += taps[k : k + 1, :] * later[ahead_rows : ahead_rows + rows, :]
        d_taps_ref[k : k + 1, :] += jnp.sum(
            d_conv_out * padded[start : start + rows, :], axis=0, keepdims=True
        )
    d_taps_ref[KCONV : KCONV + 1, :] += jnp.sum(d_conv_out, axis=0, keepdims=True)
    d_rest_ref[:, :conv] = d_conv_in.astype(BF16)
    d_rest = d_rest_ref[...]
    total[...] += dot(low_ref[0], d_rest, COL_COL)
    d_normed = dot(d_gate_ref[0], weight_gate_ref[...], ROW_ROW) + dot(
        d_rest, weight_rest_ref[...], ROW_ROW
    )
    tokens = tokens_ref[0].astype(F32)
    scale = lax.rsqrt(jnp.mean(tokens * tokens, axis=1, keepdims=True) + NORM_EPS)
    d_gain_ref[...] += jnp.sum(d_normed * (tokens * scale), axis=0, keepdims=True)
    d_normed_ref[0] = d_normed.astype(BF16)

    @pl.when(block == 0)
    def _():
        grad_ref[...] = total[...].astype(grad_ref.dtype)


def whole(shape):
    return pl.BlockSpec(shape, lambda *_: (0,) * len(shape))


def by_rows(width, rows=ROWS):
    return pl.BlockSpec((1, rows, width), lambda s, b, *_: (s, b, 0))


def left_alone():
    return pl.BlockSpec(memory_space=pl.ANY)


def cost(micros):
    return pl.CostEstimate(
        flops=int(micros * 1.1e9), bytes_accessed=int(micros * 2e6), transcendentals=0
    )


def params():
    return pltpu.CompilerParams(
        vmem_limit_bytes=VMEM_BYTES
    )


def shaped(shape, dtype=F32):
    return jax.ShapeDtypeStruct(shape, dtype)


def run_forward(order, tokens, norm_gain, halves, taps, heads, skip):
    count, length, _ = tokens.shape
    inner = skip.shape[1]
    rest = halves[0].shape[1]
    conv = inner + 2 * NS
    chunks = ROWS // CHUNK
    fixed = [norm_gain, taps, heads, skip, halves[0], halves[-1]]
    return pl.pallas_call(
        functools.partial(forward_kernel, inner),
        grid_spec=pltpu.PrefetchScalarGridSpec(
            num_scalar_prefetch=1,
            grid=(count, length // ROWS),
            in_specs=[by_rows(D)] + [whole(value.shape) for value in fixed],
            out_specs=[
                by_rows(D),
                by_rows(rest),
                by_rows(inner),
                pl.BlockSpec((1, chunks, NS, inner), lambda s, b, *_: (s, b, 0, 0)),
                whole((D, rest)),
            ],
            scratch_shapes=[pltpu.VMEM((RIM + ROWS, conv), F32), pltpu.VMEM((NS, inner), F32)],
        ),
        out_shape=[
            shaped((count, length, D), BF16),
            shaped((count, length, rest)),
            shaped((count, length, inner)),
            shaped((count, length // CHUNK, NS, inner), BF16),
            shaped((D, rest), BF16),
        ],
        compiler_params=params(),
        cost_estimate=cost(1),
        name="forward_mixer",
    )(order, tokens, *fixed)


def run_stats(order, upstream, low, mixed, gate_gain, weights):
    count, length, inner = mixed.shape
    joined = len(weights) == 1
    found_specs = [whole((inner, D)), whole((D, inner))] * joined
    found_shapes = [shaped((inner, D), BF16), shaped((D, inner), BF16)] * joined
    found = pl.pallas_call(
        functools.partial(stats_kernel, joined),
        grid_spec=pltpu.PrefetchScalarGridSpec(
            num_scalar_prefetch=1,
            grid=(count, length // TALL),
            in_specs=[by_rows(D, TALL), by_rows(D, TALL), by_rows(inner, TALL), whole((1, inner))]
            + [whole(weight.shape) for weight in weights],
            out_specs=found_specs
            + [
                by_rows(inner, TALL),
                by_rows(inner, TALL),
                pl.BlockSpec((1, 2, TALL), lambda s, b, *_: (s, 0, b)),
            ],
        ),
        out_shape=found_shapes
        + [
            shaped((count, length, inner)),
            shaped((count, length, inner), BF16),
            shaped((count, 2, length)),
        ],
        compiler_params=params(),
        cost_estimate=cost(1),
        name="gate_stats",
    )(order, upstream, low, mixed, gate_gain, *weights)
    return found if joined else [*weights, *found]


def run_gate_back(upstream, weight, gate, mixed, gate_gain, d_out, stats, low):
    count, length, inner = gate.shape
    last = length // TALL - 1

    def branch_rows(own):
        def place(s, b):
            return (0, jnp.where(s < own, 0, jnp.where(s > own, last, b)), 0)

        return pl.BlockSpec((1, TALL, D), place)

    return pl.pallas_call(
        gate_back_kernel,
        grid=(count, length // TALL),
        in_specs=[
            by_rows(D, TALL),
            whole((inner, D)),
            by_rows(inner, TALL),
            by_rows(inner, TALL),
            whole((1, inner)),
            by_rows(inner, TALL),
            pl.BlockSpec((stats.shape[0], 1, 2, TALL), lambda s, b: (0, s, 0, b)),
            by_rows(D, TALL),
        ],
        out_specs=[branch_rows(s) for s in range(count)]
        + [
            whole((inner, D)),
            whole((D, inner)),
            by_rows(inner, TALL),
            by_rows(inner, TALL),
            whole((1, inner)),
        ],
        out_shape=[shaped((1, length, D), BF16)] * count
        + [
            shaped((inner, D), BF16),
            shaped((D, inner), BF16),
            shaped((count, length, inner), BF16),
            shaped((count, length, inner), BF16),
            shaped((1, inner)),
        ],
        scratch_shapes=[pltpu.VMEM((inner, D), F32), pltpu.VMEM((D, inner), F32)],
        compiler_params=params(),
        cost_estimate=cost(1),
        name="gate_back",
    )(upstream, weight, gate, mixed, gate_gain, d_out, stats, low)


def run_mixer_back(s, saved, fixed, weights, after, part):
    rest, mixed, d_mixed, incoming, low, d_gate, tokens = saved
    taps, heads, skip = fixed
    count, length, inner = mixed.shape
    conv = inner + 2 * NS
    last = length // ROWS - 1
    chunks = ROWS // CHUNK
    width = rest.shape[2]

    def rows(width):
        return pl.BlockSpec((1, ROWS, width), lambda b: (s, last - b, 0))

    return pl.pallas_call(
        functools.partial(mixer_back_kernel, inner, s == 0),
        grid=(length // ROWS,),
        in_specs=[
            rows(width),
            pl.BlockSpec(
                (1, RIM, width),
                lambda b: (s, jnp.maximum((last - b) * (ROWS // RIM) - 1, 0), 0),
            ),
            rows(inner),
            rows(inner),
            pl.BlockSpec((1, chunks, NS, inner), lambda b: (s, last - b, 0, 0)),
            whole((RIM, conv)),
            whole((8, LANES)),
            whole((1, inner)),
            rows(D),
            rows(inner),
            rows(D),
            whole((D, inner)),
            whole((D, width)),
            left_alone(),
            left_alone(),
        ],
        out_specs=[
            pl.BlockSpec((1, ROWS, D), lambda b: (0, last - b, 0)),
            whole((1, D)),
            whole((D, width)),
            whole((RIM, conv)),
            whole((8, LANES)),
            whole((1, inner)),
        ],
        out_shape=[
            shaped((1, length, D), BF16),
            shaped((1, D)),
            shaped((D, width), BF16 if s == count - 1 else F32),
            shaped((RIM, conv)),
            shaped((8, LANES)),
            shaped((1, inner)),
        ],
        scratch_shapes=[
            pltpu.VMEM((RIM + ROWS, conv), F32),
            pltpu.VMEM((RIM + ROWS, conv), F32),
            pltpu.VMEM((NS, inner), F32),
            pltpu.VMEM((ROWS, conv), F32),
            pltpu.VMEM((D, width), F32),
            pltpu.VMEM((ROWS, width), BF16),
        ],
        compiler_params=params(),
        cost_estimate=cost(1),
        name="mixer_back",
    )(rest, rest, mixed, d_mixed, incoming, *fixed, low, d_gate, tokens, *weights, after, part)


def swapped(value, axis, mask=1):
    count = lax.axis_size(axis)
    return lax.ppermute(value, axis, [(a, a ^ mask) for a in range(count)])


def summed_over_ctx(value):
    return lax.psum_scatter(value, "ctx", scatter_dimension=1, tiled=True)


def sum_over(value, axes):
    if len(axes) == 1:
        return lax.psum(value, axes)
    for axis in axes:
        value = value + swapped(value, axis)
    return value


def by_rank(value):
    if lax.axis_size("ctx") != 4:
        return lax.all_gather(value, "ctx", axis=0)
    rank = lax.axis_index("ctx")
    near, across = swapped(value, "ctx", 1), swapped(value, "ctx", 2)
    found = [value, near, across, swapped(across, "ctx", 1)]
    odd, high = (rank & 1) == 1, rank >= 2
    found = [jnp.where(odd, found[k ^ 1], found[k]) for k in range(4)]
    return jnp.stack([jnp.where(high, found[k ^ 2], found[k]) for k in range(4)])


def to_all(value, axes):
    return lax.all_to_all(value, axes, split_axis=0, concat_axis=0, tiled=True)


def to_every(value, axes):
    times = 1
    for axis in axes:
        times = times * lax.axis_size(axis)
    return to_all(jnp.broadcast_to(value[None], (times,) + value.shape).reshape(-1, value.shape[1]), axes)


def adam_step(weight, first_old, second_old, gradient, step_rate):
    first_new = BETA_ONE * first_old + (1.0 - BETA_ONE) * gradient
    second_new = BETA_TWO * second_old + (1.0 - BETA_TWO) * gradient * gradient
    first_hat = first_new / (1.0 - BETA_ONE**STEP)
    second_hat = second_new / (1.0 - BETA_TWO**STEP)
    weight_new = weight - step_rate * (
        first_hat / (jnp.sqrt(second_hat) + ADAM_EPS) + DECAY_WEIGHT * weight
    )
    return (second_new, weight_new)


def pad_lanes(value, width):
    return jnp.pad(value, [(0, 0)] * (value.ndim - 1) + [(0, width - value.shape[-1])])


def shards(
    dp,
    block_in,
    out_grad,
    w_in,
    w_in_m,
    w_in_v,
    w_out,
    w_out_m,
    w_out_v,
    small_params,
    small_m,
    small_v,
):
    axes = dp + ("ctx",)
    n_dp, n_ctx = lax.axis_size(dp), lax.axis_size("ctx")
    rank = lax.axis_index("ctx")
    heads = HEADS // n_ctx
    inner = heads * HD
    conv = inner + 2 * NS
    count = block_in.shape[0]

    moves = []
    for block in range(n_dp * n_ctx):
        moves.append((block, (block % n_dp) * n_ctx + block // n_dp))
    mine_out = lax.ppermute(w_out.astype(BF16), axes, moves)
    offset = 0
    pieces = []
    for amount in (D, DI, KCONV * CHANNELS, CHANNELS, HEADS, HEADS, HEADS):
        pieces.append(small_params[offset : offset + amount])
        offset = offset + amount
    norm_gain = pieces[0].reshape(1, D)
    gate_gain = lax.dynamic_slice(pieces[1], (rank * inner,), (inner,)).reshape(1, inner)
    taps_all = jnp.concatenate([pieces[2].reshape(KCONV, CHANNELS), pieces[3][None]], axis=0)
    taps = jnp.concatenate(
        [lax.dynamic_slice(taps_all, (0, rank * inner), (KCONV + 1, inner)), taps_all[:, DI:]],
        axis=1,
    )
    taps = jnp.pad(taps, ((0, RIM - KCONV - 1), (0, 0)))
    dt_bias = lax.dynamic_slice(pieces[4], (rank * heads,), (heads,))
    decay = -jnp.exp(lax.dynamic_slice(pieces[5], (rank * heads,), (heads,)))
    head_rows = jnp.pad(jnp.stack([dt_bias, decay]), ((0, 6), (0, LANES - heads)))
    skip = jnp.repeat(lax.dynamic_slice(pieces[6], (rank * heads,), (heads,)), HD).reshape(1, inner)

    high = lax.axis_index(dp[0]) if len(dp) > 1 else rank * 0
    high = high.astype(jnp.int32).reshape(1)
    tokens = lax.all_gather(block_in, "ctx", axis=1, tiled=True)
    upstream = lax.all_gather(out_grad, "ctx", axis=1, tiled=True)
    w_in_low = w_in.astype(BF16)
    slices = []
    for r in range(n_ctx):
        first = DI + CHANNELS + r * heads
        slices.append(
            jnp.concatenate(
                [
                    w_in_low[:, DI + r * inner : DI + (r + 1) * inner],
                    w_in_low[:, 2 * DI : 2 * DI + 2 * NS],
                    pad_lanes(w_in_low[:, first : first + heads], LANES),
                    w_in_low[:, r * inner : (r + 1) * inner],
                ],
                axis=1,
            )
        )
    rest = conv + LANES
    sent = jnp.concatenate(slices, axis=0)
    mine_in = to_all(sent, "ctx")
    mine_rest = mine_in[:, :rest]
    if len(dp) > 1:
        columns = [mine_out[:, k * inner : (k + 1) * inner] for k in range(D // inner)]
        mine_both = jnp.concatenate([mine_in[:, rest:]] + columns, axis=0)
        other_rest = swapped(mine_rest, dp[0])
        other_both = swapped(mine_both, dp[0])
        mine_rest, mine_out = lax.optimization_barrier((mine_rest, mine_out))
        first_half = to_every(mine_rest, dp[1:])
        other_rest, taps, head_rows, skip, norm_gain, gate_gain, high = lax.optimization_barrier(
            (other_rest, taps, head_rows, skip, norm_gain, gate_gain, high)
        )
        weight_halves = [first_half, to_every(other_rest, dp[1:])]
        both = jnp.concatenate([mine_both, other_both], axis=0)
        both, *weight_halves = lax.optimization_barrier((both, *weight_halves))
        weights = [to_every(both, dp[1:])]
    else:
        weight_halves = [lax.all_gather(mine_rest, dp, axis=0, tiled=True)]
        weights = [
            lax.all_gather(value, dp, axis=0, tiled=True)
            for value in (mine_out, mine_in[:, rest:])
        ]

    low, rest, mixed, incoming, weight_rest = run_forward(
        high, tokens, norm_gain, weight_halves, taps, head_rows, skip
    )
    weight_out, weight_gate, gate, d_out, stats = run_stats(
        high, upstream, low, mixed, gate_gain, weights
    )
    stats = lax.all_gather(stats, "ctx")
    *branches, grad_out, grad_gate, d_mixed, d_gate, d_gate_gain = run_gate_back(
        upstream, weight_out, gate, mixed, gate_gain, d_out, stats, low
    )
    grad_out = to_all(grad_out, dp)
    branches = [summed_over_ctx(branch) for branch in branches]

    own_rows = w_in.shape[0]

    def summed(got):
        return jnp.sum(got.astype(F32).reshape(-1, n_ctx, own_rows, got.shape[1]), axis=0)

    saved = (rest, mixed, d_mixed, incoming, low, d_gate, tokens)
    fixed = (taps, head_rows, skip)
    weights = (weight_gate, weight_rest)
    after = grad_rest = d_gate
    smalls = []
    normeds = []
    for s in range(count):
        d_normed, d_gain, grad_rest, d_taps, d_heads, d_skip = run_mixer_back(
            s, saved, fixed, weights, after, grad_rest
        )
        normeds.append(summed_over_ctx(d_normed))
        branches[s], d_gain = lax.optimization_barrier((branches[s], d_gain))
        if s == 0:
            grad_gate, branches[s], d_gain, after = lax.optimization_barrier(
                (grad_gate, branches[s], d_gain, grad_out)
            )
            grad_gate = to_all(grad_gate, axes)
        else:
            grad_gate, d_gain = lax.optimization_barrier((grad_gate, d_gain))
        smalls.append([d_gain, d_taps, d_heads, d_skip])
    d_norm_gain, d_taps, d_heads, d_skip = (sum(parts) for parts in zip(*smalls))
    parts = (
        d_norm_gain.reshape(-1),
        d_gate_gain.reshape(-1),
        d_taps[: KCONV + 1].reshape(-1),
        d_heads[0, :heads],
        d_heads[1, :heads],
        jnp.sum(d_skip.reshape(heads, HD), axis=1),
    )
    mine = jnp.concatenate(parts)
    mine = jnp.pad(mine, (0, -mine.shape[0] % (8 * LANES))).reshape(-1, LANES)
    every = by_rank(sum_over(mine, dp)).reshape(n_ctx, -1)
    grad_rest, every = lax.optimization_barrier((grad_rest, every))
    grad_rest = to_all(grad_rest, axes)
    d_normed = jnp.concatenate(normeds, axis=0).astype(F32)
    grad_out = jnp.sum(grad_out.astype(F32).reshape(n_dp, -1, D), axis=0)
    grad_out = lax.ppermute(grad_out, axes, [(b, a) for a, b in moves])
    grad_gate = summed(grad_gate)
    grad_rest = summed(grad_rest)
    columns = [grad_gate[r] for r in range(n_ctx)]
    columns += [grad_rest[r, :, :inner] for r in range(n_ctx)]
    columns += [jnp.sum(grad_rest[:, :, inner:conv], axis=0)]
    columns += [grad_rest[r, :, conv : conv + heads] for r in range(n_ctx)]
    grad_in = jnp.concatenate(columns, axis=1)

    offset = 0
    found = []
    for part in parts:
        found.append(every[:, offset : offset + part.shape[0]])
        offset = offset + part.shape[0]
    taps_found = found[2].reshape(n_ctx, KCONV + 1, conv)
    taps_found = jnp.concatenate(
        [
            jnp.swapaxes(taps_found[:, :, :inner], 0, 1).reshape(KCONV + 1, DI),
            jnp.sum(taps_found[:, :, inner:], axis=0),
        ],
        axis=1,
    )
    grad_small = jnp.concatenate(
        [jnp.sum(found[0], axis=0), found[1].reshape(-1), taps_found.reshape(-1)]
        + [found[k].reshape(-1) for k in (3, 4, 5)]
    )

    own = block_in.astype(F32)
    branch = jnp.concatenate(branches, axis=0)
    block_out = (own + branch.astype(F32)).astype(BF16)
    scale = lax.rsqrt(jnp.mean(own * own, axis=-1, keepdims=True) + NORM_EPS)
    d_scaled = d_normed * norm_gain
    d_own = scale * (
        d_scaled - own * scale * scale * jnp.mean(d_scaled * own, axis=-1, keepdims=True)
    )
    input_grad = (out_grad.astype(F32) + d_own).astype(BF16)
    in_second, in_new = adam_step(w_in, w_in_m, w_in_v, grad_in, RATE_BIG)
    out_second, out_new = adam_step(w_out, w_out_m, w_out_v, grad_out, RATE_BIG)
    small_second, small_updated = adam_step(small_params, small_m, small_v, grad_small, RATE_SMALL)
    return (
        block_out,
        input_grad,
        grad_in,
        in_second,
        in_new,
        grad_out,
        out_second,
        out_new,
        grad_small,
        small_second,
        small_updated,
    )


def solution(mesh):
    dp = ("dp",)
    if mesh.shape["dp"] == 8 and mesh.shape["ctx"] == 4:
        dp = ("high", "low", "side")
        mesh = Mesh(np.asarray(mesh.devices).reshape(2, 2, 2, 4), dp + ("ctx",))
    rows = P(dp + ("ctx",), None)
    spread = P(dp, "ctx", None)
    return jax.shard_map(
        functools.partial(shards, dp),
        mesh=mesh,
        in_specs=(spread, spread) + (rows,) * 6 + (P(),) * 3,
        out_specs=(spread, spread) + (rows,) * 6 + (P(),) * 3,
        check_vma=False,
    )
```

```python
import functools

import jax
import jax.numpy as jnp
import numpy as np
from jax import lax
from jax.experimental import pallas as pl
from jax.experimental.pallas import tpu as pltpu
from jax.sharding import Mesh
from jax.sharding import PartitionSpec as P

D = 1024
HEADS = 32
HD = 64
NS = 128
KCONV = 4
STEP = 10
DI = 2048
CHANNELS = DI + 2 * NS

CHUNK = 128
LANES = 128
RIM = 8
ROWS = 256
TALL = 512

NORM_EPS = 1e-05
ADAM_EPS = 1e-08
BETA_ONE = 0.9
BETA_TWO = 0.999
RATE_BIG = 0.03
RATE_SMALL = 0.3
DECAY_WEIGHT = 0.01

F32 = jnp.float32
BF16 = jnp.bfloat16
VMEM_BYTES = 60 * 1024 * 1024


def dot(a, b, contract=((1,), (0,))):
    return lax.dot_general(a, b, (contract, ((), ())), preferred_element_type=F32)


def terms(a, count):
    parts = []
    for _ in range(count):
        part = a.astype(BF16)
        parts.append(part)
        a = a - part.astype(F32)
    return parts


def spread_dot(a, spread):
    return dot(
        jnp.concatenate(terms(a, 2), axis=1), jnp.concatenate([spread, spread], axis=0)
    )


def sum_dot(ones, a, count):
    return sum(dot(ones, part) for part in terms(a, count))


ROW_ROW = ((1,), (1,))
COL_COL = ((0,), (0,))


def sigmoid(v):
    return 1.0 / (1.0 + jnp.exp(-v))


def softplus(v):
    return jnp.maximum(v, 0.0) + jnp.log1p(jnp.exp(-jnp.abs(v)))


def expander(inner):
    head = lax.broadcasted_iota(jnp.int32, (LANES, inner), 0)
    column = lax.broadcasted_iota(jnp.int32, (LANES, inner), 1)
    inside = (column >= head * HD) & (column < (head + 1) * HD)
    return jnp.where(inside, 1.0, 0.0).astype(BF16)


def lower_ones():
    row = lax.broadcasted_iota(jnp.int32, (CHUNK, CHUNK), 0)
    column = lax.broadcasted_iota(jnp.int32, (CHUNK, CHUNK), 1)
    return jnp.where(row >= column, 1.0, 0.0)


def row_sums(a):
    lanes = a[:, :LANES]
    for start in range(LANES, a.shape[1], LANES):
        lanes = lanes + a[:, start : start + LANES]
    return jnp.sum(lanes.T, axis=0, keepdims=True)


def side_by_side(pair):
    lane = lax.broadcasted_iota(jnp.int32, pair.shape, 1)
    zero = jnp.zeros_like(pair)
    return jnp.concatenate(
        [jnp.where(lane < HD, pair, zero), jnp.where(lane < HD, zero, pair)], axis=0
    )


def decay_terms(step, rate, spread, tri):
    cum = sum_dot(tri.astype(BF16), rate, 3)
    total = cum[CHUNK - 1 : CHUNK, :]
    wide = spread_dot(
        jnp.concatenate([step, jnp.exp(cum), jnp.exp(total - cum)], axis=0), spread
    )
    return cum, cum.T, wide[:CHUNK], wide[CHUNK : 2 * CHUNK], wide[2 * CHUNK :]


def pair_mixing(cum, cum_t, scores, pair):
    decays = []
    for head in (2 * pair, 2 * pair + 1):
        differ = cum[:, head : head + 1] - cum_t[head : head + 1, :]
        decays.append(jnp.exp(jnp.minimum(differ, 0.0)))
    return decays, [(decay * scores).astype(BF16) for decay in decays]


def conv_forward(padded_ref, taps, rows):
    total = taps[KCONV : KCONV + 1, :]
    for k in range(KCONV):
        start = RIM - (KCONV - 1) + k
        total = total + taps[k : k + 1, :] * padded_ref[start : start + rows, :]
    return total


def forward_kernel(
    inner,
    order_ref,
    tokens_ref,
    gain_ref,
    taps_ref,
    heads_ref,
    skip_ref,
    mine_ref,
    other_ref,
    low_ref,
    rest_ref,
    mixed_ref,
    incoming_ref,
    weight_ref,
    padded,
    state,
):
    rows = tokens_ref.shape[1]
    conv = inner + 2 * NS

    @pl.when((pl.program_id(0) == 0) & (pl.program_id(1) == 0))
    def _():
        if mine_ref.shape[0] == D:
            weight_ref[...] = mine_ref[...]
        else:
            mine = pl.multiple_of(order_ref[0] * (D // 2), D // 2)
            other = pl.multiple_of((1 - order_ref[0]) * (D // 2), D // 2)
            weight_ref[pl.ds(mine, D // 2), :] = mine_ref[...]
            weight_ref[pl.ds(other, D // 2), :] = other_ref[...]

    @pl.when(pl.program_id(1) == 0)
    def _():
        padded[0:RIM, :] = jnp.zeros((RIM, conv), F32)
        state[...] = jnp.zeros_like(state)

    @pl.when(pl.program_id(1) > 0)
    def _():
        padded[0:RIM, :] = padded[rows : rows + RIM, :]

    tokens_low = tokens_ref[0]
    tokens = tokens_low.astype(F32)
    scale = lax.rsqrt(jnp.mean(tokens * tokens, axis=1, keepdims=True) + NORM_EPS)
    low = (tokens * scale * gain_ref[...]).astype(BF16)
    low_ref[0] = low
    projected = dot(low, weight_ref[...])
    rest_ref[0] = projected
    padded[RIM : RIM + rows, :] = projected[:, :conv]
    conv_out = conv_forward(padded, taps_ref[...], rows)
    active = conv_out * sigmoid(conv_out)
    heads = heads_ref[...]
    step_all = softplus(projected[:, conv:] + heads[0:1, :])
    rate_all = heads[1:2, :] * step_all
    skip = skip_ref[...]
    spread = expander(inner)
    tri = lower_ones()
    for c in range(rows // CHUNK):
        part = slice(c * CHUNK, (c + 1) * CHUNK)
        values = active[part, :inner]
        in_b = active[part, inner : inner + NS].astype(BF16)
        out_c = active[part, inner + NS :].astype(BF16)
        cum, cum_t, step_x, grown, remain = decay_terms(
            step_all[part], rate_all[part], spread, tri
        )
        stepped = values * step_x
        stepped_low = stepped.astype(BF16)
        scores = dot(out_c, in_b, ROW_ROW) * tri
        inside = []
        for pair in range(inner // LANES):
            lanes = slice(pair * LANES, (pair + 1) * LANES)
            _, mixing = pair_mixing(cum, cum_t, scores, pair)
            inside.append(
                dot(jnp.concatenate(mixing, axis=1), side_by_side(stepped_low[:, lanes]))
            )
        before = state[...]
        before_low = before.astype(BF16)
        incoming_ref[0, c] = before_low
        outer = grown * dot(out_c, before_low)
        mixed_ref[0, part, :] = jnp.concatenate(inside, axis=1) + outer + skip * values
        state[...] = grown[CHUNK - 1 : CHUNK, :] * before + dot(
            in_b, (remain * stepped).astype(BF16), COL_COL
        )


def stats_kernel(joined, order_ref, up_ref, low_ref, mixed_ref, gain_ref, *refs):
    if joined:
        both_ref, weight_out_ref, weight_gate_ref, gate_ref, d_out_ref, stats_ref = refs
        inner = gate_ref.shape[2]

        @pl.when((pl.program_id(0) == 0) & (pl.program_id(1) == 0))
        def _():
            deep, tall = D // 8, inner // 8
            place = 0
            for quarter in range(4):
                for half in (order_ref[0], 1 - order_ref[0]):
                    block = half * 4 + quarter
                    rows = pl.ds(pl.multiple_of(block * deep, deep), deep)
                    weight_gate_ref[rows, :] = both_ref[place : place + deep, :]
                    place = place + deep
                    rows = pl.ds(pl.multiple_of(block * tall, tall), tall)
                    for k in range(D // inner):
                        columns = slice(k * inner, (k + 1) * inner)
                        weight_out_ref[rows, columns] = both_ref[place : place + tall, :]
                        place = place + tall

    else:
        weight_out_ref, weight_gate_ref, gate_ref, d_out_ref, stats_ref = refs
    d_out = dot(up_ref[0], weight_out_ref[...], ROW_ROW)
    d_out_ref[0] = d_out.astype(BF16)
    gate = dot(low_ref[0], weight_gate_ref[...])
    gate_ref[0] = gate
    gated = mixed_ref[0] * gate * sigmoid(gate)
    stats_ref[0, 0:1, :] = row_sums(gated * gated)
    stats_ref[0, 1:2, :] = row_sums(d_out * gain_ref[...] * gated)


def row_to_lanes(row):
    return jnp.broadcast_to(row, (LANES, row.shape[1])).T[:, 0:1]


def gate_back_kernel(
    up_ref,
    weight_ref,
    gate_ref,
    mixed_ref,
    gain_ref,
    d_out_ref,
    stats_ref,
    low_ref,
    *refs,
):
    *branch_refs, grad_ref, grad_gate_ref, d_mixed_ref, d_gate_ref, d_gain_ref = refs[:-2]
    total, total_gate = refs[-2:]
    first = (pl.program_id(0) == 0) & (pl.program_id(1) == 0)
    last_one = pl.program_id(0) == pl.num_programs(0) - 1
    last_two = pl.program_id(1) == pl.num_programs(1) - 1

    @pl.when(first)
    def _():
        total[...] = jnp.zeros_like(total)
        total_gate[...] = jnp.zeros_like(total_gate)
        d_gain_ref[...] = jnp.zeros_like(d_gain_ref)

    stats = stats_ref[0, 0]
    for k in range(1, stats_ref.shape[0]):
        stats = stats + stats_ref[k, 0]
    squares = row_to_lanes(stats[0:1])
    products = row_to_lanes(stats[1:2])
    scale = lax.rsqrt(squares * (1.0 / DI) + NORM_EPS)
    gate = gate_ref[0]
    mixed = mixed_ref[0]
    gain = gain_ref[...]
    d_out = d_out_ref[0].astype(F32)
    sig = sigmoid(gate)
    silu = gate * sig
    gated = mixed * silu
    unit = gated * scale
    low = (unit * gain).astype(BF16)
    branch = dot(low, weight_ref[...]).astype(BF16)
    for s, branch_ref in enumerate(branch_refs):

        @pl.when(pl.program_id(0) == s)
        def _(branch_ref=branch_ref):
            branch_ref[0] = branch

    total[...] += dot(low, up_ref[0], COL_COL)
    d_gain_ref[...] += jnp.sum(d_out * unit, axis=0, keepdims=True)
    d_gated = scale * (gain * d_out - unit * (scale * products * (1.0 / DI)))
    d_mixed_ref[0] = (d_gated * silu).astype(BF16)
    d_gate = (d_gated * mixed * (sig + silu * (1.0 - sig))).astype(BF16)
    d_gate_ref[0] = d_gate
    total_gate[...] += dot(low_ref[0], d_gate, COL_COL)

    @pl.when(last_one & last_two)
    def _():
        grad_ref[...] = total[...].astype(BF16)
        grad_gate_ref[...] = total_gate[...].astype(BF16)


def mixer_back_kernel(
    inner,
    first,
    rest_ref,
    rim_ref,
    mixed_ref,
    d_mixed_ref,
    incoming_ref,
    taps_ref,
    heads_ref,
    skip_ref,
    low_ref,
    d_gate_ref,
    tokens_ref,
    weight_gate_ref,
    weight_rest_ref,
    after_ref,
    part_ref,
    before_ref,
    d_normed_ref,
    d_gain_ref,
    grad_ref,
    d_taps_ref,
    d_heads_ref,
    d_skip_ref,
    padded,
    later,
    carried,
    d_active,
    total,
    d_rest_ref,
):
    rows = rest_ref.shape[1]
    conv = inner + 2 * NS
    block = pl.num_programs(0) - 1 - pl.program_id(0)

    @pl.when(pl.program_id(0) == 0)
    def _():
        d_taps_ref[...] = jnp.zeros_like(d_taps_ref)
        d_heads_ref[...] = jnp.zeros_like(d_heads_ref)
        d_skip_ref[...] = jnp.zeros_like(d_skip_ref)
        d_gain_ref[...] = jnp.zeros_like(d_gain_ref)
        if first:
            total[...] = jnp.zeros_like(total)
        else:
            pltpu.sync_copy(part_ref, total)
        carried[...] = jnp.zeros_like(carried)
        later[rows : rows + RIM, :] = jnp.zeros((RIM, conv), F32)

    @pl.when(pl.program_id(0) > 0)
    def _():
        later[rows : rows + RIM, :] = later[0:RIM, :]

    rim = rim_ref[0][:, :conv]
    padded[0:RIM, :] = jnp.where(block > 0, rim, jnp.zeros_like(rim))
    padded[RIM : RIM + rows, :] = rest_ref[0][:, :conv]
    taps = taps_ref[...]
    conv_out = conv_forward(padded, taps, rows)
    sig = sigmoid(conv_out)
    active = conv_out * sig
    slope = sig + active * (1.0 - sig)
    heads = heads_ref[...]
    raw = rest_ref[0][:, conv:] + heads[0:1, :]
    step_all = softplus(raw)
    rate_all = heads[1:2, :] * step_all
    skip = skip_ref[...]
    spread = expander(inner)
    tri = lower_ones()
    upper = tri.T.astype(BF16)
    for c in reversed(range(rows // CHUNK)):
        part = slice(c * CHUNK, (c + 1) * CHUNK)
        values = active[part, :inner]
        in_b = active[part, inner : inner + NS].astype(BF16)
        out_c = active[part, inner + NS :].astype(BF16)
        step = step_all[part]
        rate = rate_all[part]
        cum, cum_t, step_x, grown, remain = decay_terms(step, rate, spread, tri)
        stepped = values * step_x
        stepped_low = stepped.astype(BF16)
        scores = dot(out_c, in_b, ROW_ROW) * tri
        d_low = d_mixed_ref[0, part, :]
        d_mixed = d_low.astype(F32)
        d_scores = jnp.zeros((CHUNK, CHUNK), F32)
        inside = []
        for pair in range(inner // LANES):
            lanes = slice(pair * LANES, (pair + 1) * LANES)
            decays, mixing = pair_mixing(cum, cum_t, scores, pair)
            d_two = side_by_side(d_low[:, lanes])
            d_mixing = dot(d_two, stepped_low[:, lanes], ROW_ROW)
            d_scores += decays[0] * d_mixing[:CHUNK] + decays[1] * d_mixing[CHUNK:]
            inside.append(dot(jnp.concatenate(mixing, axis=0), d_two, COL_COL))
        before = incoming_ref[0, c]
        ahead = carried[...]
        ahead_low = ahead.astype(BF16)
        through = remain * dot(in_b, ahead_low)
        outer = (grown * d_mixed).astype(BF16)
        d_scores_low = (d_scores * tri).astype(BF16)
        d_in_b = dot((remain * stepped).astype(BF16), ahead_low, ROW_ROW) + dot(
            d_scores_low, out_c, COL_COL
        )
        d_out_c = dot(outer, before, ROW_ROW) + dot(d_scores_low, in_b)
        d_stepped = jnp.concatenate(inside, axis=1) + through
        stepped_near = stepped_low.astype(F32)
        both = d_mixed * (mixed_ref[0, part, :] - skip * values)
        d_cum_x = both - stepped_near * d_stepped
        d_step_x = d_stepped * values
        grown_total = grown[CHUNK - 1 : CHUNK, :]
        d_total_x = jnp.sum(stepped_near * through, axis=0, keepdims=True) + grown_total * jnp.sum(
            ahead * before.astype(F32), axis=0, keepdims=True
        )
        gathered = jnp.concatenate(
            [d_cum_x, d_step_x, jnp.broadcast_to(d_total_x, (16, inner))], axis=0
        )
        narrow = sum(dot(part, spread, ROW_ROW) for part in terms(gathered, 2))
        d_rate = sum_dot(upper, narrow[:CHUNK], 2) + narrow[2 * CHUNK : 2 * CHUNK + 1]
        d_raw = (narrow[CHUNK : 2 * CHUNK] + heads[1:2, :] * d_rate) * sigmoid(raw[part])
        d_heads_ref[0:1, :] += jnp.sum(d_raw, axis=0, keepdims=True)
        d_heads_ref[1:2, :] += jnp.sum(d_rate * rate, axis=0, keepdims=True)
        d_skip_ref[...] += jnp.sum(d_mixed * values, axis=0, keepdims=True)
        d_rest_ref[part, conv:] = d_raw.astype(BF16)
        d_active[part, :inner] = d_stepped * step_x + skip * d_mixed
        d_active[part, inner : inner + NS] = d_in_b
        d_active[part, inner + NS :] = d_out_c
        carried[...] = grown_total * ahead + dot(out_c, outer, COL_COL)
    d_conv_out = d_active[...] * slope
    later[0:rows, :] = d_conv_out
    d_conv_in = jnp.zeros((rows, conv), F32)
    for k in range(KCONV):
        ahead_rows = KCONV - 1 - k
        start = RIM - (KCONV - 1) + k
        d_conv_in += taps[k : k + 1, :] * later[ahead_rows : ahead_rows + rows, :]
        d_taps_ref[k : k + 1, :] += jnp.sum(
            d_conv_out * padded[start : start + rows, :], axis=0, keepdims=True
        )
    d_taps_ref[KCONV : KCONV + 1, :] += jnp.sum(d_conv_out, axis=0, keepdims=True)
    d_rest_ref[:, :conv] = d_conv_in.astype(BF16)
    d_rest = d_rest_ref[...]
    total[...] += dot(low_ref[0], d_rest, COL_COL)
    d_normed = dot(d_gate_ref[0], weight_gate_ref[...], ROW_ROW) + dot(
        d_rest, weight_rest_ref[...], ROW_ROW
    )
    tokens = tokens_ref[0].astype(F32)
    scale = lax.rsqrt(jnp.mean(tokens * tokens, axis=1, keepdims=True) + NORM_EPS)
    d_gain_ref[...] += jnp.sum(d_normed * (tokens * scale), axis=0, keepdims=True)
    d_normed_ref[0] = d_normed.astype(BF16)

    @pl.when(block == 0)
    def _():
        grad_ref[...] = total[...].astype(grad_ref.dtype)


def whole(shape):
    return pl.BlockSpec(shape, lambda *_: (0,) * len(shape))


def by_rows(width, rows=ROWS):
    return pl.BlockSpec((1, rows, width), lambda s, b, *_: (s, b, 0))


def left_alone():
    return pl.BlockSpec(memory_space=pl.ANY)


def cost(micros):
    return pl.CostEstimate(
        flops=int(micros * 1.1e9), bytes_accessed=int(micros * 2e6), transcendentals=0
    )


def params():
    return pltpu.CompilerParams(
        vmem_limit_bytes=VMEM_BYTES
    )


def shaped(shape, dtype=F32):
    return jax.ShapeDtypeStruct(shape, dtype)


def run_forward(order, tokens, norm_gain, halves, taps, heads, skip):
    count, length, _ = tokens.shape
    inner = skip.shape[1]
    rest = halves[0].shape[1]
    conv = inner + 2 * NS
    chunks = ROWS // CHUNK
    fixed = [norm_gain, taps, heads, skip, halves[0], halves[-1]]
    return pl.pallas_call(
        functools.partial(forward_kernel, inner),
        grid_spec=pltpu.PrefetchScalarGridSpec(
            num_scalar_prefetch=1,
            grid=(count, length // ROWS),
            in_specs=[by_rows(D)] + [whole(value.shape) for value in fixed],
            out_specs=[
                by_rows(D),
                by_rows(rest),
                by_rows(inner),
                pl.BlockSpec((1, chunks, NS, inner), lambda s, b, *_: (s, b, 0, 0)),
                whole((D, rest)),
            ],
            scratch_shapes=[pltpu.VMEM((RIM + ROWS, conv), F32), pltpu.VMEM((NS, inner), F32)],
        ),
        out_shape=[
            shaped((count, length, D), BF16),
            shaped((count, length, rest)),
            shaped((count, length, inner)),
            shaped((count, length // CHUNK, NS, inner), BF16),
            shaped((D, rest), BF16),
        ],
        compiler_params=params(),
        cost_estimate=cost(1),
        name="forward_mixer",
    )(order, tokens, *fixed)


def run_stats(order, upstream, low, mixed, gate_gain, weights):
    count, length, inner = mixed.shape
    joined = len(weights) == 1
    found_specs = [whole((inner, D)), whole((D, inner))] * joined
    found_shapes = [shaped((inner, D), BF16), shaped((D, inner), BF16)] * joined
    found = pl.pallas_call(
        functools.partial(stats_kernel, joined),
        grid_spec=pltpu.PrefetchScalarGridSpec(
            num_scalar_prefetch=1,
            grid=(count, length // TALL),
            in_specs=[by_rows(D, TALL), by_rows(D, TALL), by_rows(inner, TALL), whole((1, inner))]
            + [whole(weight.shape) for weight in weights],
            out_specs=found_specs
            + [
                by_rows(inner, TALL),
                by_rows(inner, TALL),
                pl.BlockSpec((1, 2, TALL), lambda s, b, *_: (s, 0, b)),
            ],
        ),
        out_shape=found_shapes
        + [
            shaped((count, length, inner)),
            shaped((count, length, inner), BF16),
            shaped((count, 2, length)),
        ],
        compiler_params=params(),
        cost_estimate=cost(1),
        name="gate_stats",
    )(order, upstream, low, mixed, gate_gain, *weights)
    return found if joined else [*weights, *found]


def run_gate_back(upstream, weight, gate, mixed, gate_gain, d_out, stats, low):
    count, length, inner = gate.shape
    last = length // TALL - 1

    def branch_rows(own):
        def place(s, b):
            return (0, jnp.where(s < own, 0, jnp.where(s > own, last, b)), 0)

        return pl.BlockSpec((1, TALL, D), place)

    return pl.pallas_call(
        gate_back_kernel,
        grid=(count, length // TALL),
        in_specs=[
            by_rows(D, TALL),
            whole((inner, D)),
            by_rows(inner, TALL),
            by_rows(inner, TALL),
            whole((1, inner)),
            by_rows(inner, TALL),
            pl.BlockSpec((stats.shape[0], 1, 2, TALL), lambda s, b: (0, s, 0, b)),
            by_rows(D, TALL),
        ],
        out_specs=[branch_rows(s) for s in range(count)]
        + [
            whole((inner, D)),
            whole((D, inner)),
            by_rows(inner, TALL),
            by_rows(inner, TALL),
            whole((1, inner)),
        ],
        out_shape=[shaped((1, length, D), BF16)] * count
        + [
            shaped((inner, D), BF16),
            shaped((D, inner), BF16),
            shaped((count, length, inner), BF16),
            shaped((count, length, inner), BF16),
            shaped((1, inner)),
        ],
        scratch_shapes=[pltpu.VMEM((inner, D), F32), pltpu.VMEM((D, inner), F32)],
        compiler_params=params(),
        cost_estimate=cost(1),
        name="gate_back",
    )(upstream, weight, gate, mixed, gate_gain, d_out, stats, low)


def run_mixer_back(s, saved, fixed, weights, after, part, before):
    rest, mixed, d_mixed, incoming, low, d_gate, tokens = saved
    taps, heads, skip = fixed
    count, length, inner = mixed.shape
    conv = inner + 2 * NS
    last = length // ROWS - 1
    chunks = ROWS // CHUNK
    width = rest.shape[2]

    def rows(width):
        return pl.BlockSpec((1, ROWS, width), lambda b: (s, last - b, 0))

    return pl.pallas_call(
        functools.partial(mixer_back_kernel, inner, s == 0),
        grid=(length // ROWS,),
        in_specs=[
            rows(width),
            pl.BlockSpec(
                (1, RIM, width),
                lambda b: (s, jnp.maximum((last - b) * (ROWS // RIM) - 1, 0), 0),
            ),
            rows(inner),
            rows(inner),
            pl.BlockSpec((1, chunks, NS, inner), lambda b: (s, last - b, 0, 0)),
            whole((RIM, conv)),
            whole((8, LANES)),
            whole((1, inner)),
            rows(D),
            rows(inner),
            rows(D),
            whole((D, inner)),
            whole((D, width)),
            left_alone(),
            left_alone(),
            left_alone(),
        ],
        out_specs=[
            rows(D),
            whole((1, D)),
            whole((D, width)),
            whole((RIM, conv)),
            whole((8, LANES)),
            whole((1, inner)),
        ],
        out_shape=[
            shaped((count, length, D), BF16),
            shaped((1, D)),
            shaped((D, width), BF16 if s == count - 1 else F32),
            shaped((RIM, conv)),
            shaped((8, LANES)),
            shaped((1, inner)),
        ],
        scratch_shapes=[
            pltpu.VMEM((RIM + ROWS, conv), F32),
            pltpu.VMEM((RIM + ROWS, conv), F32),
            pltpu.VMEM((NS, inner), F32),
            pltpu.VMEM((ROWS, conv), F32),
            pltpu.VMEM((D, width), F32),
            pltpu.VMEM((ROWS, width), BF16),
        ],
        compiler_params=params(),
        cost_estimate=cost(1),
        input_output_aliases={15: 0} if s > 0 else {},
        name="mixer_back",
    )(rest, rest, mixed, d_mixed, incoming, *fixed, low, d_gate, tokens, *weights, after, part, before)


def swapped(value, axis, mask=1):
    count = lax.axis_size(axis)
    return lax.ppermute(value, axis, [(a, a ^ mask) for a in range(count)])


def summed_over_ctx(value):
    return lax.psum_scatter(value, "ctx", scatter_dimension=1, tiled=True)


def sum_over(value, axes):
    if len(axes) == 1:
        return lax.psum(value, axes)
    for axis in axes:
        value = value + swapped(value, axis)
    return value


def by_rank(value):
    if lax.axis_size("ctx") != 4:
        return lax.all_gather(value, "ctx", axis=0)
    rank = lax.axis_index("ctx")
    near, across = swapped(value, "ctx", 1), swapped(value, "ctx", 2)
    found = [value, near, across, swapped(across, "ctx", 1)]
    odd, high = (rank & 1) == 1, rank >= 2
    found = [jnp.where(odd, found[k ^ 1], found[k]) for k in range(4)]
    return jnp.stack([jnp.where(high, found[k ^ 2], found[k]) for k in range(4)])


def to_all(value, axes):
    return lax.all_to_all(value, axes, split_axis=0, concat_axis=0, tiled=True)


def to_every(value, axes):
    times = 1
    for axis in axes:
        times = times * lax.axis_size(axis)
    return to_all(jnp.broadcast_to(value[None], (times,) + value.shape).reshape(-1, value.shape[1]), axes)


def adam_step(weight, first_old, second_old, gradient, step_rate):
    first_new = BETA_ONE * first_old + (1.0 - BETA_ONE) * gradient
    second_new = BETA_TWO * second_old + (1.0 - BETA_TWO) * gradient * gradient
    first_hat = first_new / (1.0 - BETA_ONE**STEP)
    second_hat = second_new / (1.0 - BETA_TWO**STEP)
    weight_new = weight - step_rate * (
        first_hat / (jnp.sqrt(second_hat) + ADAM_EPS) + DECAY_WEIGHT * weight
    )
    return (second_new, weight_new)


def pad_lanes(value, width):
    return jnp.pad(value, [(0, 0)] * (value.ndim - 1) + [(0, width - value.shape[-1])])


def shards(
    dp,
    block_in,
    out_grad,
    w_in,
    w_in_m,
    w_in_v,
    w_out,
    w_out_m,
    w_out_v,
    small_params,
    small_m,
    small_v,
):
    axes = dp + ("ctx",)
    n_dp, n_ctx = lax.axis_size(dp), lax.axis_size("ctx")
    rank = lax.axis_index("ctx")
    heads = HEADS // n_ctx
    inner = heads * HD
    conv = inner + 2 * NS
    count = block_in.shape[0]

    moves = []
    for block in range(n_dp * n_ctx):
        moves.append((block, (block % n_dp) * n_ctx + block // n_dp))
    mine_out = lax.ppermute(w_out.astype(BF16), axes, moves)
    offset = 0
    pieces = []
    for amount in (D, DI, KCONV * CHANNELS, CHANNELS, HEADS, HEADS, HEADS):
        pieces.append(small_params[offset : offset + amount])
        offset = offset + amount
    norm_gain = pieces[0].reshape(1, D)
    gate_gain = lax.dynamic_slice(pieces[1], (rank * inner,), (inner,)).reshape(1, inner)
    taps_all = jnp.concatenate([pieces[2].reshape(KCONV, CHANNELS), pieces[3][None]], axis=0)
    taps = jnp.concatenate(
        [lax.dynamic_slice(taps_all, (0, rank * inner), (KCONV + 1, inner)), taps_all[:, DI:]],
        axis=1,
    )
    taps = jnp.pad(taps, ((0, RIM - KCONV - 1), (0, 0)))
    dt_bias = lax.dynamic_slice(pieces[4], (rank * heads,), (heads,))
    decay = -jnp.exp(lax.dynamic_slice(pieces[5], (rank * heads,), (heads,)))
    head_rows = jnp.pad(jnp.stack([dt_bias, decay]), ((0, 6), (0, LANES - heads)))
    skip = jnp.repeat(lax.dynamic_slice(pieces[6], (rank * heads,), (heads,)), HD).reshape(1, inner)

    high = lax.axis_index(dp[0]) if len(dp) > 1 else rank * 0
    high = high.astype(jnp.int32).reshape(1)
    tokens = lax.all_gather(block_in, "ctx", axis=1, tiled=True)
    upstream = lax.all_gather(out_grad, "ctx", axis=1, tiled=True)
    w_in_low = w_in.astype(BF16)
    slices = []
    for r in range(n_ctx):
        first = DI + CHANNELS + r * heads
        slices.append(
            jnp.concatenate(
                [
                    w_in_low[:, DI + r * inner : DI + (r + 1) * inner],
                    w_in_low[:, 2 * DI : 2 * DI + 2 * NS],
                    pad_lanes(w_in_low[:, first : first + heads], LANES),
                    w_in_low[:, r * inner : (r + 1) * inner],
                ],
                axis=1,
            )
        )
    rest = conv + LANES
    sent = jnp.concatenate(slices, axis=0)
    mine_in = to_all(sent, "ctx")
    mine_rest = mine_in[:, :rest]
    if len(dp) > 1:
        columns = [mine_out[:, k * inner : (k + 1) * inner] for k in range(D // inner)]
        mine_both = jnp.concatenate([mine_in[:, rest:]] + columns, axis=0)
        other_rest = swapped(mine_rest, dp[0])
        other_both = swapped(mine_both, dp[0])
        mine_rest, mine_out = lax.optimization_barrier((mine_rest, mine_out))
        first_half = to_every(mine_rest, dp[1:])
        other_rest, taps, head_rows, skip, norm_gain, gate_gain, high = lax.optimization_barrier(
            (other_rest, taps, head_rows, skip, norm_gain, gate_gain, high)
        )
        weight_halves = [first_half, to_every(other_rest, dp[1:])]
        both = jnp.concatenate([mine_both, other_both], axis=0)
        both, *weight_halves = lax.optimization_barrier((both, *weight_halves))
        weights = [to_every(both, dp[1:])]
    else:
        weight_halves = [lax.all_gather(mine_rest, dp, axis=0, tiled=True)]
        weights = [
            lax.all_gather(value, dp, axis=0, tiled=True)
            for value in (mine_out, mine_in[:, rest:])
        ]

    low, rest, mixed, incoming, weight_rest = run_forward(
        high, tokens, norm_gain, weight_halves, taps, head_rows, skip
    )
    weight_out, weight_gate, gate, d_out, stats = run_stats(
        high, upstream, low, mixed, gate_gain, weights
    )
    stats = lax.all_gather(stats, "ctx")
    *branches, grad_out, grad_gate, d_mixed, d_gate, d_gate_gain = run_gate_back(
        upstream, weight_out, gate, mixed, gate_gain, d_out, stats, low
    )
    grad_out = to_all(grad_out, dp)
    branches = [summed_over_ctx(branch) for branch in branches]

    own_rows = w_in.shape[0]

    def summed(got):
        return jnp.sum(got.astype(F32).reshape(-1, n_ctx, own_rows, got.shape[1]), axis=0)

    saved = (rest, mixed, d_mixed, incoming, low, d_gate, tokens)
    fixed = (taps, head_rows, skip)
    weights = (weight_gate, weight_rest)
    after = grad_rest = d_normed = d_gate
    smalls = []
    for s in range(count):
        d_normed, d_gain, grad_rest, d_taps, d_heads, d_skip = run_mixer_back(
            s, saved, fixed, weights, after, grad_rest, d_normed
        )
        branches[s], d_gain = lax.optimization_barrier((branches[s], d_gain))
        if s == 0:
            grad_gate, branches[s], d_gain, after = lax.optimization_barrier(
                (grad_gate, branches[s], d_gain, grad_out)
            )
            grad_gate = to_all(grad_gate, axes)
        else:
            grad_gate, d_gain = lax.optimization_barrier((grad_gate, d_gain))
        smalls.append([d_gain, d_taps, d_heads, d_skip])
    d_norm_gain, d_taps, d_heads, d_skip = (sum(parts) for parts in zip(*smalls))
    parts = (
        d_norm_gain.reshape(-1),
        d_gate_gain.reshape(-1),
        d_taps[: KCONV + 1].reshape(-1),
        d_heads[0, :heads],
        d_heads[1, :heads],
        jnp.sum(d_skip.reshape(heads, HD), axis=1),
    )
    mine = jnp.concatenate(parts)
    mine = jnp.pad(mine, (0, -mine.shape[0] % (8 * LANES))).reshape(-1, LANES)
    every = by_rank(sum_over(mine, dp)).reshape(n_ctx, -1)
    grad_rest, every = lax.optimization_barrier((grad_rest, every))
    grad_rest = to_all(grad_rest, axes)
    d_normed = summed_over_ctx(d_normed).astype(F32)
    grad_out = jnp.sum(grad_out.astype(F32).reshape(n_dp, -1, D), axis=0)
    grad_out = lax.ppermute(grad_out, axes, [(b, a) for a, b in moves])
    grad_gate = summed(grad_gate)
    grad_rest = summed(grad_rest)
    columns = [grad_gate[r] for r in range(n_ctx)]
    columns += [grad_rest[r, :, :inner] for r in range(n_ctx)]
    columns += [jnp.sum(grad_rest[:, :, inner:conv], axis=0)]
    columns += [grad_rest[r, :, conv : conv + heads] for r in range(n_ctx)]
    grad_in = jnp.concatenate(columns, axis=1)

    offset = 0
    found = []
    for part in parts:
        found.append(every[:, offset : offset + part.shape[0]])
        offset = offset + part.shape[0]
    taps_found = found[2].reshape(n_ctx, KCONV + 1, conv)
    taps_found = jnp.concatenate(
        [
            jnp.swapaxes(taps_found[:, :, :inner], 0, 1).reshape(KCONV + 1, DI),
            jnp.sum(taps_found[:, :, inner:], axis=0),
        ],
        axis=1,
    )
    grad_small = jnp.concatenate(
        [jnp.sum(found[0], axis=0), found[1].reshape(-1), taps_found.reshape(-1)]
        + [found[k].reshape(-1) for k in (3, 4, 5)]
    )

    own = block_in.astype(F32)
    branch = jnp.concatenate(branches, axis=0)
    block_out = (own + branch.astype(F32)).astype(BF16)
    scale = lax.rsqrt(jnp.mean(own * own, axis=-1, keepdims=True) + NORM_EPS)
    d_scaled = d_normed * norm_gain
    d_own = scale * (
        d_scaled - own * scale * scale * jnp.mean(d_scaled * own, axis=-1, keepdims=True)
    )
    input_grad = (out_grad.astype(F32) + d_own).astype(BF16)
    in_second, in_new = adam_step(w_in, w_in_m, w_in_v, grad_in, RATE_BIG)
    out_second, out_new = adam_step(w_out, w_out_m, w_out_v, grad_out, RATE_BIG)
    small_second, small_updated = adam_step(small_params, small_m, small_v, grad_small, RATE_SMALL)
    return (
        block_out,
        input_grad,
        grad_in,
        in_second,
        in_new,
        grad_out,
        out_second,
        out_new,
        grad_small,
        small_second,
        small_updated,
    )


def solution(mesh):
    dp = ("dp",)
    if mesh.shape["dp"] == 8 and mesh.shape["ctx"] == 4:
        dp = ("high", "low", "side")
        mesh = Mesh(np.asarray(mesh.devices).reshape(2, 2, 2, 4), dp + ("ctx",))
    rows = P(dp + ("ctx",), None)
    spread = P(dp, "ctx", None)
    return jax.shard_map(
        functools.partial(shards, dp),
        mesh=mesh,
        in_specs=(spread, spread) + (rows,) * 6 + (P(),) * 3,
        out_specs=(spread, spread) + (rows,) * 6 + (P(),) * 3,
        check_vma=False,
    )
```

```python
import functools

import jax
import jax.numpy as jnp
import numpy as np
from jax import lax
from jax.experimental import pallas as pl
from jax.experimental.pallas import tpu as pltpu
from jax.sharding import Mesh
from jax.sharding import PartitionSpec as P

D = 1024
HEADS = 32
HD = 64
NS = 128
KCONV = 4
STEP = 10
DI = 2048
CHANNELS = DI + 2 * NS

CHUNK = 128
LANES = 128
RIM = 8
ROWS = 512
TALL = 512

NORM_EPS = 1e-05
ADAM_EPS = 1e-08
BETA_ONE = 0.9
BETA_TWO = 0.999
RATE_BIG = 0.03
RATE_SMALL = 0.3
DECAY_WEIGHT = 0.01

F32 = jnp.float32
BF16 = jnp.bfloat16
VMEM_BYTES = 60 * 1024 * 1024


def dot(a, b, contract=((1,), (0,))):
    return lax.dot_general(a, b, (contract, ((), ())), preferred_element_type=F32)


def terms(a, count):
    parts = []
    for _ in range(count):
        part = a.astype(BF16)
        parts.append(part)
        a = a - part.astype(F32)
    return parts


def spread_dot(a, spread):
    return dot(
        jnp.concatenate(terms(a, 2), axis=1), jnp.concatenate([spread, spread], axis=0)
    )


def sum_dot(ones, a, count):
    return sum(dot(ones, part) for part in terms(a, count))


ROW_ROW = ((1,), (1,))
COL_COL = ((0,), (0,))


def sigmoid(v):
    return 1.0 / (1.0 + jnp.exp(-v))


def softplus(v):
    return jnp.maximum(v, 0.0) + jnp.log1p(jnp.exp(-jnp.abs(v)))


def expander(inner):
    head = lax.broadcasted_iota(jnp.int32, (LANES, inner), 0)
    column = lax.broadcasted_iota(jnp.int32, (LANES, inner), 1)
    inside = (column >= head * HD) & (column < (head + 1) * HD)
    return jnp.where(inside, 1.0, 0.0).astype(BF16)


def lower_ones():
    row = lax.broadcasted_iota(jnp.int32, (CHUNK, CHUNK), 0)
    column = lax.broadcasted_iota(jnp.int32, (CHUNK, CHUNK), 1)
    return jnp.where(row >= column, 1.0, 0.0)


def row_sums(a):
    lanes = a[:, :LANES]
    for start in range(LANES, a.shape[1], LANES):
        lanes = lanes + a[:, start : start + LANES]
    return jnp.sum(lanes.T, axis=0, keepdims=True)


def side_by_side(pair):
    lane = lax.broadcasted_iota(jnp.int32, pair.shape, 1)
    zero = jnp.zeros_like(pair)
    return jnp.concatenate(
        [jnp.where(lane < HD, pair, zero), jnp.where(lane < HD, zero, pair)], axis=0
    )


def decay_terms(step, rate, spread, tri):
    cum = sum_dot(tri.astype(BF16), rate, 3)
    total = cum[CHUNK - 1 : CHUNK, :]
    wide = spread_dot(
        jnp.concatenate([step, jnp.exp(cum), jnp.exp(total - cum)], axis=0), spread
    )
    return cum, cum.T, wide[:CHUNK], wide[CHUNK : 2 * CHUNK], wide[2 * CHUNK :]


def pair_mixing(cum, cum_t, scores, pair):
    decays = []
    for head in (2 * pair, 2 * pair + 1):
        differ = cum[:, head : head + 1] - cum_t[head : head + 1, :]
        decays.append(jnp.exp(jnp.minimum(differ, 0.0)))
    return decays, [(decay * scores).astype(BF16) for decay in decays]


def conv_forward(padded_ref, taps, rows):
    total = taps[KCONV : KCONV + 1, :]
    for k in range(KCONV):
        start = RIM - (KCONV - 1) + k
        total = total + taps[k : k + 1, :] * padded_ref[start : start + rows, :]
    return total


def forward_kernel(
    inner,
    order_ref,
    tokens_ref,
    gain_ref,
    taps_ref,
    heads_ref,
    skip_ref,
    mine_ref,
    other_ref,
    low_ref,
    rest_ref,
    mixed_ref,
    incoming_ref,
    weight_ref,
    padded,
    state,
):
    rows = tokens_ref.shape[1]
    conv = inner + 2 * NS

    @pl.when((pl.program_id(0) == 0) & (pl.program_id(1) == 0))
    def _():
        if mine_ref.shape[0] == D:
            weight_ref[...] = mine_ref[...]
        else:
            mine = pl.multiple_of(order_ref[0] * (D // 2), D // 2)
            other = pl.multiple_of((1 - order_ref[0]) * (D // 2), D // 2)
            weight_ref[pl.ds(mine, D // 2), :] = mine_ref[...]
            weight_ref[pl.ds(other, D // 2), :] = other_ref[...]

    @pl.when(pl.program_id(1) == 0)
    def _():
        padded[0:RIM, :] = jnp.zeros((RIM, conv), F32)
        state[...] = jnp.zeros_like(state)

    @pl.when(pl.program_id(1) > 0)
    def _():
        padded[0:RIM, :] = padded[rows : rows + RIM, :]

    tokens_low = tokens_ref[0]
    tokens = tokens_low.astype(F32)
    scale = lax.rsqrt(jnp.mean(tokens * tokens, axis=1, keepdims=True) + NORM_EPS)
    low = (tokens * scale * gain_ref[...]).astype(BF16)
    low_ref[0] = low
    projected = dot(low, weight_ref[...])
    rest_ref[0] = projected
    padded[RIM : RIM + rows, :] = projected[:, :conv]
    conv_out = conv_forward(padded, taps_ref[...], rows)
    active = conv_out * sigmoid(conv_out)
    heads = heads_ref[...]
    step_all = softplus(projected[:, conv:] + heads[0:1, :])
    rate_all = heads[1:2, :] * step_all
    skip = skip_ref[...]
    spread = expander(inner)
    tri = lower_ones()
    for c in range(rows // CHUNK):
        part = slice(c * CHUNK, (c + 1) * CHUNK)
        values = active[part, :inner]
        in_b = active[part, inner : inner + NS].astype(BF16)
        out_c = active[part, inner + NS :].astype(BF16)
        cum, cum_t, step_x, grown, remain = decay_terms(
            step_all[part], rate_all[part], spread, tri
        )
        stepped = values * step_x
        stepped_low = stepped.astype(BF16)
        scores = dot(out_c, in_b, ROW_ROW) * tri
        inside = []
        for pair in range(inner // LANES):
            lanes = slice(pair * LANES, (pair + 1) * LANES)
            _, mixing = pair_mixing(cum, cum_t, scores, pair)
            inside.append(
                dot(jnp.concatenate(mixing, axis=1), side_by_side(stepped_low[:, lanes]))
            )
        before = state[...]
        before_low = before.astype(BF16)
        incoming_ref[0, c] = before_low
        outer = grown * dot(out_c, before_low)
        mixed_ref[0, part, :] = jnp.concatenate(inside, axis=1) + outer + skip * values
        state[...] = grown[CHUNK - 1 : CHUNK, :] * before + dot(
            in_b, (remain * stepped).astype(BF16), COL_COL
        )


def stats_kernel(joined, order_ref, up_ref, low_ref, mixed_ref, gain_ref, *refs):
    if joined:
        both_ref, weight_out_ref, weight_gate_ref, gate_ref, d_out_ref, stats_ref = refs
        inner = gate_ref.shape[2]

        @pl.when((pl.program_id(0) == 0) & (pl.program_id(1) == 0))
        def _():
            deep, tall = D // 8, inner // 8
            place = 0
            for quarter in range(4):
                for half in (order_ref[0], 1 - order_ref[0]):
                    block = half * 4 + quarter
                    rows = pl.ds(pl.multiple_of(block * deep, deep), deep)
                    weight_gate_ref[rows, :] = both_ref[place : place + deep, :]
                    place = place + deep
                    rows = pl.ds(pl.multiple_of(block * tall, tall), tall)
                    for k in range(D // inner):
                        columns = slice(k * inner, (k + 1) * inner)
                        weight_out_ref[rows, columns] = both_ref[place : place + tall, :]
                        place = place + tall

    else:
        weight_out_ref, weight_gate_ref, gate_ref, d_out_ref, stats_ref = refs
    d_out = dot(up_ref[0], weight_out_ref[...], ROW_ROW)
    d_out_ref[0] = d_out.astype(BF16)
    gate = dot(low_ref[0], weight_gate_ref[...])
    gate_ref[0] = gate
    gated = mixed_ref[0] * gate * sigmoid(gate)
    stats_ref[0, 0:1, :] = row_sums(gated * gated)
    stats_ref[0, 1:2, :] = row_sums(d_out * gain_ref[...] * gated)


def row_to_lanes(row):
    return jnp.broadcast_to(row, (LANES, row.shape[1])).T[:, 0:1]


def gate_back_kernel(
    up_ref,
    weight_ref,
    gate_ref,
    mixed_ref,
    gain_ref,
    d_out_ref,
    stats_ref,
    low_ref,
    *refs,
):
    *branch_refs, grad_ref, grad_gate_ref, d_mixed_ref, d_gate_ref, d_gain_ref = refs[:-2]
    total, total_gate = refs[-2:]
    first = (pl.program_id(0) == 0) & (pl.program_id(1) == 0)
    last_one = pl.program_id(0) == pl.num_programs(0) - 1
    last_two = pl.program_id(1) == pl.num_programs(1) - 1

    @pl.when(first)
    def _():
        total[...] = jnp.zeros_like(total)
        total_gate[...] = jnp.zeros_like(total_gate)
        d_gain_ref[...] = jnp.zeros_like(d_gain_ref)

    stats = stats_ref[0, 0]
    for k in range(1, stats_ref.shape[0]):
        stats = stats + stats_ref[k, 0]
    squares = row_to_lanes(stats[0:1])
    products = row_to_lanes(stats[1:2])
    scale = lax.rsqrt(squares * (1.0 / DI) + NORM_EPS)
    gate = gate_ref[0]
    mixed = mixed_ref[0]
    gain = gain_ref[...]
    d_out = d_out_ref[0].astype(F32)
    sig = sigmoid(gate)
    silu = gate * sig
    gated = mixed * silu
    unit = gated * scale
    low = (unit * gain).astype(BF16)
    branch = dot(low, weight_ref[...]).astype(BF16)
    for s, branch_ref in enumerate(branch_refs):

        @pl.when(pl.program_id(0) == s)
        def _(branch_ref=branch_ref):
            branch_ref[0] = branch

    total[...] += dot(low, up_ref[0], COL_COL)
    d_gain_ref[...] += jnp.sum(d_out * unit, axis=0, keepdims=True)
    d_gated = scale * (gain * d_out - unit * (scale * products * (1.0 / DI)))
    d_mixed_ref[0] = (d_gated * silu).astype(BF16)
    d_gate = (d_gated * mixed * (sig + silu * (1.0 - sig))).astype(BF16)
    d_gate_ref[0] = d_gate
    total_gate[...] += dot(low_ref[0], d_gate, COL_COL)

    @pl.when(last_one & last_two)
    def _():
        grad_ref[...] = total[...].astype(BF16)
        grad_gate_ref[...] = total_gate[...].astype(BF16)


def mixer_back_kernel(
    inner,
    first,
    rest_ref,
    rim_ref,
    mixed_ref,
    d_mixed_ref,
    incoming_ref,
    taps_ref,
    heads_ref,
    skip_ref,
    low_ref,
    d_gate_ref,
    tokens_ref,
    weight_gate_ref,
    weight_rest_ref,
    after_ref,
    part_ref,
    before_ref,
    d_normed_ref,
    d_gain_ref,
    grad_ref,
    d_taps_ref,
    d_heads_ref,
    d_skip_ref,
    padded,
    later,
    carried,
    d_active,
    total,
    d_rest_ref,
):
    rows = rest_ref.shape[1]
    conv = inner + 2 * NS
    block = pl.num_programs(0) - 1 - pl.program_id(0)

    @pl.when(pl.program_id(0) == 0)
    def _():
        d_taps_ref[...] = jnp.zeros_like(d_taps_ref)
        d_heads_ref[...] = jnp.zeros_like(d_heads_ref)
        d_skip_ref[...] = jnp.zeros_like(d_skip_ref)
        d_gain_ref[...] = jnp.zeros_like(d_gain_ref)
        if first:
            total[...] = jnp.zeros_like(total)
        else:
            pltpu.sync_copy(part_ref, total)
        carried[...] = jnp.zeros_like(carried)
        later[rows : rows + RIM, :] = jnp.zeros((RIM, conv), F32)

    @pl.when(pl.program_id(0) > 0)
    def _():
        later[rows : rows + RIM, :] = later[0:RIM, :]

    rim = rim_ref[0][:, :conv]
    padded[0:RIM, :] = jnp.where(block > 0, rim, jnp.zeros_like(rim))
    padded[RIM : RIM + rows, :] = rest_ref[0][:, :conv]
    taps = taps_ref[...]
    conv_out = conv_forward(padded, taps, rows)
    sig = sigmoid(conv_out)
    active = conv_out * sig
    slope = sig + active * (1.0 - sig)
    heads = heads_ref[...]
    raw = rest_ref[0][:, conv:] + heads[0:1, :]
    step_all = softplus(raw)
    rate_all = heads[1:2, :] * step_all
    skip = skip_ref[...]
    spread = expander(inner)
    tri = lower_ones()
    upper = tri.T.astype(BF16)
    for c in reversed(range(rows // CHUNK)):
        part = slice(c * CHUNK, (c + 1) * CHUNK)
        values = active[part, :inner]
        in_b = active[part, inner : inner + NS].astype(BF16)
        out_c = active[part, inner + NS :].astype(BF16)
        step = step_all[part]
        rate = rate_all[part]
        cum, cum_t, step_x, grown, remain = decay_terms(step, rate, spread, tri)
        stepped = values * step_x
        stepped_low = stepped.astype(BF16)
        scores = dot(out_c, in_b, ROW_ROW) * tri
        d_low = d_mixed_ref[0, part, :]
        d_mixed = d_low.astype(F32)
        d_scores = jnp.zeros((CHUNK, CHUNK), F32)
        inside = []
        for pair in range(inner // LANES):
            lanes = slice(pair * LANES, (pair + 1) * LANES)
            decays, mixing = pair_mixing(cum, cum_t, scores, pair)
            d_two = side_by_side(d_low[:, lanes])
            d_mixing = dot(d_two, stepped_low[:, lanes], ROW_ROW)
            d_scores += decays[0] * d_mixing[:CHUNK] + decays[1] * d_mixing[CHUNK:]
            inside.append(dot(jnp.concatenate(mixing, axis=0), d_two, COL_COL))
        before = incoming_ref[0, c]
        ahead = carried[...]
        ahead_low = ahead.astype(BF16)
        through = remain * dot(in_b, ahead_low)
        outer = (grown * d_mixed).astype(BF16)
        d_scores_low = (d_scores * tri).astype(BF16)
        d_in_b = dot((remain * stepped).astype(BF16), ahead_low, ROW_ROW) + dot(
            d_scores_low, out_c, COL_COL
        )
        d_out_c = dot(outer, before, ROW_ROW) + dot(d_scores_low, in_b)
        d_stepped = jnp.concatenate(inside, axis=1) + through
        stepped_near = stepped_low.astype(F32)
        both = d_mixed * (mixed_ref[0, part, :] - skip * values)
        d_cum_x = both - stepped_near * d_stepped
        d_step_x = d_stepped * values
        grown_total = grown[CHUNK - 1 : CHUNK, :]
        d_total_x = jnp.sum(stepped_near * through, axis=0, keepdims=True) + grown_total * jnp.sum(
            ahead * before.astype(F32), axis=0, keepdims=True
        )
        gathered = jnp.concatenate(
            [d_cum_x, d_step_x, jnp.broadcast_to(d_total_x, (16, inner))], axis=0
        )
        narrow = sum(dot(part, spread, ROW_ROW) for part in terms(gathered, 2))
        d_rate = sum_dot(upper, narrow[:CHUNK], 2) + narrow[2 * CHUNK : 2 * CHUNK + 1]
        d_raw = (narrow[CHUNK : 2 * CHUNK] + heads[1:2, :] * d_rate) * sigmoid(raw[part])
        d_heads_ref[0:1, :] += jnp.sum(d_raw, axis=0, keepdims=True)
        d_heads_ref[1:2, :] += jnp.sum(d_rate * rate, axis=0, keepdims=True)
        d_skip_ref[...] += jnp.sum(d_mixed * values, axis=0, keepdims=True)
        d_rest_ref[part, conv:] = d_raw.astype(BF16)
        d_active[part, :inner] = d_stepped * step_x + skip * d_mixed
        d_active[part, inner : inner + NS] = d_in_b
        d_active[part, inner + NS :] = d_out_c
        carried[...] = grown_total * ahead + dot(out_c, outer, COL_COL)
    d_conv_out = d_active[...] * slope
    later[0:rows, :] = d_conv_out
    d_conv_in = jnp.zeros((rows, conv), F32)
    for k in range(KCONV):
        ahead_rows = KCONV - 1 - k
        start = RIM - (KCONV - 1) + k
        d_conv_in += taps[k : k + 1, :] * later[ahead_rows : ahead_rows + rows, :]
        d_taps_ref[k : k + 1, :] += jnp.sum(
            d_conv_out * padded[start : start + rows, :], axis=0, keepdims=True
        )
    d_taps_ref[KCONV : KCONV + 1, :] += jnp.sum(d_conv_out, axis=0, keepdims=True)
    d_rest_ref[:, :conv] = d_conv_in.astype(BF16)
    d_rest = d_rest_ref[...]
    total[...] += dot(low_ref[0], d_rest, COL_COL)
    d_normed = dot(d_gate_ref[0], weight_gate_ref[...], ROW_ROW) + dot(
        d_rest, weight_rest_ref[...], ROW_ROW
    )
    tokens = tokens_ref[0].astype(F32)
    scale = lax.rsqrt(jnp.mean(tokens * tokens, axis=1, keepdims=True) + NORM_EPS)
    d_gain_ref[...] += jnp.sum(d_normed * (tokens * scale), axis=0, keepdims=True)
    d_normed_ref[0] = d_normed.astype(BF16)

    @pl.when(block == 0)
    def _():
        grad_ref[...] = total[...].astype(grad_ref.dtype)


def whole(shape):
    return pl.BlockSpec(shape, lambda *_: (0,) * len(shape))


def by_rows(width, rows=ROWS):
    return pl.BlockSpec((1, rows, width), lambda s, b, *_: (s, b, 0))


def left_alone():
    return pl.BlockSpec(memory_space=pl.ANY)


def cost(micros):
    return pl.CostEstimate(
        flops=int(micros * 1.1e9), bytes_accessed=int(micros * 2e6), transcendentals=0
    )


def params():
    return pltpu.CompilerParams(
        vmem_limit_bytes=VMEM_BYTES
    )


def shaped(shape, dtype=F32):
    return jax.ShapeDtypeStruct(shape, dtype)


def run_forward(order, tokens, norm_gain, halves, taps, heads, skip):
    count, length, _ = tokens.shape
    inner = skip.shape[1]
    rest = halves[0].shape[1]
    conv = inner + 2 * NS
    chunks = ROWS // CHUNK
    fixed = [norm_gain, taps, heads, skip, halves[0], halves[-1]]
    return pl.pallas_call(
        functools.partial(forward_kernel, inner),
        grid_spec=pltpu.PrefetchScalarGridSpec(
            num_scalar_prefetch=1,
            grid=(count, length // ROWS),
            in_specs=[by_rows(D)] + [whole(value.shape) for value in fixed],
            out_specs=[
                by_rows(D),
                by_rows(rest),
                by_rows(inner),
                pl.BlockSpec((1, chunks, NS, inner), lambda s, b, *_: (s, b, 0, 0)),
                whole((D, rest)),
            ],
            scratch_shapes=[pltpu.VMEM((RIM + ROWS, conv), F32), pltpu.VMEM((NS, inner), F32)],
        ),
        out_shape=[
            shaped((count, length, D), BF16),
            shaped((count, length, rest)),
            shaped((count, length, inner)),
            shaped((count, length // CHUNK, NS, inner), BF16),
            shaped((D, rest), BF16),
        ],
        compiler_params=params(),
        cost_estimate=cost(1),
        name="forward_mixer",
    )(order, tokens, *fixed)


def run_stats(order, upstream, low, mixed, gate_gain, weights):
    count, length, inner = mixed.shape
    joined = len(weights) == 1
    found_specs = [whole((inner, D)), whole((D, inner))] * joined
    found_shapes = [shaped((inner, D), BF16), shaped((D, inner), BF16)] * joined
    found = pl.pallas_call(
        functools.partial(stats_kernel, joined),
        grid_spec=pltpu.PrefetchScalarGridSpec(
            num_scalar_prefetch=1,
            grid=(count, length // TALL),
            in_specs=[by_rows(D, TALL), by_rows(D, TALL), by_rows(inner, TALL), whole((1, inner))]
            + [whole(weight.shape) for weight in weights],
            out_specs=found_specs
            + [
                by_rows(inner, TALL),
                by_rows(inner, TALL),
                pl.BlockSpec((1, 2, TALL), lambda s, b, *_: (s, 0, b)),
            ],
        ),
        out_shape=found_shapes
        + [
            shaped((count, length, inner)),
            shaped((count, length, inner), BF16),
            shaped((count, 2, length)),
        ],
        compiler_params=params(),
        cost_estimate=cost(1),
        name="gate_stats",
    )(order, upstream, low, mixed, gate_gain, *weights)
    return found if joined else [*weights, *found]


def run_gate_back(upstream, weight, gate, mixed, gate_gain, d_out, stats, low):
    count, length, inner = gate.shape
    last = length // TALL - 1

    def branch_rows(own):
        def place(s, b):
            return (0, jnp.where(s < own, 0, jnp.where(s > own, last, b)), 0)

        return pl.BlockSpec((1, TALL, D), place)

    return pl.pallas_call(
        gate_back_kernel,
        grid=(count, length // TALL),
        in_specs=[
            by_rows(D, TALL),
            whole((inner, D)),
            by_rows(inner, TALL),
            by_rows(inner, TALL),
            whole((1, inner)),
            by_rows(inner, TALL),
            pl.BlockSpec((stats.shape[0], 1, 2, TALL), lambda s, b: (0, s, 0, b)),
            by_rows(D, TALL),
        ],
        out_specs=[branch_rows(s) for s in range(count)]
        + [
            whole((inner, D)),
            whole((D, inner)),
            by_rows(inner, TALL),
            by_rows(inner, TALL),
            whole((1, inner)),
        ],
        out_shape=[shaped((1, length, D), BF16)] * count
        + [
            shaped((inner, D), BF16),
            shaped((D, inner), BF16),
            shaped((count, length, inner), BF16),
            shaped((count, length, inner), BF16),
            shaped((1, inner)),
        ],
        scratch_shapes=[pltpu.VMEM((inner, D), F32), pltpu.VMEM((D, inner), F32)],
        compiler_params=params(),
        cost_estimate=cost(1),
        name="gate_back",
    )(upstream, weight, gate, mixed, gate_gain, d_out, stats, low)


def run_mixer_back(s, saved, fixed, weights, after, part, before):
    rest, mixed, d_mixed, incoming, low, d_gate, tokens = saved
    taps, heads, skip = fixed
    count, length, inner = mixed.shape
    conv = inner + 2 * NS
    last = length // ROWS - 1
    chunks = ROWS // CHUNK
    width = rest.shape[2]

    def rows(width):
        return pl.BlockSpec((1, ROWS, width), lambda b: (s, last - b, 0))

    return pl.pallas_call(
        functools.partial(mixer_back_kernel, inner, s == 0),
        grid=(length // ROWS,),
        in_specs=[
            rows(width),
            pl.BlockSpec(
                (1, RIM, width),
                lambda b: (s, jnp.maximum((last - b) * (ROWS // RIM) - 1, 0), 0),
            ),
            rows(inner),
            rows(inner),
            pl.BlockSpec((1, chunks, NS, inner), lambda b: (s, last - b, 0, 0)),
            whole((RIM, conv)),
            whole((8, LANES)),
            whole((1, inner)),
            rows(D),
            rows(inner),
            rows(D),
            whole((D, inner)),
            whole((D, width)),
            left_alone(),
            left_alone(),
            left_alone(),
        ],
        out_specs=[
            rows(D),
            whole((1, D)),
            whole((D, width)),
            whole((RIM, conv)),
            whole((8, LANES)),
            whole((1, inner)),
        ],
        out_shape=[
            shaped((count, length, D), BF16),
            shaped((1, D)),
            shaped((D, width), BF16 if s == count - 1 else F32),
            shaped((RIM, conv)),
            shaped((8, LANES)),
            shaped((1, inner)),
        ],
        scratch_shapes=[
            pltpu.VMEM((RIM + ROWS, conv), F32),
            pltpu.VMEM((RIM + ROWS, conv), F32),
            pltpu.VMEM((NS, inner), F32),
            pltpu.VMEM((ROWS, conv), F32),
            pltpu.VMEM((D, width), F32),
            pltpu.VMEM((ROWS, width), BF16),
        ],
        compiler_params=params(),
        cost_estimate=cost(1),
        input_output_aliases={15: 0} if s > 0 else {},
        name="mixer_back",
    )(rest, rest, mixed, d_mixed, incoming, *fixed, low, d_gate, tokens, *weights, after, part, before)


def swapped(value, axis, mask=1):
    count = lax.axis_size(axis)
    return lax.ppermute(value, axis, [(a, a ^ mask) for a in range(count)])


def summed_over_ctx(value):
    return lax.psum_scatter(value, "ctx", scatter_dimension=1, tiled=True)


def sum_over(value, axes):
    if len(axes) == 1:
        return lax.psum(value, axes)
    for axis in axes:
        value = value + swapped(value, axis)
    return value


def by_rank(value):
    if lax.axis_size("ctx") != 4:
        return lax.all_gather(value, "ctx", axis=0)
    rank = lax.axis_index("ctx")
    near, across = swapped(value, "ctx", 1), swapped(value, "ctx", 2)
    found = [value, near, across, swapped(value, "ctx", 3)]
    odd, high = (rank & 1) == 1, rank >= 2
    found = [jnp.where(odd, found[k ^ 1], found[k]) for k in range(4)]
    return jnp.stack([jnp.where(high, found[k ^ 2], found[k]) for k in range(4)])


def to_all(value, axes):
    return lax.all_to_all(value, axes, split_axis=0, concat_axis=0, tiled=True)


def to_every(value, axes):
    times = 1
    for axis in axes:
        times = times * lax.axis_size(axis)
    return to_all(jnp.broadcast_to(value[None], (times,) + value.shape).reshape(-1, value.shape[1]), axes)


def adam_step(weight, first_old, second_old, gradient, step_rate):
    first_new = BETA_ONE * first_old + (1.0 - BETA_ONE) * gradient
    second_new = BETA_TWO * second_old + (1.0 - BETA_TWO) * gradient * gradient
    first_hat = first_new / (1.0 - BETA_ONE**STEP)
    second_hat = second_new / (1.0 - BETA_TWO**STEP)
    weight_new = weight - step_rate * (
        first_hat / (jnp.sqrt(second_hat) + ADAM_EPS) + DECAY_WEIGHT * weight
    )
    return (second_new, weight_new)


def pad_lanes(value, width):
    return jnp.pad(value, [(0, 0)] * (value.ndim - 1) + [(0, width - value.shape[-1])])


def shards(
    dp,
    block_in,
    out_grad,
    w_in,
    w_in_m,
    w_in_v,
    w_out,
    w_out_m,
    w_out_v,
    small_params,
    small_m,
    small_v,
):
    axes = dp + ("ctx",)
    n_dp, n_ctx = lax.axis_size(dp), lax.axis_size("ctx")
    rank = lax.axis_index("ctx")
    heads = HEADS // n_ctx
    inner = heads * HD
    conv = inner + 2 * NS
    count = block_in.shape[0]

    moves = []
    for block in range(n_dp * n_ctx):
        moves.append((block, (block % n_dp) * n_ctx + block // n_dp))
    mine_out = lax.ppermute(w_out.astype(BF16), axes, moves)
    offset = 0
    pieces = []
    for amount in (D, DI, KCONV * CHANNELS, CHANNELS, HEADS, HEADS, HEADS):
        pieces.append(small_params[offset : offset + amount])
        offset = offset + amount
    norm_gain = pieces[0].reshape(1, D)
    gate_gain = lax.dynamic_slice(pieces[1], (rank * inner,), (inner,)).reshape(1, inner)
    taps_all = jnp.concatenate([pieces[2].reshape(KCONV, CHANNELS), pieces[3][None]], axis=0)
    taps = jnp.concatenate(
        [lax.dynamic_slice(taps_all, (0, rank * inner), (KCONV + 1, inner)), taps_all[:, DI:]],
        axis=1,
    )
    taps = jnp.pad(taps, ((0, RIM - KCONV - 1), (0, 0)))
    dt_bias = lax.dynamic_slice(pieces[4], (rank * heads,), (heads,))
    decay = -jnp.exp(lax.dynamic_slice(pieces[5], (rank * heads,), (heads,)))
    head_rows = jnp.pad(jnp.stack([dt_bias, decay]), ((0, 6), (0, LANES - heads)))
    skip = jnp.repeat(lax.dynamic_slice(pieces[6], (rank * heads,), (heads,)), HD).reshape(1, inner)

    high = lax.axis_index(dp[0]) if len(dp) > 1 else rank * 0
    high = high.astype(jnp.int32).reshape(1)
    tokens = lax.all_gather(block_in, "ctx", axis=1, tiled=True)
    upstream = lax.all_gather(out_grad, "ctx", axis=1, tiled=True)
    w_in_low = w_in.astype(BF16)
    slices = []
    for r in range(n_ctx):
        first = DI + CHANNELS + r * heads
        slices.append(
            jnp.concatenate(
                [
                    w_in_low[:, DI + r * inner : DI + (r + 1) * inner],
                    w_in_low[:, 2 * DI : 2 * DI + 2 * NS],
                    pad_lanes(w_in_low[:, first : first + heads], LANES),
                    w_in_low[:, r * inner : (r + 1) * inner],
                ],
                axis=1,
            )
        )
    rest = conv + LANES
    sent = jnp.concatenate(slices, axis=0)
    mine_in = to_all(sent, "ctx")
    mine_rest = mine_in[:, :rest]
    if len(dp) > 1:
        columns = [mine_out[:, k * inner : (k + 1) * inner] for k in range(D // inner)]
        mine_both = jnp.concatenate([mine_in[:, rest:]] + columns, axis=0)
        other_rest = swapped(mine_rest, dp[0])
        other_both = swapped(mine_both, dp[0])
        mine_rest, mine_out = lax.optimization_barrier((mine_rest, mine_out))
        first_half = to_every(mine_rest, dp[1:])
        other_rest, taps, head_rows, skip, norm_gain, gate_gain, high = lax.optimization_barrier(
            (other_rest, taps, head_rows, skip, norm_gain, gate_gain, high)
        )
        weight_halves = [first_half, to_every(other_rest, dp[1:])]
        both = jnp.concatenate([mine_both, other_both], axis=0)
        both, *weight_halves = lax.optimization_barrier((both, *weight_halves))
        weights = [to_every(both, dp[1:])]
    else:
        weight_halves = [lax.all_gather(mine_rest, dp, axis=0, tiled=True)]
        weights = [
            lax.all_gather(value, dp, axis=0, tiled=True)
            for value in (mine_out, mine_in[:, rest:])
        ]

    low, rest, mixed, incoming, weight_rest = run_forward(
        high, tokens, norm_gain, weight_halves, taps, head_rows, skip
    )
    weight_out, weight_gate, gate, d_out, stats = run_stats(
        high, upstream, low, mixed, gate_gain, weights
    )
    stats = lax.all_gather(stats, "ctx")
    *branches, grad_out, grad_gate, d_mixed, d_gate, d_gate_gain = run_gate_back(
        upstream, weight_out, gate, mixed, gate_gain, d_out, stats, low
    )
    grad_out = to_all(grad_out, dp)
    branches = [summed_over_ctx(branch) for branch in branches]

    own_rows = w_in.shape[0]

    def summed(got):
        return jnp.sum(got.astype(F32).reshape(-1, n_ctx, own_rows, got.shape[1]), axis=0)

    saved = (rest, mixed, d_mixed, incoming, low, d_gate, tokens)
    fixed = (taps, head_rows, skip)
    weights = (weight_gate, weight_rest)
    after = grad_rest = d_normed = d_gate
    smalls = []
    for s in range(count):
        d_normed, d_gain, grad_rest, d_taps, d_heads, d_skip = run_mixer_back(
            s, saved, fixed, weights, after, grad_rest, d_normed
        )
        branches[s], d_gain = lax.optimization_barrier((branches[s], d_gain))
        if s == 0:
            grad_gate, branches[s], d_gain, after = lax.optimization_barrier(
                (grad_gate, branches[s], d_gain, grad_out)
            )
            grad_gate = to_all(grad_gate, axes)
        else:
            grad_gate, d_gain = lax.optimization_barrier((grad_gate, d_gain))
        smalls.append([d_gain, d_taps, d_heads, d_skip])
    d_norm_gain, d_taps, d_heads, d_skip = (sum(parts) for parts in zip(*smalls))
    parts = (
        d_norm_gain.reshape(-1),
        d_gate_gain.reshape(-1),
        d_taps[: KCONV + 1].reshape(-1),
        d_heads[0, :heads],
        d_heads[1, :heads],
        jnp.sum(d_skip.reshape(heads, HD), axis=1),
    )
    mine = jnp.concatenate(parts)
    mine = jnp.pad(mine, (0, -mine.shape[0] % (8 * LANES))).reshape(-1, LANES)
    every = by_rank(sum_over(mine, dp)).reshape(n_ctx, -1)
    grad_rest, every = lax.optimization_barrier((grad_rest, every))
    grad_rest = to_all(grad_rest, axes)
    d_normed = summed_over_ctx(d_normed).astype(F32)
    grad_out = jnp.sum(grad_out.astype(F32).reshape(n_dp, -1, D), axis=0)
    grad_out = lax.ppermute(grad_out, axes, [(b, a) for a, b in moves])
    grad_gate = summed(grad_gate)
    grad_rest = summed(grad_rest)
    columns = [grad_gate[r] for r in range(n_ctx)]
    columns += [grad_rest[r, :, :inner] for r in range(n_ctx)]
    columns += [jnp.sum(grad_rest[:, :, inner:conv], axis=0)]
    columns += [grad_rest[r, :, conv : conv + heads] for r in range(n_ctx)]
    grad_in = jnp.concatenate(columns, axis=1)

    offset = 0
    found = []
    for part in parts:
        found.append(every[:, offset : offset + part.shape[0]])
        offset = offset + part.shape[0]
    taps_found = found[2].reshape(n_ctx, KCONV + 1, conv)
    taps_found = jnp.concatenate(
        [
            jnp.swapaxes(taps_found[:, :, :inner], 0, 1).reshape(KCONV + 1, DI),
            jnp.sum(taps_found[:, :, inner:], axis=0),
        ],
        axis=1,
    )
    grad_small = jnp.concatenate(
        [jnp.sum(found[0], axis=0), found[1].reshape(-1), taps_found.reshape(-1)]
        + [found[k].reshape(-1) for k in (3, 4, 5)]
    )

    own = block_in.astype(F32)
    branch = jnp.concatenate(branches, axis=0)
    block_out = (own + branch.astype(F32)).astype(BF16)
    scale = lax.rsqrt(jnp.mean(own * own, axis=-1, keepdims=True) + NORM_EPS)
    d_scaled = d_normed * norm_gain
    d_own = scale * (
        d_scaled - own * scale * scale * jnp.mean(d_scaled * own, axis=-1, keepdims=True)
    )
    input_grad = (out_grad.astype(F32) + d_own).astype(BF16)
    in_second, in_new = adam_step(w_in, w_in_m, w_in_v, grad_in, RATE_BIG)
    out_second, out_new = adam_step(w_out, w_out_m, w_out_v, grad_out, RATE_BIG)
    small_second, small_updated = adam_step(small_params, small_m, small_v, grad_small, RATE_SMALL)
    return (
        block_out,
        input_grad,
        grad_in,
        in_second,
        in_new,
        grad_out,
        out_second,
        out_new,
        grad_small,
        small_second,
        small_updated,
    )


def solution(mesh):
    dp = ("dp",)
    if mesh.shape["dp"] == 8 and mesh.shape["ctx"] == 4:
        dp = ("high", "low", "side")
        mesh = Mesh(np.asarray(mesh.devices).reshape(2, 2, 2, 4), dp + ("ctx",))
    rows = P(dp + ("ctx",), None)
    spread = P(dp, "ctx", None)
    return jax.shard_map(
        functools.partial(shards, dp),
        mesh=mesh,
        in_specs=(spread, spread) + (rows,) * 6 + (P(),) * 3,
        out_specs=(spread, spread) + (rows,) * 6 + (P(),) * 3,
        check_vma=False,
    )
```
